32 devices in a mesh: section: 2 (over x), dp: 16 (over z, y, core).
Axes of the slice: x: 2, y: 2, z: 4, core: 2. Of those that a mesh axis runs over, the one named last changes fastest.
Arguments:
- tokens: bfloat16 [2, 8192, 768], P(None, 'dp'), may hold values from -6 to 6
- segments: int32 [2, 8192], P(None, 'dp'), may hold values from 0 to 31, never falling along the last dimension, each value on 1 to 512 neighbouring positions
- cotangent: float32 [2, 8192, 768], P(None, 'dp'), may hold values from -6 to 6
- ln1_gain: bfloat16 [2, 768], P('section', 'dp'), may hold values from 0.099609375 to 1.8984375
- ln1_bias: bfloat16 [2, 768], P('section', 'dp'), may hold values from -3 to 3
- ln2_gain: bfloat16 [2, 768], P('section', 'dp'), may hold values from 0.099609375 to 1.8984375
- ln2_bias: bfloat16 [2, 768], P('section', 'dp'), may hold values from -3 to 3
- qkv_weight: bfloat16 [2, 768, 2304], P('section', 'dp'), may hold values from -0.21875 to 0.21875
- qkv_bias: bfloat16 [2, 2304], P('section', 'dp'), may hold values from -3 to 3
- out_weight: bfloat16 [2, 768, 768], P('section', 'dp'), may hold values from -0.875 to 0.875
- out_bias: bfloat16 [2, 768], P('section', 'dp'), may hold values from -3 to 3
- up_weight: bfloat16 [2, 768, 3072], P('section', 'dp'), may hold values from -0.21875 to 0.21875
- up_bias: bfloat16 [2, 3072], P('section', 'dp'), may hold values from -3 to 3
- down_weight: bfloat16 [2, 3072, 768], P('section', 'dp'), may hold values from -0.15625 to 0.15625
- down_bias: bfloat16 [2, 768], P('section', 'dp'), may hold values from -3 to 3
Outputs:
- section_outputs: bfloat16 [2, 2, 8192, 768], P('section', None, 'dp')
- input_grads: float32 [2, 2, 8192, 768], P('section', None, 'dp')
- ln1_gain_grad: float32 [2, 768], P('section', 'dp')
- ln1_bias_grad: float32 [2, 768], P('section', 'dp')
- ln2_gain_grad: float32 [2, 768], P('section', 'dp')
- ln2_bias_grad: float32 [2, 768], P('section', 'dp')
- qkv_weight_grad: float32 [2, 768, 2304], P('section', 'dp')
- qkv_bias_grad: float32 [2, 2304], P('section', 'dp')
- out_weight_grad: float32 [2, 768, 768], P('section', 'dp')
- out_bias_grad: float32 [2, 768], P('section', 'dp')
- up_weight_grad: float32 [2, 768, 3072], P('section', 'dp')
- up_bias_grad: float32 [2, 3072], P('section', 'dp')
- down_weight_grad: float32 [2, 3072, 768], P('section', 'dp')
- down_bias_grad: float32 [2, 768], P('section', 'dp')
The draws below stay inside these ranges and needn't reach their ends.
Inputs may be any that keep to these rules, and one draw needn't show every extreme that they name: `segments`: along each micro-batch row the segment number never falls; each document covers 1 to 512 consecutive positions, one exactly 512, and every number of 0 to 31 occurs.
All inputs are finite; a program needn't handle non-finite values.
Results may differ from the reference program's by a relative error of at most 0.014.
Values may be sent and summed in bfloat16 or wider, within the bound.
No kernel may reach another device: no remote copies, remote signals or barrier semaphores. Data moves between devices by JAX's collectives and lax.ppermute only.
A program may use at most 320 MiB of HBM per device.

```python
import math
import jax
import jax.numpy as jnp
import numpy as np
from jax import lax

D = 768
HEADS = 12
HEAD_DIM = 64
FF = 3072
ROT = 16
LEN = 512
MICRO = 2
DOC = 256
LAYERS = 2
TOKENS = 8192
SEGS = 32


def spiked(array, own_key, source, target, parts, factor):
    def block_of(dim):
        return (jnp.arange(array.shape[dim]) // (array.shape[dim] // parts)).reshape((-1,) + (1,) * (array.ndim - 1 - dim))

    near = jax.random.permutation(own_key, parts)[block_of(target)]
    far = (block_of(target) + parts // 2) % parts
    return jnp.where((block_of(source) == near) | (block_of(source) == far), factor * array, array)


def block_levels(key, extent, cuts, least, largest):
    gain, own = 1.0, jax.random.fold_in(key, 6)
    for position, shards_of in cuts:
        steps = jnp.exp(jax.random.uniform(jax.random.fold_in(own, position), (shards_of,), jnp.float32, least / len(cuts), largest / len(cuts)))
        gain = gain * jnp.repeat(steps, extent[position] // shards_of).reshape([-1 if axis == position else 1 for axis in range(len(extent))])
    return gain


def length_profile(amount, total, most, skew):
    loads = [(1 << 20) // math.isqrt(rank ** skew) + 1 for rank in range(2, amount + 1)]
    rest, holding = total - most - (amount - 1), [1] * (amount - 1)
    while rest > 0:
        candidates = [i for i in range(amount - 1) if holding[i] < most]
        pool, remaining = sum([loads[i] for i in candidates]), rest
        for i in candidates:
            addition = min(most - holding[i], max(1, remaining * loads[i] // pool), rest)
            holding[i] = holding[i] + addition
            rest = rest - addition
    return np.array([most] + holding)


def uneven(own_key, count, total, limit, skew):
    if count == 2:
        one = jax.random.randint(own_key, (), max(1, total - limit), min(limit, total - 1) + 1)
        return jnp.stack([one, total - one])
    tallies = jnp.asarray(length_profile(count, total, limit, skew), jnp.int32)
    twos = (count - 1) // 2
    donor, taker = tallies[1:1 + 2 * twos:2], tallies[2:2 + 2 * twos:2]
    room = jnp.minimum(donor - 1, limit - taker)
    moved = jax.random.randint(jax.random.fold_in(own_key, 1), (twos,), 0, 1 << 20) % (room + 1)
    tallies = tallies.at[1:1 + 2 * twos:2].set(donor - moved).at[2:2 + 2 * twos:2].set(taker + moved)
    return tallies[jax.random.permutation(jax.random.fold_in(own_key, 2), count)]


def gaussian(key, dims, scale, bound, cuts=(), held_as=jnp.bfloat16):
    level = block_levels(key, dims, cuts, -0.22, 0.18) if cuts else 1.0
    array = jax.random.normal(key, dims, jnp.float32) * scale * level
    return jnp.minimum(jnp.maximum(array, -bound), bound).astype(held_as)


def gaussian_with(stream_key, extent, scale, most, cuts, heavy, kind=jnp.bfloat16):
    values = scale * jax.random.normal(stream_key, extent, jnp.float32)
    if cuts:
        values = values * block_levels(stream_key, extent, cuts, -0.22, 0.18)
    return jnp.clip(spiked(values, jax.random.fold_in(stream_key, 3), *heavy), -most, most).astype(kind)


def setup_inputs(seed: int = 0) -> dict:
    key_of = jax.random.split(jax.random.key(seed), 16)
    return {
        "tokens": gaussian_with(key_of[0], (MICRO, TOKENS, D), 1.0, 6.0, ((1, 16),), (1, 2, 16, 2.0)),
        "segments": jax.vmap(lambda own: jnp.searchsorted(jnp.cumsum(uneven(own, SEGS, TOKENS, 2 * DOC, 1)), jnp.arange(TOKENS), side="right"))(jax.random.split(key_of[1], MICRO)).reshape((MICRO, TOKENS)).astype(jnp.int32),
        "cotangent": gaussian(key_of[2], (MICRO, TOKENS, D), 1.0, 6.0, ((1, 16),), jnp.float32),
        "ln1_gain": jnp.clip(1.0 + 0.18 * jax.random.normal(key_of[3], (LAYERS, D), jnp.float32), 0.099609375, 1.8984375).astype(jnp.bfloat16),
        "ln1_bias": gaussian(key_of[4], (LAYERS, D), 0.5, 3.0, ((0, 2), (1, 16))),
        "ln2_gain": jnp.clip(1.0 + 0.18 * jax.random.normal(key_of[5], (LAYERS, D), jnp.float32), 0.099609375, 1.8984375).astype(jnp.bfloat16),
        "ln2_bias": gaussian(key_of[6], (LAYERS, D), 0.5, 3.0, ((0, 2), (1, 16))),
        "qkv_weight": gaussian(key_of[7], (LAYERS, D, 3 * D), D ** -0.5, 0.21875, ((0, 2), (1, 16))),
        "qkv_bias": gaussian(key_of[8], (LAYERS, 3 * D), 0.5, 3.0, ((0, 2), (1, 16))),
        "out_weight": gaussian(key_of[9], (LAYERS, D, D), (D // 16) ** -0.5, 0.875, ((0, 2), (1, 16))),
        "out_bias": gaussian(key_of[10], (LAYERS, D), 0.5, 3.0, ((0, 2), (1, 16))),
        "up_weight": gaussian(key_of[11], (LAYERS, D, FF), D ** -0.5, 0.21875, ((0, 2), (1, 16))),
        "up_bias": gaussian(key_of[12], (LAYERS, FF), 0.5, 3.0, ((0, 2), (1, 16))),
        "down_weight": gaussian(key_of[13], (LAYERS, FF, D), (FF // 2) ** -0.5, 0.15625, ((0, 2), (1, 16))),
        "down_bias": gaussian(key_of[14], (LAYERS, D), 0.5, 3.0, ((0, 2), (1, 16))),
    }


@jax.custom_vjp
def low(v):
    return lax.optimization_barrier(v.astype(jnp.bfloat16)).astype(jnp.float32)

@jax.custom_vjp
def low_back(v):
    return v

def low_keep(v):
    return (low(v), None)

def low_pass(kept, grad):
    return (grad,)

def back_keep(v):
    return (v, None)

def back_low(kept, grad):
    return (low(grad),)
low.defvjp(low_keep, low_pass)
low_back.defvjp(back_keep, back_low)
HIGHEST = lax.Precision.HIGHEST

def layer_norm(values, norm_gain, norm_shift):
    center = values - lax.optimization_barrier(jnp.mean(values, axis=-1, keepdims=True))
    spread = lax.optimization_barrier(jnp.mean(center * center, axis=-1, keepdims=True))
    return center * lax.rsqrt(spread + 1e-05) * norm_gain + norm_shift

def positions(seg_row):
    index_row = jnp.arange(seg_row.shape[0], dtype=jnp.int32)
    starts = jnp.concatenate([jnp.ones((1,), dtype=jnp.bool_), seg_row[1:] != seg_row[:-1]])
    begin_at = lax.cummax(jnp.where(starts, index_row, jnp.zeros_like(index_row)), axis=0)
    return index_row - begin_at

def rotate(heads_in, pos_row):
    half_rot = ROT // 2
    frequency = 10000.0 ** (-2.0 * jnp.arange(half_rot, dtype=jnp.float32) / ROT)
    angles = pos_row.astype(jnp.float32)[:, None] * frequency[None, :]
    cosine = jnp.cos(angles)[:, None, :]
    sine_part = jnp.sin(angles)[:, None, :]
    front_half = heads_in[..., :half_rot]
    back_part = heads_in[..., half_rot:ROT]
    return jnp.concatenate([front_half * cosine - back_part * sine_part, back_part * cosine + front_half * sine_part, heads_in[..., ROT:]], axis=-1)

def attend_sequence(pieces):
    queries, key_heads, values, seg_row = pieces
    length = queries.shape[0]
    block_rows = min(512, length)
    index_row = jnp.arange(length, dtype=jnp.int32)
    score_scale = HEAD_DIM ** (-0.5)

    def one_block(block_index):
        start_row = block_index * block_rows
        query_block = lax.dynamic_slice_in_dim(queries, start_row, block_rows, 0)
        seg_block = lax.dynamic_slice_in_dim(seg_row, start_row, block_rows, 0)
        rows_at = start_row + jnp.arange(block_rows, dtype=jnp.int32)
        raw_score = jnp.einsum('qhd,khd->hqk', query_block, key_heads, precision=HIGHEST) * score_scale
        masked_score = low_back(raw_score)
        allowed = (rows_at[:, None] >= index_row[None, :]) & (seg_block[:, None] == seg_row[None, :])
        masked_score = jnp.where(allowed[None], masked_score, -1e+30)
        shifted = jnp.exp(masked_score - lax.optimization_barrier(jnp.max(masked_score, axis=-1, keepdims=True)))
        attn_prob = low(shifted / lax.optimization_barrier(jnp.sum(shifted, axis=-1, keepdims=True)))
        return jnp.einsum('hqk,khd->qhd', attn_prob, values, precision=HIGHEST)
    blocks = lax.map(jax.checkpoint(one_block), jnp.arange(length // block_rows, dtype=jnp.int32))
    return blocks.reshape(length, D)

def apply_layer(hidden_in, seg_rows, parameters):
    gain_one, shift_one, gain_two, shift_two, w_qkv, b_qkv, w_out, b_out, w_up, b_up, w_down, b_down = parameters
    rows_in = hidden_in.reshape(-1, D)
    seq_count = rows_in.shape[0] // LEN
    normed = low(layer_norm(rows_in, gain_one, shift_one))
    joined_qkv = low_back(jnp.dot(normed, w_qkv, precision=HIGHEST) + b_qkv)
    pos_rows = jax.vmap(positions)(seg_rows)
    turn_all = jax.vmap(rotate)
    queries = low(turn_all(joined_qkv[:, :D].reshape(seq_count, LEN, HEADS, HEAD_DIM), pos_rows))
    key_heads = low(turn_all(joined_qkv[:, D:2 * D].reshape(seq_count, LEN, HEADS, HEAD_DIM), pos_rows))
    values = low(joined_qkv[:, 2 * D:].reshape(seq_count, LEN, HEADS, HEAD_DIM))
    context = lax.map(attend_sequence, (queries, key_heads, values, seg_rows))
    context = low(low_back(context.reshape(-1, D)))
    second = low(layer_norm(rows_in, gain_two, shift_two))
    upward = low_back(jnp.dot(second, w_up, precision=HIGHEST) + b_up)
    middle = low(jax.nn.gelu(upward, approximate=False))
    branch = low_back(jnp.dot(context, w_out, precision=HIGHEST) + b_out + jnp.dot(middle, w_down, precision=HIGHEST) + b_down)
    return (rows_in + branch).reshape(hidden_in.shape)

def reference(tokens, segments, cotangent, ln1_gain, ln1_bias, ln2_gain, ln2_bias, qkv_weight, qkv_bias, out_weight, out_bias, up_weight, up_bias, down_weight, down_bias):
    parameters = tuple((member.astype(jnp.float32) for member in (ln1_gain, ln1_bias, ln2_gain, ln2_bias, qkv_weight, qkv_bias, out_weight, out_bias, up_weight, up_bias, down_weight, down_bias)))
    start_rows = tokens.astype(jnp.float32)
    seg_rows = segments.reshape(-1, LEN)
    zero_mid = jnp.zeros_like(start_rows)

    def forward(first_in, mid_extra, *flat):
        lower_out = apply_layer(first_in, seg_rows, tuple((member[0] for member in flat)))
        mid_value = low(low_back(lower_out)) + mid_extra
        upper_out = apply_layer(mid_value, seg_rows, tuple((member[1] for member in flat)))
        return (lower_out, upper_out)
    (lower_out, upper_out), pullback = jax.vjp(forward, start_rows, zero_mid, *parameters)
    gradients = pullback((jnp.zeros_like(lower_out), cotangent.astype(jnp.float32)))
    section_outputs = jnp.stack([lower_out, upper_out]).astype(jnp.bfloat16)
    input_grads = jnp.stack([gradients[0], gradients[1]])
    return (section_outputs, input_grads, gradients[2], gradients[3], gradients[4], gradients[5], gradients[6], gradients[7], gradients[8], gradients[9], gradients[10], gradients[11], gradients[12], gradients[13])
```

```python
import jax
import jax.numpy as jnp
import numpy as np
from jax import lax
from jax.experimental import pallas as pl
from jax.experimental.pallas import tpu as pltpu
from jax.sharding import PartitionSpec as P

D = 768
HEADS = 12
HEAD_DIM = 64
FF = 3072
ROT = 16
HALF = D // 2
PAIR = 2 * HEAD_DIM
PAIRS = HALF // PAIR
FFH = FF // 2
LANES = 2 * D
QKVH = 3 * HALF
PAD = 16
SCALE = HEAD_DIM**-0.5
F32 = jnp.float32
BF16 = jnp.bfloat16

SMALL = (1, 1, 1, 1, 3, 1, 4, 1)


def pick(is_zero, first, second):
    return jnp.where(is_zero, first, second)


def swap_core(block):
    n = lax.axis_size("dp")
    return lax.ppermute(block, "dp", [(i, i ^ 1) for i in range(n)])


def swap_section(block):
    return lax.ppermute(block, "section", [(0, 1), (1, 0)])


def ring_order(chips):
    rows = chips // 2
    return [2 * z for z in range(rows)] + [2 * z + 1 for z in reversed(range(rows))]


class Ring:
    def __init__(self, n):
        self.chips = n // 2
        self.order = ring_order(self.chips)
        place = [0] * self.chips
        for position, chip in enumerate(self.order):
            place[chip] = position
        chip = lax.axis_index("dp") // 2
        self.position = jnp.asarray(place, jnp.int32)[chip]
        self.table = jnp.asarray(self.order, jnp.int32)
        self.right = self.route(1)
        self.left = self.route(-1)

    def route(self, step):
        k = len(self.order)
        pairs = []
        for i in range(k):
            source, target = self.order[i], self.order[(i + step) % k]
            pairs += [(2 * source, 2 * target), (2 * source + 1, 2 * target + 1)]
        return pairs

    def chip_at(self, offset):
        return self.table[lax.rem(self.position + offset + self.chips, self.chips)]

    def gather(self, own):
        (own,) = yield [own]
        found = [(self.chip_at(0), own)]
        reach = self.chips // 2
        ahead = back = own
        for k in range(1, reach):
            ahead = lax.ppermute(ahead, "dp", self.right)
            back = lax.ppermute(back, "dp", self.left)
            ahead, back = yield [ahead, back]
            found += [(self.chip_at(-k), ahead), (self.chip_at(k), back)]
        cut = own.shape[0] // 32 * 16
        ahead = lax.ppermute(ahead[:cut], "dp", self.right)
        back = lax.ppermute(back[cut:], "dp", self.left)
        ahead, back = yield [ahead, back]
        found.append((self.chip_at(reach), jnp.concatenate([ahead, back])))
        return found

    def scatter(self, block_of, rows):
        reach = self.chips // 2
        cut = rows // 32 * 16
        far = block_of(self.chip_at(reach))
        ahead, back = yield [far[:cut], far[cut:]]
        ahead = lax.ppermute(ahead, "dp", self.right)
        back = lax.ppermute(back, "dp", self.left)
        ahead, back = yield [ahead, back]
        own = block_of(self.chip_at(reach - 1))
        ahead = jnp.concatenate([add_low(ahead, own[:cut]), own[cut:]])
        own = block_of(self.chip_at(1 - reach))
        back = jnp.concatenate([own[:cut], add_low(back, own[cut:])])
        for k in range(reach - 2, -1, -1):
            ahead = lax.ppermute(ahead, "dp", self.right)
            back = lax.ppermute(back, "dp", self.left)
            ahead, back = yield [ahead, back]
            if k:
                ahead = add_low(ahead, block_of(self.chip_at(k)))
                back = add_low(back, block_of(self.chip_at(-k)))
        own = block_of(self.chip_at(0))
        return own.astype(F32) + ahead.astype(F32) + back.astype(F32)


class Track:
    def __init__(self):
        self.waiting, self.active, self.held = [], None, []
        self.done = {}

    def push(self, name, steps):
        self.waiting.append((name, steps))

    def step(self, values=()):
        if self.active is None:
            if not self.waiting:
                return values
            self.active = self.waiting.pop(0)
            self.held = next(self.active[1])
        self.held, values = lax.optimization_barrier((self.held, values))
        while True:
            try:
                self.held = self.active[1].send(self.held)
                return values
            except StopIteration as end:
                self.done[self.active[0]] = end.value
                last, self.active = self.held, None
                if not self.waiting:
                    return values
                self.active = self.waiting.pop(0)
                self.held, last = lax.optimization_barrier((next(self.active[1]), last))

    def finish(self, name):
        while name not in self.done:
            self.step()
        return self.done[name]


def add_low(one, two):
    return (one.astype(F32) + two.astype(F32)).astype(BF16)


def same_core(n):
    return [[c + 2 * i for i in range(n // 2)] for c in (0, 1)]


def rotary_tables(segs):
    length = segs.shape[1]
    begin = jnp.sum((segs[:, None, :] < segs[:, :, None]).astype(jnp.int32), axis=2)
    place = (jnp.arange(length, dtype=jnp.int32)[None] - begin).reshape(-1).astype(F32)[:, None]
    half = ROT // 2
    freq = 10000.0 ** (-2.0 * jnp.arange(half, dtype=F32) / ROT)
    rest = jnp.zeros(HEAD_DIM - ROT, F32)
    freq = jnp.tile(jnp.concatenate([freq, freq, rest]), 2)[None]
    first = np.tile(np.arange(HEAD_DIM) < half, 2)[None]
    angle = place * freq
    sin = jnp.sin(angle)
    return jnp.concatenate([jnp.cos(angle), jnp.where(first, -sin, sin)], axis=1), begin.reshape(-1)[:, None]


def turned(x, table, sign):
    lane = lax.rem(lax.broadcasted_iota(jnp.int32, x.shape, 1), HEAD_DIM)
    partner = jnp.where(lane < ROT // 2, pltpu.roll(x, PAIR - ROT // 2, 1), pltpu.roll(x, ROT // 2, 1))
    moved = partner * table[:, PAIR:]
    return x * table[:, :PAIR] + moved if sign > 0 else x * table[:, :PAIR] - moved


def dot_nt(a, b):
    return lax.dot_general(a, b, (((1,), (1,)), ((), ())), preferred_element_type=F32)


def dot_tn(a, b):
    return lax.dot_general(a, b, (((0,), (0,)), ((), ())), preferred_element_type=F32)


def kept(begin, row0, rows, keys):
    key = lax.broadcasted_iota(jnp.int32, (rows, keys), 1)
    row = lax.broadcasted_iota(jnp.int32, (rows, keys), 0) + row0
    return (key <= row) & (key >= begin)


def attend_kernel(joined_ref, table_ref, begin_ref, qkv_ref, ctx_ref, lse_ref):
    length = joined_ref.shape[0]
    chunk = length // 2
    table = table_ref[...]
    qkv_ref[:, :PAIR] = turned(joined_ref[:, :PAIR], table, 1).astype(BF16)
    qkv_ref[:, PAIR : 2 * PAIR] = turned(joined_ref[:, PAIR : 2 * PAIR], table, 1).astype(BF16)
    qkv_ref[:, 2 * PAIR :] = joined_ref[:, 2 * PAIR :].astype(BF16)
    for i in range(2):
        rows, keys = pl.ds(i * chunk, chunk), (i + 1) * chunk
        allowed = kept(begin_ref[rows, :], i * chunk, chunk, keys)
        ctx, lse = [], []
        for h in range(2):
            q = qkv_ref[rows, h * HEAD_DIM : (h + 1) * HEAD_DIM] * jnp.asarray(SCALE, BF16)
            k = qkv_ref[:keys, PAIR + h * HEAD_DIM : PAIR + (h + 1) * HEAD_DIM]
            v = qkv_ref[:keys, 2 * PAIR + h * HEAD_DIM : 2 * PAIR + (h + 1) * HEAD_DIM]
            score = jnp.where(allowed, dot_nt(q, k), -1e30)
            peak = jnp.max(score, axis=1, keepdims=True)
            e = jnp.exp(score - peak)
            total = jnp.sum(e, axis=1, keepdims=True)
            prob = (e * (1.0 / total)).astype(BF16)
            ctx.append(jnp.dot(prob, v, preferred_element_type=F32))
            lse.append(jnp.broadcast_to(peak + jnp.log(total), (chunk, HEAD_DIM)))
        ctx_ref[rows, :] = jnp.concatenate(ctx, axis=1).astype(BF16)
        lse_ref[rows, :] = jnp.concatenate(lse, axis=1)


def attend_back_kernel(qkv_ref, lse_ref, dctx_ref, table_ref, begin_ref, out_ref):
    length = qkv_ref.shape[0]
    chunk = length // 2
    dqs, dks, dvs = [], [], []
    for h in range(2):
        head = slice(h * HEAD_DIM, (h + 1) * HEAD_DIM)
        k_at = slice(PAIR + h * HEAD_DIM, PAIR + (h + 1) * HEAD_DIM)
        v_at = slice(2 * PAIR + h * HEAD_DIM, 2 * PAIR + (h + 1) * HEAD_DIM)
        dq, dk, dv = [], None, None
        for i in (1, 0):
            rows, keys = pl.ds(i * chunk, chunk), (i + 1) * chunk
            allowed = kept(begin_ref[rows, :], i * chunk, chunk, keys)
            q = qkv_ref[rows, head] * jnp.asarray(SCALE, BF16)
            k, v = qkv_ref[:keys, k_at], qkv_ref[:keys, v_at]
            do = dctx_ref[rows, head]
            lse = lse_ref[rows, h * HEAD_DIM : h * HEAD_DIM + 1]
            p = jnp.exp(jnp.where(allowed, dot_nt(q, k) - lse, -1e30))
            part_v = dot_tn(p.astype(BF16), do)
            dp = dot_nt(do, v)
            inner = jnp.sum(p * dp, axis=1, keepdims=True)
            ds = (p * (dp - inner)).astype(BF16)
            dq.append(jnp.dot(ds, k, preferred_element_type=F32) * SCALE)
            part_k = dot_tn(ds, q)
            if dk is None:
                dk, dv = part_k, part_v
            else:
                dk = jnp.concatenate([dk[:chunk] + part_k, dk[chunk:]])
                dv = jnp.concatenate([dv[:chunk] + part_v, dv[chunk:]])
        dqs.append(jnp.concatenate([dq[1], dq[0]]))
        dks.append(dk)
        dvs.append(dv)
    table = table_ref[...]
    out_ref[:, :PAIR] = turned(jnp.concatenate(dqs, axis=1), table, -1).astype(BF16)
    out_ref[:, PAIR : 2 * PAIR] = turned(jnp.concatenate(dks, axis=1), table, -1).astype(BF16)
    out_ref[:, 2 * PAIR :] = jnp.concatenate(dvs, axis=1).astype(BF16)


def kernel_params():
    return pltpu.CompilerParams(vmem_limit_bytes=40 * 1024 * 1024)


def per_pair(length, width):
    return pl.BlockSpec((length, width), lambda s, p: (s, p))


def per_row(length, width):
    return pl.BlockSpec((length, width), lambda s, p: (s, 0))


def attend(joined, table, begin):
    tokens = joined.shape[0]
    length = tokens // 2
    return pl.pallas_call(
        attend_kernel,
        grid=(2, PAIRS),
        in_specs=[per_pair(length, 3 * PAIR), per_row(length, 2 * PAIR), per_row(length, 1)],
        out_specs=[per_pair(length, 3 * PAIR), per_pair(length, PAIR), per_pair(length, PAIR)],
        out_shape=[
            jax.ShapeDtypeStruct((tokens, QKVH), BF16),
            jax.ShapeDtypeStruct((tokens, HALF), BF16),
            jax.ShapeDtypeStruct((tokens, HALF), F32),
        ],
        compiler_params=kernel_params(),
        cost_estimate=pl.CostEstimate(flops=20_000_000_000, bytes_accessed=12_000_000, transcendentals=3_000_000),
    )(joined, table, begin)


def attend_back(qkv, lse, dctx, table, begin):
    tokens = qkv.shape[0]
    length = tokens // 2
    return pl.pallas_call(
        attend_back_kernel,
        grid=(2, PAIRS),
        in_specs=[
            per_pair(length, 3 * PAIR),
            per_pair(length, PAIR),
            per_pair(length, PAIR),
            per_row(length, 2 * PAIR),
            per_row(length, 1),
        ],
        out_specs=per_pair(length, 3 * PAIR),
        out_shape=jax.ShapeDtypeStruct((tokens, QKVH), BF16),
        compiler_params=kernel_params(),
        cost_estimate=pl.CostEstimate(flops=30_000_000_000, bytes_accessed=12_000_000, transcendentals=3_000_000),
    )(qkv, lse, dctx, table, begin)


def normalized(rows):
    center = rows - jnp.mean(rows, axis=-1, keepdims=True)
    spread = jnp.mean(center * center, axis=-1, keepdims=True)
    scale = lax.rsqrt(spread + 1e-05)
    return center * scale, scale


def matmul(a, b):
    return jnp.dot(a, b, preferred_element_type=F32)


def forward_attend(source, weights, table, begin, track):
    normed, scale = normalized(source.astype(F32))
    one = (normed * weights["g1"] + weights["b1"]).astype(BF16)
    two = (normed * weights["g2"] + weights["b2"]).astype(BF16)
    joined = matmul(one, weights["qkv"]) + weights["bqkv"]
    one, two, joined = track.step((one, two, joined))
    qkv, ctx, lse = track.step(attend(joined, table, begin))
    return source, one, two, qkv, ctx, lse


def forward_hidden(saved, weights, track):
    two, ctx = saved[2], saved[4]
    up = matmul(two, weights["up"]) + weights["bup"]
    phi = 0.5 * (1.0 + lax.erf(up * np.float32(0.5**0.5)))
    middle = (up * phi).astype(BF16)
    slope = (phi + up * jnp.exp(-0.5 * up * up) * np.float32((2 * np.pi) ** -0.5)).astype(BF16)
    middle, slope = track.step((middle, slope))
    part = matmul(ctx, weights["out"]) + matmul(middle, weights["down"])
    (part,) = track.step((part,))
    return part, (*saved, middle, slope)


def backward(saved, grad, weights, table, begin, track, send_hidden):
    source, one, two, qkv, ctx, lse, middle, slope = saved
    d_up = (dot_nt(grad, weights["down"]) * slope.astype(F32)).astype(BF16)
    (d_up,) = track.step((d_up,))
    down_grad = dot_tn(middle, grad).astype(BF16)
    up_grad = dot_tn(two, d_up).astype(BF16)
    send_hidden(up_grad, down_grad)
    d_ctx = dot_nt(grad, weights["out"]).astype(BF16)
    (d_ctx, d_up) = track.step((d_ctx, d_up))
    d_fused = attend_back(qkv, lse, d_ctx, table, begin)
    (d_fused, d_up) = track.step((d_fused, d_up))
    d_two = dot_nt(d_up, weights["up"])
    out_grad = dot_tn(ctx, grad).astype(BF16)
    qkv_grad = dot_tn(one, d_fused).astype(BF16)
    d_one = dot_nt(d_fused, weights["qkv"])
    d_one, d_two = track.step((d_one, d_two))
    normed, scale = normalized(source.astype(F32))
    mixed = d_one * weights["g1"] + d_two * weights["g2"]
    part = scale * (
        mixed
        - jnp.mean(mixed, axis=-1, keepdims=True)
        - normed * jnp.mean(mixed * normed, axis=-1, keepdims=True)
    )
    small = (
        jnp.sum(d_one * normed, axis=0),
        jnp.sum(d_one, axis=0),
        jnp.sum(d_two * normed, axis=0),
        jnp.sum(d_two, axis=0),
        jnp.sum(d_fused.astype(F32), axis=0),
        None,
        jnp.sum(d_up.astype(F32), axis=0),
        None,
    )
    return part, qkv_grad, out_grad, small


def body(
    tokens,
    segments,
    cotangent,
    ln1_gain,
    ln1_bias,
    ln2_gain,
    ln2_bias,
    qkv_weight,
    qkv_bias,
    out_weight,
    out_bias,
    up_weight,
    up_bias,
    down_weight,
    down_bias,
):
    n = lax.axis_size("dp")
    chips = n // 2
    r = D // n
    u = 2 * r
    f = FF // n
    section = lax.axis_index("section")
    dp = lax.axis_index("dp")
    core = lax.rem(dp, 2)
    low_core, low_section = core == 0, section == 0
    ring = Ring(n) if chips == 8 else None

    track = Track()

    def columns_for(t):
        wq, wo = qkv_weight[0], out_weight[0]
        columns = [
            wq[:, D * i + HALF * t + PAIR * p : D * i + HALF * t + PAIR * (p + 1)]
            for p in range(PAIRS)
            for i in range(3)
        ] + [wo[:, HALF * t : HALF * (t + 1)]]
        return jnp.concatenate(columns, axis=1)

    def hidden_for(t):
        return up_weight[0].reshape(r, chips, 2, f)[:, :, t].reshape(r, FFH)

    vectors = (ln1_gain, ln1_bias, ln2_gain, ln2_bias, qkv_bias, out_bias, up_bias, down_bias)
    own_small = jnp.concatenate([jnp.pad(v, ((0, 0), (0, LANES - v.shape[1]))) for v in vectors])

    def shared(for_core, rest):
        zero, one_ = for_core(0), for_core(1)
        mine, sent = pick(low_core, zero, one_), pick(low_core, one_, zero)
        if rest is not None:
            mine, sent = jnp.concatenate([mine, rest]), jnp.concatenate([sent, rest])
        theirs = swap_core(sent)
        return pick(low_core, mine, theirs), pick(low_core, theirs, mine)

    a, b = shared(columns_for, own_small)
    attn_block = jnp.concatenate([a[:r], b[:r], a[r:], b[r:]])
    other = swap_section(attn_block)
    attn_blocks = (pick(low_section, attn_block, other), pick(low_section, other, attn_block))
    a, b = shared(hidden_for, None)
    down = down_weight[0]
    mlp_block = jnp.concatenate([a, b, jnp.concatenate([down[:u], down[u:]], axis=1)])
    other = swap_section(mlp_block)
    mlp_blocks = (pick(low_section, mlp_block, other), pick(low_section, other, mlp_block))

    for layer in (0, 1):
        for kind, blocks in (("attn", attn_blocks), ("mlp", mlp_blocks)):
            if ring is not None:
                track.push((kind, layer), ring.gather(blocks[layer]))

    def gathered(kind, layer, sizes):
        if ring is None:
            own = (attn_blocks if kind == "attn" else mlp_blocks)[layer]
            every = lax.all_gather(own, "dp", axis=0, axis_index_groups=same_core(n))
            return every[:, : sizes[0]], every[:, sizes[0] :]
        parts = [jnp.zeros((chips, k, LANES), BF16) for k in sizes]
        for chip, piece in track.finish((kind, layer)):
            cuts = (piece[: sizes[0]], piece[sizes[0] :])
            parts = [lax.dynamic_update_index_in_dim(p, c, chip, 0) for p, c in zip(parts, cuts)]
        return parts

    def attn_weights(layer):
        qo, small = gathered("attn", layer, (u, PAD))
        qo = qo.reshape(D, LANES)
        columns = qo[:, QKVH:]
        halves = (columns[:HALF], columns[HALF:])
        kept_rows = pick(low_core, *halves)
        got = swap_core(pick(low_core, *halves[::-1]))
        small = small.reshape(n, len(SMALL), LANES).astype(F32)
        vectors = [small[:, i, : size * r].reshape(size * D) for i, size in enumerate(SMALL)]
        bq = vectors[4].reshape(3, 2, PAIRS, PAIR)
        bu = vectors[6].reshape(chips, 2, f)
        return {
            "g1": vectors[0],
            "b1": vectors[1],
            "g2": vectors[2],
            "b2": vectors[3],
            "qkv": qo[:, :QKVH],
            "bqkv": pick(low_core, bq[:, 0], bq[:, 1]).transpose(1, 0, 2).reshape(QKVH),
            "out": jnp.concatenate(
                [pick(low_core, kept_rows, got), pick(low_core, got, kept_rows)], axis=1
            ),
            "bout": vectors[5] + vectors[7],
            "bup": pick(low_core, bu[:, 0], bu[:, 1]).reshape(FFH),
        }

    def mlp_weights(layer):
        up, folded = gathered("mlp", layer, (u, u))
        return {
            "up": up.reshape(D, FFH),
            "down": jnp.stack([folded[:, :, :D], folded[:, :, D:]], axis=1).reshape(FFH, D),
        }

    length = tokens.shape[1]

    def paired(own):
        got = swap_core(own)
        return jnp.concatenate([pick(low_core, own, got), pick(low_core, got, own)])

    def own_half(rows):
        return pick(low_core, rows[:length], rows[length:])

    def other_half(rows):
        return pick(low_core, rows[length:], rows[:length])

    def summed(part):
        return own_half(part) + swap_core(other_half(part).astype(BF16)).astype(F32)

    own_tokens = pick(low_section, tokens[0], tokens[1])
    own_seg = pick(low_section, segments[0], segments[1])
    own_cot = pick(low_section, cotangent[0], cotangent[1])
    cot_low = own_cot.astype(BF16)
    (both, own_seg) = track.step((own_tokens, own_seg))
    table, begin = rotary_tables(paired(own_seg[None]))
    both = paired(both)

    weights_0 = attn_weights(0)
    saved_0 = forward_attend(both, weights_0, table, begin, track)
    weights_0.update(mlp_weights(0))
    part, saved_0 = forward_hidden(saved_0, weights_0, track)
    mid = (own_tokens.astype(F32) + summed(part) + weights_0["bout"]).astype(BF16)
    (mid,) = track.step((mid,))
    both = paired(mid)
    weights_1 = attn_weights(1)
    saved_1 = forward_attend(both, weights_1, table, begin, track)
    weights_1.update(mlp_weights(1))
    part, saved_1 = forward_hidden(saved_1, weights_1, track)
    last = (mid.astype(F32) + summed(part) + weights_1["bout"]).astype(BF16)
    kept_rows, got = pick(low_section, mid, last), swap_section(pick(low_section, last, mid))
    outputs = jnp.stack([pick(low_section, kept_rows, got), pick(low_section, got, kept_rows)])

    def reduce_group(name, group):
        if ring is None:
            block = jnp.concatenate(group, axis=1)
            summed_block = lax.psum_scatter(block, "dp", scatter_dimension=0, axis_index_groups=same_core(n))
            track.done[name] = summed_block.astype(F32)
            return

        def block_of(chip):
            cuts = [lax.dynamic_index_in_dim(g, chip, 0, keepdims=False) for g in group]
            return jnp.concatenate(cuts)

        track.push(name, ring.scatter(block_of, sum(g.shape[1] for g in group)))

    def send_mlp(layer, up_grad, down_grad):
        down_rows = down_grad.reshape(chips, 2, u, D)
        down_rows = jnp.concatenate([down_rows[:, 0], down_rows[:, 1]], axis=2)
        reduce_group(("d_mlp", layer), (up_grad.reshape(chips, u, LANES), down_rows))

    def send_attn(layer, qkv_grad, out_grad, small, own_grad):
        halves = (out_grad[:, :HALF], out_grad[:, HALF:])
        kept_columns = pick(low_core, *halves)
        got = swap_core(pick(low_core, *halves[::-1]))
        out_rows = jnp.concatenate([pick(low_core, kept_columns, got), pick(low_core, got, kept_columns)])
        bias = jnp.sum(own_grad.astype(F32), axis=0)
        bq = small[4].reshape(PAIRS, 3, PAIR).transpose(1, 0, 2)
        bu = small[6].reshape(chips, f)
        none_q, none_u = jnp.zeros_like(bq), jnp.zeros_like(bu)
        bq = jnp.stack([pick(low_core, bq, none_q), pick(low_core, none_q, bq)], axis=1)
        bu = jnp.stack([pick(low_core, bu, none_u), pick(low_core, none_u, bu)], axis=1)
        vectors = [v.reshape(n, 1, -1) for v in (*small[:4], bq, bias, bu, bias)]
        rows = [jnp.pad(v, ((0, 0), (0, 0), (0, LANES - v.shape[2]))) for v in vectors]
        flat = jnp.concatenate(rows, axis=1).astype(BF16).reshape(chips, PAD, LANES)
        qo = jnp.concatenate([qkv_grad, out_rows], axis=1).reshape(chips, u, LANES)
        reduce_group(("d_attn", layer), (qo, flat))

    both_grad = paired(cot_low)
    part, qkv_grad, out_grad, small = backward(
        saved_1, both_grad, weights_1, table, begin, track, lambda *g: send_mlp(1, *g)
    )
    send_attn(1, qkv_grad, out_grad, small, cot_low)
    grad_1 = own_cot + summed(part)
    low_1 = grad_1.astype(BF16)
    (low_1, grad_1) = track.step((low_1, grad_1))
    both_grad = paired(low_1)
    part, qkv_grad, out_grad, small = backward(
        saved_0, both_grad, weights_0, table, begin, track, lambda *g: send_mlp(0, *g)
    )
    send_attn(0, qkv_grad, out_grad, small, low_1)
    grad_0 = low_1.astype(F32) + summed(part)
    (grad_0,) = track.step((grad_0,))
    sent = swap_section(pick(low_section, grad_1, grad_0).astype(BF16)).astype(F32)
    kept_rows = pick(low_section, grad_0, grad_1)
    in_grads = jnp.stack([pick(low_section, kept_rows, sent), pick(low_section, sent, kept_rows)])

    def of_section(kind):
        zero, one_ = track.finish((kind, 0)), track.finish((kind, 1))
        got = swap_section(pick(low_section, one_, zero).astype(BF16))
        return pick(low_section, zero, one_) + got.astype(F32)

    def of_core(block, half):
        keep = pick(low_core, block[:half], block[half:])
        got = swap_core(pick(low_core, block[half:], block[:half]).astype(BF16)).astype(F32)
        return pick(low_core, keep, got), pick(low_core, got, keep), keep + got

    mlp = of_section("d_mlp")
    m0, m1, _ = of_core(mlp[:u], r)
    up_out = jnp.stack([m0.reshape(r, chips, f), m1.reshape(r, chips, f)], axis=2).reshape(r, FF)
    down_out = jnp.concatenate([mlp[u:, :D], mlp[u:, D:]])
    attn = of_section("d_attn")
    rows = len(SMALL)
    a0, a1, both_sum = of_core(
        jnp.concatenate([attn[:r], attn[u : u + rows], attn[r:u], attn[u + rows :]]), r + rows
    )
    qkv_out = jnp.concatenate(
        [
            half[:r, (3 * p + i) * PAIR : (3 * p + i + 1) * PAIR]
            for i in range(3)
            for half in (a0, a1)
            for p in range(PAIRS)
        ],
        axis=1,
    )
    out_out = jnp.concatenate([a0[:r, QKVH:], a1[:r, QKVH:]], axis=1)
    g1, b1, g2, b2, bq, bo, bu, bd = [both_sum[r + i : r + i + 1, : size * r] for i, size in enumerate(SMALL)]
    return (
        outputs[None],
        in_grads[None],
        g1,
        b1,
        g2,
        b2,
        qkv_out[None],
        bq,
        out_out[None],
        bo,
        up_out[None],
        bu,
        down_out[None],
        bd,
    )


def solution(mesh):
    row, matrix = P("section", "dp"), P("section", "dp", None)
    params = (row, row, row, row, matrix, row, matrix, row, matrix, row, matrix, row)
    return jax.shard_map(
        body,
        mesh=mesh,
        in_specs=(P(None, "dp", None), P(None, "dp"), P(None, "dp", None)) + params,
        out_specs=(P("section", None, "dp", None), P("section", None, "dp", None)) + params,
        check_vma=False,
    )
```

```python
import jax
import jax.numpy as jnp
import numpy as np
from jax import lax
from jax.experimental import pallas as pl
from jax.experimental.pallas import tpu as pltpu
from jax.sharding import PartitionSpec as P

D = 768
HEADS = 12
HEAD_DIM = 64
FF = 3072
ROT = 16
HALF = D // 2
PAIR = 2 * HEAD_DIM
PAIRS = HALF // PAIR
FFH = FF // 2
LANES = 2 * D
QKVH = 3 * HALF
PAD = 16
SCALE = HEAD_DIM**-0.5
F32 = jnp.float32
BF16 = jnp.bfloat16

SMALL = (1, 1, 1, 1, 3, 1, 4, 1)


def pick(is_zero, first, second):
    return jnp.where(is_zero, first, second)


def swap_core(block):
    n = lax.axis_size("dp")
    return lax.ppermute(block, "dp", [(i, i ^ 1) for i in range(n)])


def swap_section(block):
    return lax.ppermute(block, "section", [(0, 1), (1, 0)])


def ring_order(chips):
    rows = chips // 2
    return [2 * z for z in range(rows)] + [2 * z + 1 for z in reversed(range(rows))]


class Ring:
    def __init__(self, n):
        self.chips = n // 2
        self.order = ring_order(self.chips)
        place = [0] * self.chips
        for position, chip in enumerate(self.order):
            place[chip] = position
        chip = lax.axis_index("dp") // 2
        self.position = jnp.asarray(place, jnp.int32)[chip]
        self.table = jnp.asarray(self.order, jnp.int32)
        self.right = self.route(1)
        self.left = self.route(-1)

    def route(self, step):
        k = len(self.order)
        pairs = []
        for i in range(k):
            source, target = self.order[i], self.order[(i + step) % k]
            pairs += [(2 * source, 2 * target), (2 * source + 1, 2 * target + 1)]
        return pairs

    def chip_at(self, offset):
        return self.table[lax.rem(self.position + offset + self.chips, self.chips)]

    def gather(self, own):
        (own,) = yield [own]
        found = [own]
        reach = self.chips // 2
        ahead = back = own
        for k in range(1, reach):
            ahead = lax.ppermute(ahead, "dp", self.right)
            back = lax.ppermute(back, "dp", self.left)
            ahead, back = yield [ahead, back]
            found += [ahead, back]
        cut = own.shape[0] // 32 * 16
        ahead = lax.ppermute(ahead[:cut], "dp", self.right)
        back = lax.ppermute(back[cut:], "dp", self.left)
        ahead, back = yield [ahead, back]
        return found + [ahead, back]

    def found_at(self):
        reach = self.chips // 2
        offsets = [0] + [o for k in range(1, reach) for o in (-k, k)] + [reach]
        return jnp.stack([self.chip_at(o) for o in offsets])

    def scatter(self, block_of, rows):
        reach = self.chips // 2
        cut = rows // 32 * 16
        far = block_of(self.chip_at(reach))
        ahead, back = yield [far[:cut], far[cut:]]
        ahead = lax.ppermute(ahead, "dp", self.right)
        back = lax.ppermute(back, "dp", self.left)
        ahead, back = yield [ahead, back]
        own = block_of(self.chip_at(reach - 1))
        ahead = jnp.concatenate([add_low(ahead, own[:cut]), own[cut:]])
        own = block_of(self.chip_at(1 - reach))
        back = jnp.concatenate([own[:cut], add_low(back, own[cut:])])
        for k in range(reach - 2, -1, -1):
            ahead = lax.ppermute(ahead, "dp", self.right)
            back = lax.ppermute(back, "dp", self.left)
            ahead, back = yield [ahead, back]
            if k:
                ahead = add_low(ahead, block_of(self.chip_at(k)))
                back = add_low(back, block_of(self.chip_at(-k)))
        own = block_of(self.chip_at(0))
        return own.astype(F32) + ahead.astype(F32) + back.astype(F32)


class Track:
    def __init__(self):
        self.waiting, self.active, self.held = [], None, []
        self.done = {}

    def push(self, name, steps):
        self.waiting.append((name, steps))

    def step(self, values=()):
        if self.active is None:
            if not self.waiting:
                return values
            self.active = self.waiting.pop(0)
            self.held = next(self.active[1])
        self.held, values = lax.optimization_barrier((self.held, values))
        while True:
            try:
                self.held = self.active[1].send(self.held)
                return values
            except StopIteration as end:
                self.done[self.active[0]] = end.value
                last, self.active = self.held, None
                if not self.waiting:
                    return values
                self.active = self.waiting.pop(0)
                self.held, last = lax.optimization_barrier((next(self.active[1]), last))

    def finish(self, name):
        while name not in self.done:
            self.step()
        return self.done[name]


def add_low(one, two):
    return (one.astype(F32) + two.astype(F32)).astype(BF16)


def same_core(n):
    return [[c + 2 * i for i in range(n // 2)] for c in (0, 1)]


def rotary_tables(segs):
    length = segs.shape[1]
    begin = jnp.sum((segs[:, None, :] < segs[:, :, None]).astype(jnp.int32), axis=2)
    place = (jnp.arange(length, dtype=jnp.int32)[None] - begin).reshape(-1).astype(F32)[:, None]
    half = ROT // 2
    freq = 10000.0 ** (-2.0 * jnp.arange(half, dtype=F32) / ROT)
    rest = jnp.zeros(HEAD_DIM - ROT, F32)
    freq = jnp.tile(jnp.concatenate([freq, freq, rest]), 2)[None]
    first = np.tile(np.arange(HEAD_DIM) < half, 2)[None]
    angle = place * freq
    sin = jnp.sin(angle)
    return jnp.concatenate([jnp.cos(angle), jnp.where(first, -sin, sin)], axis=1), begin.reshape(-1)[:, None]


def turned(x, table, sign):
    lane = lax.rem(lax.broadcasted_iota(jnp.int32, x.shape, 1), HEAD_DIM)
    partner = jnp.where(lane < ROT // 2, pltpu.roll(x, PAIR - ROT // 2, 1), pltpu.roll(x, ROT // 2, 1))
    moved = partner * table[:, PAIR:]
    return x * table[:, :PAIR] + moved if sign > 0 else x * table[:, :PAIR] - moved


def dot_nt(a, b):
    return lax.dot_general(a, b, (((1,), (1,)), ((), ())), preferred_element_type=F32)


def dot_tn(a, b):
    return lax.dot_general(a, b, (((0,), (0,)), ((), ())), preferred_element_type=F32)


def kept(begin, row0, rows, keys):
    key = lax.broadcasted_iota(jnp.int32, (rows, keys), 1)
    row = lax.broadcasted_iota(jnp.int32, (rows, keys), 0) + row0
    return (key <= row) & (key >= begin)


def attend_kernel(joined_ref, table_ref, begin_ref, qkv_ref, ctx_ref, lse_ref):
    length = joined_ref.shape[0]
    chunk = length // 2
    table = table_ref[...]
    qkv_ref[:, :PAIR] = turned(joined_ref[:, :PAIR], table, 1).astype(BF16)
    qkv_ref[:, PAIR : 2 * PAIR] = turned(joined_ref[:, PAIR : 2 * PAIR], table, 1).astype(BF16)
    qkv_ref[:, 2 * PAIR :] = joined_ref[:, 2 * PAIR :].astype(BF16)
    for i in range(2):
        rows, keys = pl.ds(i * chunk, chunk), (i + 1) * chunk
        allowed = kept(begin_ref[rows, :], i * chunk, chunk, keys)
        ctx, lse = [], []
        for h in range(2):
            q = qkv_ref[rows, h * HEAD_DIM : (h + 1) * HEAD_DIM] * jnp.asarray(SCALE, BF16)
            k = qkv_ref[:keys, PAIR + h * HEAD_DIM : PAIR + (h + 1) * HEAD_DIM]
            v = qkv_ref[:keys, 2 * PAIR + h * HEAD_DIM : 2 * PAIR + (h + 1) * HEAD_DIM]
            score = jnp.where(allowed, dot_nt(q, k), -1e30)
            peak = jnp.max(score, axis=1, keepdims=True)
            e = jnp.exp(score - peak)
            total = jnp.sum(e, axis=1, keepdims=True)
            prob = (e * (1.0 / total)).astype(BF16)
            ctx.append(jnp.dot(prob, v, preferred_element_type=F32))
            lse.append(jnp.broadcast_to(peak + jnp.log(total), (chunk, HEAD_DIM)))
        ctx_ref[rows, :] = jnp.concatenate(ctx, axis=1).astype(BF16)
        lse_ref[rows, :] = jnp.concatenate(lse, axis=1)


def attend_back_kernel(qkv_ref, lse_ref, dctx_ref, table_ref, begin_ref, out_ref):
    length = qkv_ref.shape[0]
    chunk = length // 2
    dqs, dks, dvs = [], [], []
    for h in range(2):
        head = slice(h * HEAD_DIM, (h + 1) * HEAD_DIM)
        k_at = slice(PAIR + h * HEAD_DIM, PAIR + (h + 1) * HEAD_DIM)
        v_at = slice(2 * PAIR + h * HEAD_DIM, 2 * PAIR + (h + 1) * HEAD_DIM)
        dq, dk, dv = [], None, None
        for i in (1, 0):
            rows, keys = pl.ds(i * chunk, chunk), (i + 1) * chunk
            allowed = kept(begin_ref[rows, :], i * chunk, chunk, keys)
            q = qkv_ref[rows, head] * jnp.asarray(SCALE, BF16)
            k, v = qkv_ref[:keys, k_at], qkv_ref[:keys, v_at]
            do = dctx_ref[rows, head]
            lse = lse_ref[rows, h * HEAD_DIM : h * HEAD_DIM + 1]
            p = jnp.exp(jnp.where(allowed, dot_nt(q, k) - lse, -1e30))
            part_v = dot_tn(p.astype(BF16), do)
            dp = dot_nt(do, v)
            inner = jnp.sum(p * dp, axis=1, keepdims=True)
            ds = (p * (dp - inner)).astype(BF16)
            dq.append(jnp.dot(ds, k, preferred_element_type=F32) * SCALE)
            part_k = dot_tn(ds, q)
            if dk is None:
                dk, dv = part_k, part_v
            else:
                dk = jnp.concatenate([dk[:chunk] + part_k, dk[chunk:]])
                dv = jnp.concatenate([dv[:chunk] + part_v, dv[chunk:]])
        dqs.append(jnp.concatenate([dq[1], dq[0]]))
        dks.append(dk)
        dvs.append(dv)
    table = table_ref[...]
    out_ref[:, :PAIR] = turned(jnp.concatenate(dqs, axis=1), table, -1).astype(BF16)
    out_ref[:, PAIR : 2 * PAIR] = turned(jnp.concatenate(dks, axis=1), table, -1).astype(BF16)
    out_ref[:, 2 * PAIR :] = jnp.concatenate(dvs, axis=1).astype(BF16)


def smem():
    return pl.BlockSpec(memory_space=pltpu.SMEM)


def vmem():
    return pl.BlockSpec(memory_space=pltpu.VMEM)


def pack_kernel(core_ref, wq_ref, wo_ref, wu_ref, wd_ref, *refs):
    small_refs, (attn_keep, attn_send, mlp_keep, mlp_send, fold_ref, rows_ref) = refs[:-6], refs[-6:]
    r, chips, f = wq_ref.shape[1], D // wq_ref.shape[1] // 2, wd_ref.shape[1]
    rows_ref[...] = jnp.zeros_like(rows_ref)
    for i, ref in enumerate(small_refs):
        rows_ref[i : i + 1, : ref.shape[1]] = ref[...].astype(F32)
    rows = rows_ref[...].astype(BF16)
    attn_keep[r:, :] = rows
    attn_send[r:, :] = rows
    fold_ref[:, :D] = wd_ref[0, : f // 2]
    fold_ref[:, D:] = wd_ref[0, f // 2 :]
    for core, targets in ((0, (attn_keep, attn_send)), (1, (attn_send, attn_keep))):

        @pl.when(core_ref[0] == core)
        def _(targets=targets):
            for t, ref in enumerate(targets):
                for p in range(PAIRS):
                    for i in range(3):
                        at, to = D * i + HALF * t + PAIR * p, (3 * p + i) * PAIR
                        ref[:r, to : to + PAIR] = wq_ref[0, :, at : at + PAIR]
                ref[:r, QKVH:] = wo_ref[0, :, HALF * t : HALF * (t + 1)]

    for core, targets in ((0, (mlp_keep, mlp_send)), (1, (mlp_send, mlp_keep))):

        @pl.when(core_ref[0] == core)
        def _(targets=targets):
            for t, ref in enumerate(targets):
                for j in range(chips):
                    at = (2 * j + t) * f
                    ref[:, j * f : (j + 1) * f] = wu_ref[0, :, at : at + f]


def assemble_attn_kernel(place_ref, *refs):
    blocks, (qkv_ref, keep_ref, send_ref, vec_ref, col_ref, row_ref, all_ref, bq_ref, bu_ref) = refs[:-9], refs[-9:]
    chips = len(blocks) - 1
    core = place_ref[chips]
    u = blocks[0].shape[0] - PAD
    n = 2 * chips
    r, f = u // 2, 2 * u
    for k in range(chips):
        chip = place_ref[k]
        if k < chips - 1:
            parts = [(0, u, blocks[k], 0)]
            small = blocks[k][u:, :]
        else:
            cut = blocks[k].shape[0]
            parts = [(0, cut, blocks[k], 0), (cut, u - cut, blocks[k + 1], 0)]
            small = blocks[k + 1][u - cut :, :]
        for start, count, ref, at in parts:
            rows = pl.ds(pl.multiple_of(chip * u + start, 16), count)
            qkv_ref[rows, :] = ref[at : at + count, :QKVH]
            col_ref[rows, :] = ref[at : at + count, QKVH:]
        row_ref[chip] = small[:, : row_ref.shape[2]].astype(F32)
    keep_ref[...] = col_ref[pl.ds(pl.multiple_of(core * HALF, HALF), HALF), :]
    send_ref[...] = col_ref[pl.ds(pl.multiple_of((1 - core) * HALF, HALF), HALF), :]
    for i in range(n):
        piece = row_ref[i // 2, 8 * (i % 2) : 8 * (i % 2) + 8, :]
        all_ref[:, r * i : r * (i + 1)] = piece[:, :r]
        bq_ref[:, 3 * r * i : 3 * r * (i + 1)] = piece[4:5, : 3 * r]
        bu_ref[i % 2, :, f * (i // 2) : f * (i // 2 + 1)] = piece[6:7, :f]
    vec_ref[...] = jnp.zeros_like(vec_ref)
    vec_ref[:, :D] = all_ref[...]
    vec_ref[5:6, :D] = all_ref[5:6, :] + all_ref[7:8, :]
    for c in range(2):

        @pl.when(core == c)
        def _(c=c):
            for p in range(PAIRS):
                for i in range(3):
                    at, to = D * i + HALF * c + PAIR * p, (3 * p + i) * PAIR
                    vec_ref[4:5, to : to + PAIR] = bq_ref[:, at : at + PAIR]
            vec_ref[6:7, :] = bu_ref[c]


def assemble_mlp_kernel(place_ref, *refs):
    blocks, (up_ref, down_ref) = refs[:-2], refs[-2:]
    chips = len(blocks) - 1
    u = blocks[0].shape[0] // 2
    for k in range(chips):
        chip = place_ref[k]
        if k < chips - 1:
            up, down = blocks[k].at[:u], blocks[k].at[u:]
        else:
            up, down = blocks[k], blocks[k + 1]
        up_ref[pl.ds(pl.multiple_of(chip * u, 16), u), :] = up[...]
        down_ref[pl.ds(pl.multiple_of(chip * 2 * u, 16), u), :] = down[:, :D]
        down_ref[pl.ds(pl.multiple_of(chip * 2 * u + u, 16), u), :] = down[:, D:]


def grads_mlp_kernel(two_ref, d_up_ref, middle_ref, grad_ref, out_ref):
    count, u = out_ref.shape[0], out_ref.shape[1] // 2
    up = dot_tn(two_ref[...], d_up_ref[...]).astype(BF16)
    for i in range(count):
        out_ref[i, :u, :] = up[u * i : u * (i + 1)]
    down = dot_tn(middle_ref[...], grad_ref[...]).astype(BF16)
    for i in range(count):
        out_ref[i, u:, :D] = down[2 * u * i : 2 * u * i + u]
        out_ref[i, u:, D:] = down[2 * u * i + u : 2 * u * (i + 1)]


def grads_attn_kernel(one_ref, fused_ref, out_rows_ref, all_ref, bq_ref, bu_ref, out_ref, row_ref):
    count, u = out_ref.shape[0], out_ref.shape[1] - PAD
    r = u // 2
    qkv = dot_tn(one_ref[...], fused_ref[...]).astype(BF16)
    for i in range(count):
        out_ref[i, :u, :QKVH] = qkv[u * i : u * (i + 1)]
        out_ref[i, :u, QKVH:] = out_rows_ref[u * i : u * (i + 1), :]
        row_ref[...] = jnp.zeros_like(row_ref)
        for c in range(2):
            d = 2 * i + c
            row_ref[8 * c : 8 * c + 8, :r] = all_ref[:, r * d : r * (d + 1)]
            row_ref[8 * c + 4 : 8 * c + 5, : 3 * r] = bq_ref[:, 3 * r * d : 3 * r * (d + 1)]
            row_ref[8 * c + 6 : 8 * c + 7, : 4 * r] = bu_ref[:, 4 * r * d : 4 * r * (d + 1)]
        out_ref[i, u:, :] = row_ref[...].astype(BF16)


def kernel_params():
    return pltpu.CompilerParams(vmem_limit_bytes=40 * 1024 * 1024)


def per_pair(length, width):
    return pl.BlockSpec((length, width), lambda s, p: (s, p))


def per_row(length, width):
    return pl.BlockSpec((length, width), lambda s, p: (s, 0))


def attend(joined, table, begin):
    tokens = joined.shape[0]
    length = tokens // 2
    return pl.pallas_call(
        attend_kernel,
        grid=(2, PAIRS),
        in_specs=[per_pair(length, 3 * PAIR), per_row(length, 2 * PAIR), per_row(length, 1)],
        out_specs=[per_pair(length, 3 * PAIR), per_pair(length, PAIR), per_pair(length, PAIR)],
        out_shape=[
            jax.ShapeDtypeStruct((tokens, QKVH), BF16),
            jax.ShapeDtypeStruct((tokens, HALF), BF16),
            jax.ShapeDtypeStruct((tokens, HALF), F32),
        ],
        compiler_params=kernel_params(),
        cost_estimate=pl.CostEstimate(flops=20_000_000_000, bytes_accessed=12_000_000, transcendentals=3_000_000),
    )(joined, table, begin)


def attend_back(qkv, lse, dctx, table, begin):
    tokens = qkv.shape[0]
    length = tokens // 2
    return pl.pallas_call(
        attend_back_kernel,
        grid=(2, PAIRS),
        in_specs=[
            per_pair(length, 3 * PAIR),
            per_pair(length, PAIR),
            per_pair(length, PAIR),
            per_row(length, 2 * PAIR),
            per_row(length, 1),
        ],
        out_specs=per_pair(length, 3 * PAIR),
        out_shape=jax.ShapeDtypeStruct((tokens, QKVH), BF16),
        compiler_params=kernel_params(),
        cost_estimate=pl.CostEstimate(flops=30_000_000_000, bytes_accessed=12_000_000, transcendentals=3_000_000),
    )(qkv, lse, dctx, table, begin)


def normalized(rows):
    center = rows - jnp.mean(rows, axis=-1, keepdims=True)
    spread = jnp.mean(center * center, axis=-1, keepdims=True)
    scale = lax.rsqrt(spread + 1e-05)
    return center * scale, scale


def matmul(a, b):
    return jnp.dot(a, b, preferred_element_type=F32)


def forward_attend(source, weights, table, begin, track):
    normed, scale = normalized(source.astype(F32))
    one = (normed * weights["g1"] + weights["b1"]).astype(BF16)
    two = (normed * weights["g2"] + weights["b2"]).astype(BF16)
    joined = matmul(one, weights["qkv"]) + weights["bqkv"]
    one, two, joined = track.step((one, two, joined))
    qkv, ctx, lse = track.step(attend(joined, table, begin))
    return source, one, two, qkv, ctx, lse


def forward_hidden(saved, weights, track):
    two, ctx = saved[2], saved[4]
    up = matmul(two, weights["up"]) + weights["bup"]
    phi = 0.5 * (1.0 + lax.erf(up * np.float32(0.5**0.5)))
    middle = (up * phi).astype(BF16)
    slope = (phi + up * jnp.exp(-0.5 * up * up) * np.float32((2 * np.pi) ** -0.5)).astype(BF16)
    middle, slope = track.step((middle, slope))
    part = matmul(ctx, weights["out"]) + matmul(middle, weights["down"])
    (part,) = track.step((part,))
    return part, (*saved, middle, slope)


def backward(saved, grad, weights, table, begin, track, send_hidden):
    source, one, two, qkv, ctx, lse, middle, slope = saved
    d_up = (dot_nt(grad, weights["down"]) * slope.astype(F32)).astype(BF16)
    (d_up,) = track.step((d_up,))
    send_hidden(two, d_up, middle, grad)
    d_ctx = dot_nt(grad, weights["out"]).astype(BF16)
    (d_ctx, d_up) = track.step((d_ctx, d_up))
    d_fused = attend_back(qkv, lse, d_ctx, table, begin)
    (d_fused, d_up) = track.step((d_fused, d_up))
    d_two = dot_nt(d_up, weights["up"])
    d_one = dot_nt(d_fused, weights["qkv"])
    d_one, d_two = track.step((d_one, d_two))
    normed, scale = normalized(source.astype(F32))
    mixed = d_one * weights["g1"] + d_two * weights["g2"]
    part = scale * (
        mixed
        - jnp.mean(mixed, axis=-1, keepdims=True)
        - normed * jnp.mean(mixed * normed, axis=-1, keepdims=True)
    )
    small = (
        jnp.sum(d_one * normed, axis=0),
        jnp.sum(d_one, axis=0),
        jnp.sum(d_two * normed, axis=0),
        jnp.sum(d_two, axis=0),
        jnp.sum(d_fused.astype(F32), axis=0),
        None,
        jnp.sum(d_up.astype(F32), axis=0),
        None,
    )
    return part, d_fused, small


def body(
    tokens,
    segments,
    cotangent,
    ln1_gain,
    ln1_bias,
    ln2_gain,
    ln2_bias,
    qkv_weight,
    qkv_bias,
    out_weight,
    out_bias,
    up_weight,
    up_bias,
    down_weight,
    down_bias,
):
    n = lax.axis_size("dp")
    chips = n // 2
    r = D // n
    u = 2 * r
    f = FF // n
    section = lax.axis_index("section")
    dp = lax.axis_index("dp")
    core = lax.rem(dp, 2)
    low_core, low_section = core == 0, section == 0
    ring = Ring(n) if chips == 8 else None

    track = Track()

    vectors = (ln1_gain, ln1_bias, ln2_gain, ln2_bias, qkv_bias, out_bias, up_bias, down_bias)
    core_scalar = core[None].astype(jnp.int32)

    def packed():
        if ring is not None:
            shapes = [(r + 8, LANES)] * 2 + [(r, LANES)] * 2 + [(u, LANES)]
            return pl.pallas_call(
                pack_kernel,
                in_specs=[smem()] + [vmem()] * (4 + len(vectors)),
                out_specs=[vmem()] * 5,
                out_shape=[jax.ShapeDtypeStruct(shape, BF16) for shape in shapes],
                scratch_shapes=[pltpu.VMEM((8, LANES), F32)],
                compiler_params=kernel_params(),
            )(core_scalar, qkv_weight, out_weight, up_weight, down_weight, *vectors)
        rows = jnp.concatenate([jnp.pad(v, ((0, 0), (0, LANES - v.shape[1]))) for v in vectors])
        attn, hidden = [], []
        for t in (0, 1):
            columns = [
                qkv_weight[0, :, D * i + HALF * t + PAIR * p : D * i + HALF * t + PAIR * (p + 1)]
                for p in range(PAIRS)
                for i in range(3)
            ] + [out_weight[0, :, HALF * t : HALF * (t + 1)]]
            attn.append(jnp.concatenate([jnp.concatenate(columns, axis=1), rows]))
            hidden.append(up_weight[0].reshape(r, chips, 2, f)[:, :, t].reshape(r, FFH))
        halves = [pick(low_core, *x) for x in (attn, attn[::-1], hidden, hidden[::-1])]
        down = down_weight[0]
        return halves + [jnp.concatenate([down[:u], down[u:]], axis=1)]

    def shared(mine, sent):
        theirs = swap_core(sent)
        return pick(low_core, mine, theirs), pick(low_core, theirs, mine)

    attn_keep, attn_send, mlp_keep, mlp_send, folded = packed()
    a, b = shared(attn_keep, attn_send)
    attn_block = jnp.concatenate([a[:r], b[:r], a[r:], b[r:]])
    other = swap_section(attn_block)
    attn_blocks = (pick(low_section, attn_block, other), pick(low_section, other, attn_block))
    a, b = shared(mlp_keep, mlp_send)
    mlp_block = jnp.concatenate([a, b, folded])
    other = swap_section(mlp_block)
    mlp_blocks = (pick(low_section, mlp_block, other), pick(low_section, other, mlp_block))

    for layer in (0, 1):
        for kind, blocks in (("attn", attn_blocks), ("mlp", mlp_blocks)):
            if ring is not None:
                track.push((kind, layer), ring.gather(blocks[layer]))

    place = None if ring is None else jnp.concatenate([ring.found_at().astype(jnp.int32), core_scalar])

    def gathered(own):
        return lax.all_gather(own, "dp", axis=0, axis_index_groups=same_core(n))

    def attn_weights(layer):
        if ring is None:
            every = gathered(attn_blocks[layer])
            qo = every[:, :u].reshape(D, LANES)
            columns = qo[:, QKVH:]
            halves = (columns[:HALF], columns[HALF:])
            qkv, kept_rows, sent = qo[:, :QKVH], pick(low_core, *halves), pick(low_core, *halves[::-1])
            small = every[:, u:].reshape(n, len(SMALL), LANES).astype(F32)
            found = [small[:, i, : size * r].reshape(size * D) for i, size in enumerate(SMALL)]
            bq, bu = found[4].reshape(3, 2, PAIRS, PAIR), found[6].reshape(chips, 2, f)
            found[4] = pick(low_core, bq[:, 0], bq[:, 1]).transpose(1, 0, 2).reshape(QKVH)
            found[5] = found[5] + found[7]
            found[6] = pick(low_core, bu[:, 0], bu[:, 1]).reshape(FFH)
        else:
            shapes = [((D, QKVH), BF16), ((HALF, HALF), BF16), ((HALF, HALF), BF16), ((8, LANES), F32)]
            qkv, kept_rows, sent, vec = pl.pallas_call(
                assemble_attn_kernel,
                in_specs=[smem()] + [vmem()] * (chips + 1),
                out_specs=[vmem()] * 4,
                out_shape=[jax.ShapeDtypeStruct(*shape) for shape in shapes],
                scratch_shapes=[
                    pltpu.VMEM((D, HALF), BF16),
                    pltpu.VMEM((chips, PAD, 256), F32),
                    pltpu.VMEM((8, D), F32),
                    pltpu.VMEM((1, 3 * D), F32),
                    pltpu.VMEM((2, 1, FFH), F32),
                ],
                compiler_params=kernel_params(),
            )(place, *track.finish(("attn", layer)))
            widths = (D, D, D, D, QKVH, D, FFH)
            found = [vec[i, :w] for i, w in enumerate(widths)]
        got = swap_core(sent)
        out = jnp.concatenate([pick(low_core, kept_rows, got), pick(low_core, got, kept_rows)], axis=1)
        names = ("g1", "b1", "g2", "b2", "bqkv", "bout", "bup")
        return {"qkv": qkv, "out": out, **dict(zip(names, found))}

    def mlp_weights(layer):
        if ring is None:
            every = gathered(mlp_blocks[layer])
            up, folded = every[:, :u].reshape(D, FFH), every[:, u:]
            down = jnp.stack([folded[:, :, :D], folded[:, :, D:]], axis=1).reshape(FFH, D)
        else:
            up, down = pl.pallas_call(
                assemble_mlp_kernel,
                in_specs=[smem()] + [vmem()] * (chips + 1),
                out_specs=[vmem()] * 2,
                out_shape=[jax.ShapeDtypeStruct((D, FFH), BF16), jax.ShapeDtypeStruct((FFH, D), BF16)],
                compiler_params=kernel_params(),
            )(place, *track.finish(("mlp", layer)))
        return {"up": up, "down": down}

    length = tokens.shape[1]

    def paired(own):
        got = swap_core(own)
        return jnp.concatenate([pick(low_core, own, got), pick(low_core, got, own)])

    def own_half(rows):
        return pick(low_core, rows[:length], rows[length:])

    def other_half(rows):
        return pick(low_core, rows[length:], rows[:length])

    def summed(part):
        return own_half(part) + swap_core(other_half(part).astype(BF16)).astype(F32)

    own_tokens = pick(low_section, tokens[0], tokens[1])
    own_seg = pick(low_section, segments[0], segments[1])
    own_cot = pick(low_section, cotangent[0], cotangent[1])
    cot_low = own_cot.astype(BF16)
    (both, own_seg) = track.step((own_tokens, own_seg))
    table, begin = rotary_tables(paired(own_seg[None]))
    both = paired(both)

    weights_0 = attn_weights(0)
    saved_0 = forward_attend(both, weights_0, table, begin, track)
    weights_0.update(mlp_weights(0))
    part, saved_0 = forward_hidden(saved_0, weights_0, track)
    mid = (own_tokens.astype(F32) + summed(part) + weights_0["bout"]).astype(BF16)
    (mid,) = track.step((mid,))
    both = paired(mid)
    weights_1 = attn_weights(1)
    saved_1 = forward_attend(both, weights_1, table, begin, track)
    weights_1.update(mlp_weights(1))
    part, saved_1 = forward_hidden(saved_1, weights_1, track)
    last = (mid.astype(F32) + summed(part) + weights_1["bout"]).astype(BF16)
    kept_rows, got = pick(low_section, mid, last), swap_section(pick(low_section, last, mid))
    outputs = jnp.stack([pick(low_section, kept_rows, got), pick(low_section, got, kept_rows)])

    def reduce_group(name, group):
        if ring is None:
            total = lax.psum_scatter(group, "dp", scatter_dimension=0, axis_index_groups=same_core(n))
            track.done[name] = total.astype(F32)
            return
        block_of = lambda chip: lax.dynamic_index_in_dim(group, chip, 0, keepdims=False)
        track.push(name, ring.scatter(block_of, group.shape[1]))

    def send_mlp(layer, two, d_up, middle, grad):
        if ring is None:
            up_grad, down_rows = dot_tn(two, d_up), dot_tn(middle, grad).reshape(chips, 2, u, D)
            down_rows = jnp.concatenate([down_rows[:, 0], down_rows[:, 1]], axis=2)
            group = jnp.concatenate([up_grad.reshape(chips, u, LANES), down_rows], axis=1).astype(BF16)
        else:
            rows = two.shape[0]
            group = pl.pallas_call(
                grads_mlp_kernel,
                grid=(2,),
                in_specs=[
                    pl.BlockSpec((rows, HALF), lambda g: (0, g)),
                    pl.BlockSpec((rows, FFH), lambda g: (0, 0)),
                    pl.BlockSpec((rows, FFH // 2), lambda g: (0, g)),
                    pl.BlockSpec((rows, D), lambda g: (0, 0)),
                ],
                out_specs=pl.BlockSpec((chips // 2, 2 * u, LANES), lambda g: (g, 0, 0)),
                out_shape=jax.ShapeDtypeStruct((chips, 2 * u, LANES), BF16),
                compiler_params=kernel_params(),
            )(two, d_up, middle, grad)
        reduce_group(("d_mlp", layer), group)

    def send_attn(layer, one, d_fused, out_rows, small, bias):
        bq = small[4].reshape(PAIRS, 3, PAIR).transpose(1, 0, 2)
        bu = small[6].reshape(chips, f)
        none_q, none_u = jnp.zeros_like(bq), jnp.zeros_like(bu)
        bq = jnp.stack([pick(low_core, bq, none_q), pick(low_core, none_q, bq)], axis=1).reshape(1, 3 * D)
        bu = jnp.stack([pick(low_core, bu, none_u), pick(low_core, none_u, bu)], axis=1).reshape(1, FF)
        if ring is None:
            vectors = [v.reshape(n, 1, -1) for v in (*small[:4], bq, bias, bu, bias)]
            rows = [jnp.pad(v, ((0, 0), (0, 0), (0, LANES - v.shape[2]))) for v in vectors]
            flat = jnp.concatenate(rows, axis=1).astype(BF16).reshape(chips, PAD, LANES)
            qo = jnp.concatenate([dot_tn(one, d_fused).astype(BF16), out_rows], axis=1)
            group = jnp.concatenate([qo.reshape(chips, u, LANES), flat], axis=1)
        else:
            unit = jnp.stack([*small[:4], bias, bias, bias, bias])
            rows = one.shape[0]
            group = pl.pallas_call(
                grads_attn_kernel,
                grid=(2,),
                in_specs=[
                    pl.BlockSpec((rows, HALF), lambda g: (0, g)),
                    pl.BlockSpec((rows, QKVH), lambda g: (0, 0)),
                    pl.BlockSpec((HALF, HALF), lambda g: (g, 0)),
                    pl.BlockSpec((8, HALF), lambda g: (0, g)),
                    pl.BlockSpec((1, 3 * HALF), lambda g: (0, g)),
                    pl.BlockSpec((1, FFH), lambda g: (0, g)),
                ],
                out_specs=pl.BlockSpec((chips // 2, u + PAD, LANES), lambda g: (g, 0, 0)),
                out_shape=jax.ShapeDtypeStruct((chips, u + PAD, LANES), BF16),
                scratch_shapes=[pltpu.VMEM((PAD, LANES), F32)],
                compiler_params=kernel_params(),
            )(one, d_fused, out_rows, unit, bq, bu)
        reduce_group(("d_attn", layer), group)

    def out_rows_of(ctx, grad):
        out_grad = dot_tn(ctx, grad).astype(BF16)
        halves = (out_grad[:, :HALF], out_grad[:, HALF:])
        kept_columns = pick(low_core, *halves)
        got = swap_core(pick(low_core, *halves[::-1]))
        return jnp.concatenate([pick(low_core, kept_columns, got), pick(low_core, got, kept_columns)])

    def back(layer, saved, weights, low_grad):
        grad = paired(low_grad)
        part, d_fused, small = backward(
            saved, grad, weights, table, begin, track, lambda *parts: send_mlp(layer, *parts)
        )
        out_rows = out_rows_of(saved[4], grad)
        send_attn(layer, saved[1], d_fused, out_rows, small, jnp.sum(low_grad.astype(F32), axis=0))
        return part

    part = back(1, saved_1, weights_1, cot_low)
    grad_1 = own_cot + summed(part)
    low_1 = grad_1.astype(BF16)
    (low_1, grad_1) = track.step((low_1, grad_1))
    part = back(0, saved_0, weights_0, low_1)
    grad_0 = low_1.astype(F32) + summed(part)
    (grad_0,) = track.step((grad_0,))
    sent = swap_section(pick(low_section, grad_1, grad_0).astype(BF16)).astype(F32)
    kept_rows = pick(low_section, grad_0, grad_1)
    in_grads = jnp.stack([pick(low_section, kept_rows, sent), pick(low_section, sent, kept_rows)])

    def of_section(kind):
        zero, one_ = track.finish((kind, 0)), track.finish((kind, 1))
        got = swap_section(pick(low_section, one_, zero).astype(BF16))
        return pick(low_section, zero, one_) + got.astype(F32)

    def of_core(block, half):
        keep = pick(low_core, block[:half], block[half:])
        got = swap_core(pick(low_core, block[half:], block[:half]).astype(BF16)).astype(F32)
        return pick(low_core, keep, got), pick(low_core, got, keep), keep + got

    mlp = of_section("d_mlp")
    m0, m1, _ = of_core(mlp[:u], r)
    up_out = jnp.stack([m0.reshape(r, chips, f), m1.reshape(r, chips, f)], axis=2).reshape(r, FF)
    down_out = jnp.concatenate([mlp[u:, :D], mlp[u:, D:]])
    attn = of_section("d_attn")
    rows = len(SMALL)
    a0, a1, both_sum = of_core(
        jnp.concatenate([attn[:r], attn[u : u + rows], attn[r:u], attn[u + rows :]]), r + rows
    )
    qkv_out = jnp.concatenate(
        [
            half[:r, (3 * p + i) * PAIR : (3 * p + i + 1) * PAIR]
            for i in range(3)
            for half in (a0, a1)
            for p in range(PAIRS)
        ],
        axis=1,
    )
    out_out = jnp.concatenate([a0[:r, QKVH:], a1[:r, QKVH:]], axis=1)
    g1, b1, g2, b2, bq, bo, bu, bd = [both_sum[r + i : r + i + 1, : size * r] for i, size in enumerate(SMALL)]
    return (
        outputs[None],
        in_grads[None],
        g1,
        b1,
        g2,
        b2,
        qkv_out[None],
        bq,
        out_out[None],
        bo,
        up_out[None],
        bu,
        down_out[None],
        bd,
    )


def solution(mesh):
    row, matrix = P("section", "dp"), P("section", "dp", None)
    params = (row, row, row, row, matrix, row, matrix, row, matrix, row, matrix, row)
    return jax.shard_map(
        body,
        mesh=mesh,
        in_specs=(P(None, "dp", None), P(None, "dp"), P(None, "dp", None)) + params,
        out_specs=(P("section", None, "dp", None), P("section", None, "dp", None)) + params,
        check_vma=False,
    )
```

```python
import jax
import jax.numpy as jnp
import numpy as np
from jax import lax
from jax.experimental import pallas as pl
from jax.experimental.pallas import tpu as pltpu
from jax.sharding import PartitionSpec as P

D = 768
HEADS = 12
HEAD_DIM = 64
FF = 3072
ROT = 16
HALF = D // 2
PAIR = 2 * HEAD_DIM
PAIRS = HALF // PAIR
FFH = FF // 2
LANES = 2 * D
QKVH = 3 * HALF
PAD = 16
SCALE = HEAD_DIM**-0.5
F32 = jnp.float32
BF16 = jnp.bfloat16

SMALL = (1, 1, 1, 1, 3, 1, 4, 1)


def pick(is_zero, first, second):
    return jnp.where(is_zero, first, second)


def swap_core(block):
    n = lax.axis_size("dp")
    return lax.ppermute(block, "dp", [(i, i ^ 1) for i in range(n)])


def swap_section(block):
    return lax.ppermute(block, "section", [(0, 1), (1, 0)])


def ring_order(chips):
    rows = chips // 2
    return [2 * z for z in range(rows)] + [2 * z + 1 for z in reversed(range(rows))]


class Ring:
    def __init__(self, n):
        self.chips = n // 2
        self.order = ring_order(self.chips)
        chip = lax.axis_index("dp") // 2
        row = chip // 2
        self.position = jnp.where(chip % 2 == 0, row, self.chips - 1 - row)
        self.right = self.route(1)
        self.left = self.route(-1)

    def route(self, step):
        k = len(self.order)
        pairs = []
        for i in range(k):
            source, target = self.order[i], self.order[(i + step) % k]
            pairs += [(2 * source, 2 * target), (2 * source + 1, 2 * target + 1)]
        return pairs

    def chip_at(self, offset):
        at = (self.position + offset + self.chips) % self.chips
        turn = at >= self.chips // 2
        return 2 * jnp.where(turn, self.chips - 1 - at, at) + turn.astype(jnp.int32)

    def gather(self, own):
        (own,) = yield [own]
        found = [own]
        reach = self.chips // 2
        ahead = back = own
        for k in range(1, reach):
            ahead = lax.ppermute(ahead, "dp", self.right)
            back = lax.ppermute(back, "dp", self.left)
            ahead, back = yield [ahead, back]
            found += [ahead, back]
        cut = own.shape[0] // 32 * 16
        ahead = lax.ppermute(ahead[:cut], "dp", self.right)
        back = lax.ppermute(back[cut:], "dp", self.left)
        ahead, back = yield [ahead, back]
        return found + [ahead, back]

    def found_at(self):
        reach = self.chips // 2
        offsets = [0] + [o for k in range(1, reach) for o in (-k, k)] + [reach]
        return self.chip_at(jnp.asarray(np.array(offsets, np.int32)))

    def scatter(self, block_of, rows):
        reach = self.chips // 2
        cut = rows // 32 * 16
        far = block_of(self.chip_at(reach))
        ahead, back = yield [far[:cut], far[cut:]]
        ahead = lax.ppermute(ahead, "dp", self.right)
        back = lax.ppermute(back, "dp", self.left)
        ahead, back = yield [ahead, back]
        own = block_of(self.chip_at(reach - 1))
        ahead = jnp.concatenate([add_low(ahead, own[:cut]), own[cut:]])
        own = block_of(self.chip_at(1 - reach))
        back = jnp.concatenate([own[:cut], add_low(back, own[cut:])])
        for k in range(reach - 2, -1, -1):
            ahead = lax.ppermute(ahead, "dp", self.right)
            back = lax.ppermute(back, "dp", self.left)
            ahead, back = yield [ahead, back]
            if k:
                ahead = add_low(ahead, block_of(self.chip_at(k)))
                back = add_low(back, block_of(self.chip_at(-k)))
        own = block_of(self.chip_at(0))
        return own.astype(F32) + ahead.astype(F32) + back.astype(F32)


class Track:
    def __init__(self):
        self.waiting, self.active, self.held = [], None, []
        self.done = {}

    def push(self, name, steps):
        self.waiting.append((name, steps))

    def step(self, values=()):
        if self.active is None:
            if not self.waiting:
                return values
            self.active = self.waiting.pop(0)
            self.held = next(self.active[1])
        self.held, values = lax.optimization_barrier((self.held, values))
        while True:
            try:
                self.held = self.active[1].send(self.held)
                return values
            except StopIteration as end:
                self.done[self.active[0]] = end.value
                last, self.active = self.held, None
                if not self.waiting:
                    return values
                self.active = self.waiting.pop(0)
                self.held, last = lax.optimization_barrier((next(self.active[1]), last))


class Tracks:
    def __init__(self):
        self.rows = (Track(), Track())

    def push(self, row, name, steps):
        self.rows[row].push(name, steps)

    def step(self, values=()):
        for row in self.rows:
            values = row.step(values)
        return values

    def finish(self, name):
        while all(name not in row.done for row in self.rows):
            self.step()
        return {**self.rows[0].done, **self.rows[1].done}[name]


def add_low(one, two):
    return (one.astype(F32) + two.astype(F32)).astype(BF16)


def same_core(n):
    return [[c + 2 * i for i in range(n // 2)] for c in (0, 1)]


def rotary_tables(segs):
    length = segs.shape[1]
    begin = jnp.sum((segs[:, None, :] < segs[:, :, None]).astype(jnp.int32), axis=2)
    place = (jnp.arange(length, dtype=jnp.int32)[None] - begin).reshape(-1).astype(F32)[:, None]
    half = ROT // 2
    freq = 10000.0 ** (-2.0 * jnp.arange(half, dtype=F32) / ROT)
    rest = jnp.zeros(HEAD_DIM - ROT, F32)
    freq = jnp.tile(jnp.concatenate([freq, freq, rest]), 2)[None]
    first = np.tile(np.arange(HEAD_DIM) < half, 2)[None]
    angle = place * freq
    sin = jnp.sin(angle)
    return jnp.concatenate([jnp.cos(angle), jnp.where(first, -sin, sin)], axis=1), begin.reshape(-1)[:, None]


def turned(x, table, sign):
    lane = lax.broadcasted_iota(jnp.int32, x.shape, 1) & (HEAD_DIM - 1)
    partner = jnp.where(lane < ROT // 2, pltpu.roll(x, PAIR - ROT // 2, 1), pltpu.roll(x, ROT // 2, 1))
    moved = partner * table[:, PAIR:]
    return x * table[:, :PAIR] + moved if sign > 0 else x * table[:, :PAIR] - moved


def dot_nt(a, b):
    return lax.dot_general(a, b, (((1,), (1,)), ((), ())), preferred_element_type=F32)


def dot_tn(a, b):
    return lax.dot_general(a, b, (((0,), (0,)), ((), ())), preferred_element_type=F32)


def kept(begin, row0, rows, keys):
    key = lax.broadcasted_iota(jnp.int32, (rows, keys), 1)
    row = lax.broadcasted_iota(jnp.int32, (rows, keys), 0) + row0
    return (key <= row) & (key >= begin)


def attend_kernel(joined_ref, table_ref, begin_ref, qkv_ref, ctx_ref, lse_ref):
    length = joined_ref.shape[0]
    table = table_ref[...]
    query = turned(joined_ref[:, :PAIR], table, 1).astype(BF16)
    key = turned(joined_ref[:, PAIR : 2 * PAIR], table, 1).astype(BF16)
    value = joined_ref[:, 2 * PAIR :].astype(BF16)
    qkv_ref[:, :PAIR] = query
    qkv_ref[:, PAIR : 2 * PAIR] = key
    qkv_ref[:, 2 * PAIR :] = value
    allowed = kept(begin_ref[...], 0, length, length)
    first = lax.broadcasted_iota(jnp.int32, (length, PAIR), 1) < HEAD_DIM
    scaled = query.astype(F32) * SCALE
    heads = [jnp.where(first == (h == 0), scaled, 0.0).astype(BF16) for h in range(2)]
    scores = [jnp.where(allowed, dot_nt(q, key), -1e30) for q in heads]
    peaks = [jnp.max(s, axis=1, keepdims=True) for s in scores]
    exps = [jnp.exp(s - p) for s, p in zip(scores, peaks)]
    totals = [jnp.sum(e, axis=1, keepdims=True) for e in exps]
    ctx = [
        jnp.dot(e.astype(BF16), value, preferred_element_type=F32) * (1.0 / t) for e, t in zip(exps, totals)
    ]
    lses = [p + jnp.log(t) for p, t in zip(peaks, totals)]
    ctx_ref[...] = jnp.where(first, ctx[0], ctx[1]).astype(BF16)
    lse_ref[...] = jnp.where(first, lses[0], lses[1])


def attend_back_kernel(qkv_ref, lse_ref, dctx_ref, table_ref, begin_ref, out_ref):
    length = qkv_ref.shape[0]
    chunk = length // 2
    first = lax.broadcasted_iota(jnp.int32, (chunk, PAIR), 1) < HEAD_DIM
    parts = []
    for i in range(2):
        rows, keys = pl.ds(i * chunk, chunk), (i + 1) * chunk
        allowed = kept(begin_ref[rows, :], i * chunk, chunk, keys)
        key, value = qkv_ref[:keys, PAIR : 2 * PAIR], qkv_ref[:keys, 2 * PAIR :]
        scaled, grad = qkv_ref[rows, :PAIR].astype(F32) * SCALE, dctx_ref[rows, :].astype(F32)
        qs = [jnp.where(first == (h == 0), scaled, 0.0).astype(BF16) for h in range(2)]
        dos = [jnp.where(first == (h == 0), grad, 0.0).astype(BF16) for h in range(2)]
        lses = [lse_ref[rows, h * HEAD_DIM : h * HEAD_DIM + 1] for h in range(2)]
        ps = [jnp.exp(jnp.where(allowed, dot_nt(q, key) - lse, -1e30)) for q, lse in zip(qs, lses)]
        dps = [dot_nt(do, value) for do in dos]
        inner = [jnp.sum(p * dp, axis=1, keepdims=True) for p, dp in zip(ps, dps)]
        dss = [(p * (dp - m)).astype(BF16) for p, dp, m in zip(ps, dps, inner)]
        dqs = [jnp.dot(ds, key, preferred_element_type=F32) for ds in dss]
        dv = dot_tn(ps[0].astype(BF16), dos[0]) + dot_tn(ps[1].astype(BF16), dos[1])
        dk = dot_tn(dss[0], qs[0]) + dot_tn(dss[1], qs[1])
        parts.append((jnp.where(first, dqs[0], dqs[1]) * SCALE, dk, dv))
    (dq0, dk0, dv0), (dq1, dk1, dv1) = parts
    table = table_ref[...]
    out_ref[:, :PAIR] = turned(jnp.concatenate([dq0, dq1]), table, -1).astype(BF16)
    dk = jnp.concatenate([dk0 + dk1[:chunk], dk1[chunk:]])
    out_ref[:, PAIR : 2 * PAIR] = turned(dk, table, -1).astype(BF16)
    out_ref[:, 2 * PAIR :] = jnp.concatenate([dv0 + dv1[:chunk], dv1[chunk:]]).astype(BF16)


def smem():
    return pl.BlockSpec(memory_space=pltpu.SMEM)


def whole(shape):
    return pl.BlockSpec(shape, lambda i: (0,) * len(shape))


def vmem():
    return pl.BlockSpec(memory_space=pltpu.VMEM)


def pack_kernel(core_ref, wq_ref, wo_ref, wu_ref, wd_ref, *refs):
    small_refs, (attn_keep, attn_send, mlp_keep, mlp_send, fold_ref, rows_ref) = refs[:-6], refs[-6:]
    r, chips, f = wq_ref.shape[1], D // wq_ref.shape[1] // 2, wd_ref.shape[1]
    rows_ref[...] = jnp.zeros_like(rows_ref)
    for i, ref in enumerate(small_refs):
        rows_ref[i : i + 1, : ref.shape[1]] = ref[...].astype(F32)
    rows = rows_ref[...].astype(BF16)
    attn_keep[r:, :] = rows
    attn_send[r:, :] = rows
    fold_ref[:, :D] = wd_ref[0, : f // 2]
    fold_ref[:, D:] = wd_ref[0, f // 2 :]
    for core, targets in ((0, (attn_keep, attn_send)), (1, (attn_send, attn_keep))):

        @pl.when(core_ref[0] == core)
        def _(targets=targets):
            for t, ref in enumerate(targets):
                for p in range(PAIRS):
                    for i in range(3):
                        at, to = D * i + HALF * t + PAIR * p, (3 * p + i) * PAIR
                        ref[:r, to : to + PAIR] = wq_ref[0, :, at : at + PAIR]
                ref[:r, QKVH:] = wo_ref[0, :, HALF * t : HALF * (t + 1)]

    for core, targets in ((0, (mlp_keep, mlp_send)), (1, (mlp_send, mlp_keep))):

        @pl.when(core_ref[0] == core)
        def _(targets=targets):
            for t, ref in enumerate(targets):
                for j in range(chips):
                    at = (2 * j + t) * f
                    ref[:, j * f : (j + 1) * f] = wu_ref[0, :, at : at + f]


def assemble_attn_kernel(place_ref, *refs):
    blocks, (qkv_ref, keep_ref, send_ref, vec_ref, col_ref, row_ref, all_ref, bq_ref, bu_ref) = refs[:-9], refs[-9:]
    chips = len(blocks) - 1
    core = place_ref[chips]
    u = blocks[0].shape[0] - PAD
    n = 2 * chips
    r, f = u // 2, 2 * u
    for k in range(chips):
        chip = place_ref[k]
        if k < chips - 1:
            parts = [(0, u, blocks[k], 0)]
            small = blocks[k][u:, :]
        else:
            cut = blocks[k].shape[0]
            parts = [(0, cut, blocks[k], 0), (cut, u - cut, blocks[k + 1], 0)]
            small = blocks[k + 1][u - cut :, :]
        for start, count, ref, at in parts:
            rows = pl.ds(pl.multiple_of(chip * u + start, 16), count)
            qkv_ref[rows, :] = ref[at : at + count, :QKVH]
            col_ref[rows, :] = ref[at : at + count, QKVH:]
        row_ref[chip] = small[:, : row_ref.shape[2]].astype(F32)
    keep_ref[...] = col_ref[pl.ds(pl.multiple_of(core * HALF, HALF), HALF), :]
    send_ref[...] = col_ref[pl.ds(pl.multiple_of((1 - core) * HALF, HALF), HALF), :]
    for i in range(n):
        piece = row_ref[i // 2, 8 * (i % 2) : 8 * (i % 2) + 8, :]
        all_ref[:, r * i : r * (i + 1)] = piece[:, :r]
        bq_ref[:, 3 * r * i : 3 * r * (i + 1)] = piece[4:5, : 3 * r]
        bu_ref[i % 2, :, f * (i // 2) : f * (i // 2 + 1)] = piece[6:7, :f]
    vec_ref[...] = jnp.zeros_like(vec_ref)
    vec_ref[:, :D] = all_ref[...]
    vec_ref[5:6, :D] = all_ref[5:6, :] + all_ref[7:8, :]
    for c in range(2):

        @pl.when(core == c)
        def _(c=c):
            for p in range(PAIRS):
                for i in range(3):
                    at, to = D * i + HALF * c + PAIR * p, (3 * p + i) * PAIR
                    vec_ref[4:5, to : to + PAIR] = bq_ref[:, at : at + PAIR]
            vec_ref[6:7, :] = bu_ref[c]


def assemble_mlp_kernel(place_ref, *refs):
    blocks, (up_ref, down_ref) = refs[:-2], refs[-2:]
    chips = len(blocks) - 1
    u = blocks[0].shape[0] // 2
    for k in range(chips):
        chip = place_ref[k]
        if k < chips - 1:
            up, down = blocks[k].at[:u], blocks[k].at[u:]
        else:
            up, down = blocks[k], blocks[k + 1]
        up_ref[pl.ds(pl.multiple_of(chip * u, 16), u), :] = up[...]
        down_ref[pl.ds(pl.multiple_of(chip * 2 * u, 16), u), :] = down[:, :D]
        down_ref[pl.ds(pl.multiple_of(chip * 2 * u + u, 16), u), :] = down[:, D:]


def assemble_whole_kernel(every_ref, up_ref, down_ref):
    u = every_ref.shape[1] // 2
    for chip in range(every_ref.shape[0]):
        up_ref[u * chip : u * (chip + 1), :] = every_ref[chip, :u, :]
        down_ref[2 * u * chip : 2 * u * chip + u, :] = every_ref[chip, u:, :D]
        down_ref[2 * u * chip + u : 2 * u * (chip + 1), :] = every_ref[chip, u:, D:]


def grads_mlp_kernel(two_ref, d_up_ref, middle_ref, grad_ref, out_ref):
    count, u = out_ref.shape[0], out_ref.shape[1] // 2
    up = dot_tn(two_ref[...], d_up_ref[...]).astype(BF16)
    for i in range(count):
        out_ref[i, :u, :] = up[u * i : u * (i + 1)]
    down = dot_tn(middle_ref[...], grad_ref[...]).astype(BF16)
    for i in range(count):
        out_ref[i, u:, :D] = down[2 * u * i : 2 * u * i + u]
        out_ref[i, u:, D:] = down[2 * u * i + u : 2 * u * (i + 1)]


def grads_attn_kernel(one_ref, fused_ref, out_rows_ref, all_ref, bq_ref, bu_ref, out_ref, row_ref):
    count, u = out_ref.shape[0], out_ref.shape[1] - PAD
    r = u // 2
    qkv = dot_tn(one_ref[...], fused_ref[...]).astype(BF16)
    for i in range(count):
        out_ref[i, :u, :QKVH] = qkv[u * i : u * (i + 1)]
        out_ref[i, :u, QKVH:] = out_rows_ref[u * i : u * (i + 1), :]
        row_ref[...] = jnp.zeros_like(row_ref)
        for c in range(2):
            d = 2 * i + c
            row_ref[8 * c : 8 * c + 8, :r] = all_ref[:, r * d : r * (d + 1)]
            row_ref[8 * c + 4 : 8 * c + 5, : 3 * r] = bq_ref[:, 3 * r * d : 3 * r * (d + 1)]
            row_ref[8 * c + 6 : 8 * c + 7, : 4 * r] = bu_ref[:, 4 * r * d : 4 * r * (d + 1)]
        out_ref[i, u:, :] = row_ref[...].astype(BF16)


def kernel_params():
    return pltpu.CompilerParams(vmem_limit_bytes=40 * 1024 * 1024)


def per_pair(length, width):
    return pl.BlockSpec((length, width), lambda s, p: (s, p))


def per_row(length, width):
    return pl.BlockSpec((length, width), lambda s, p: (s, 0))


def attend(joined, table, begin):
    tokens = joined.shape[0]
    length = tokens // 2
    return pl.pallas_call(
        attend_kernel,
        grid=(2, PAIRS),
        in_specs=[per_pair(length, 3 * PAIR), per_row(length, 2 * PAIR), per_row(length, 1)],
        out_specs=[per_pair(length, 3 * PAIR), per_pair(length, PAIR), per_pair(length, PAIR)],
        out_shape=[
            jax.ShapeDtypeStruct((tokens, QKVH), BF16),
            jax.ShapeDtypeStruct((tokens, HALF), BF16),
            jax.ShapeDtypeStruct((tokens, HALF), F32),
        ],
        compiler_params=kernel_params(),
        cost_estimate=pl.CostEstimate(flops=20_000_000_000, bytes_accessed=12_000_000, transcendentals=3_000_000),
    )(joined, table, begin)


def attend_back(qkv, lse, dctx, table, begin):
    tokens = qkv.shape[0]
    length = tokens // 2
    return pl.pallas_call(
        attend_back_kernel,
        grid=(2, PAIRS),
        in_specs=[
            per_pair(length, 3 * PAIR),
            per_pair(length, PAIR),
            per_pair(length, PAIR),
            per_row(length, 2 * PAIR),
            per_row(length, 1),
        ],
        out_specs=per_pair(length, 3 * PAIR),
        out_shape=jax.ShapeDtypeStruct((tokens, QKVH), BF16),
        compiler_params=kernel_params(),
        cost_estimate=pl.CostEstimate(flops=30_000_000_000, bytes_accessed=12_000_000, transcendentals=3_000_000),
    )(qkv, lse, dctx, table, begin)


def normalized(rows):
    center = rows - jnp.mean(rows, axis=-1, keepdims=True)
    spread = jnp.mean(center * center, axis=-1, keepdims=True)
    scale = lax.rsqrt(spread + 1e-05)
    return center * scale, scale


def matmul(a, b):
    return jnp.dot(a, b, preferred_element_type=F32)


def forward_attend(source, weights, table, begin, track):
    normed, scale = normalized(source.astype(F32))
    one = (normed * weights["g1"] + weights["b1"]).astype(BF16)
    two = (normed * weights["g2"] + weights["b2"]).astype(BF16)
    joined = matmul(one, weights["qkv"]) + weights["bqkv"]
    one, two, joined = track.step((one, two, joined))
    qkv, ctx, lse = track.step(attend(joined, table, begin))
    return source, one, two, qkv, ctx, lse


def forward_hidden(saved, weights, track):
    two, ctx = saved[2], saved[4]
    up = matmul(two, weights["up"]) + weights["bup"]
    phi = 0.5 * (1.0 + lax.erf(up * np.float32(0.5**0.5)))
    middle = (up * phi).astype(BF16)
    slope = (phi + up * jnp.exp(-0.5 * up * up) * np.float32((2 * np.pi) ** -0.5)).astype(BF16)
    middle, slope = track.step((middle, slope))
    part = matmul(ctx, weights["out"]) + matmul(middle, weights["down"])
    (part,) = track.step((part,))
    return part, (*saved, middle, slope)


def backward(saved, grad, weights, table, begin, track, send_hidden):
    source, one, two, qkv, ctx, lse, middle, slope = saved
    d_up = (dot_nt(grad, weights["down"]) * slope.astype(F32)).astype(BF16)
    (d_up,) = track.step((d_up,))
    send_hidden(two, d_up, middle, grad)
    d_ctx = dot_nt(grad, weights["out"]).astype(BF16)
    d_two = dot_nt(d_up, weights["up"])
    (d_ctx, d_two) = track.step((d_ctx, d_two))
    d_fused = attend_back(qkv, lse, d_ctx, table, begin)
    (d_fused,) = track.step((d_fused,))
    d_one = dot_nt(d_fused, weights["qkv"])
    d_one, d_two = track.step((d_one, d_two))
    normed, scale = normalized(source.astype(F32))
    mixed = d_one * weights["g1"] + d_two * weights["g2"]
    part = scale * (
        mixed
        - jnp.mean(mixed, axis=-1, keepdims=True)
        - normed * jnp.mean(mixed * normed, axis=-1, keepdims=True)
    )
    small = (
        jnp.sum(d_one * normed, axis=0),
        jnp.sum(d_one, axis=0),
        jnp.sum(d_two * normed, axis=0),
        jnp.sum(d_two, axis=0),
        jnp.sum(d_fused.astype(F32), axis=0),
        None,
        jnp.sum(d_up.astype(F32), axis=0),
        None,
    )
    return part, d_fused, small


def body(
    tokens,
    segments,
    cotangent,
    ln1_gain,
    ln1_bias,
    ln2_gain,
    ln2_bias,
    qkv_weight,
    qkv_bias,
    out_weight,
    out_bias,
    up_weight,
    up_bias,
    down_weight,
    down_bias,
):
    n = lax.axis_size("dp")
    chips = n // 2
    r = D // n
    u = 2 * r
    f = FF // n
    section = lax.axis_index("section")
    dp = lax.axis_index("dp")
    core = lax.rem(dp, 2)
    low_core, low_section = core == 0, section == 0
    ring = Ring(n) if chips == 8 else None

    track = Tracks()

    vectors = (ln1_gain, ln1_bias, ln2_gain, ln2_bias, qkv_bias, out_bias, up_bias, down_bias)
    core_scalar = core[None].astype(jnp.int32)
    weights_in = (qkv_weight, out_weight, up_weight, down_weight)

    def packed():
        if ring is not None:
            shapes = [(r + 8, LANES)] * 2 + [(r, LANES)] * 2 + [(u, LANES)]
            return pl.pallas_call(
                pack_kernel,
                grid=(1,),
                in_specs=[smem()] + [whole(v.shape) for v in weights_in + vectors],
                out_specs=[vmem()] * 5,
                out_shape=[jax.ShapeDtypeStruct(shape, BF16) for shape in shapes],
                scratch_shapes=[pltpu.VMEM((8, LANES), F32)],
                compiler_params=kernel_params(),
            )(core_scalar, *weights_in, *vectors)
        rows = jnp.concatenate([jnp.pad(v, ((0, 0), (0, LANES - v.shape[1]))) for v in vectors])
        attn, hidden = [], []
        for t in (0, 1):
            columns = [
                qkv_weight[0, :, D * i + HALF * t + PAIR * p : D * i + HALF * t + PAIR * (p + 1)]
                for p in range(PAIRS)
                for i in range(3)
            ] + [out_weight[0, :, HALF * t : HALF * (t + 1)]]
            attn.append(jnp.concatenate([jnp.concatenate(columns, axis=1), rows]))
            hidden.append(up_weight[0].reshape(r, chips, 2, f)[:, :, t].reshape(r, FFH))
        halves = [pick(low_core, *x) for x in (attn, attn[::-1], hidden, hidden[::-1])]
        down = down_weight[0]
        return halves + [jnp.concatenate([down[:u], down[u:]], axis=1)]

    def shared(mine, sent):
        theirs = swap_core(sent)
        return pick(low_core, mine, theirs), pick(low_core, theirs, mine)

    attn_keep, attn_send, mlp_keep, mlp_send, folded = packed()
    a, b = shared(attn_keep, attn_send)
    attn_block = jnp.concatenate([a[:r], b[:r], a[r:], b[r:]])
    other = swap_section(attn_block)
    attn_blocks = (pick(low_section, attn_block, other), pick(low_section, other, attn_block))
    a, b = shared(mlp_keep, mlp_send)
    mlp_block = jnp.concatenate([a, b, folded])
    other = swap_section(mlp_block)
    mlp_blocks = (pick(low_section, mlp_block, other), pick(low_section, other, mlp_block))

    if ring is not None:
        track.push(0, ("attn", 0), ring.gather(attn_blocks[0]))

    place = None if ring is None else jnp.append(ring.found_at(), core)

    def gathered(own):
        return lax.all_gather(own, "dp", axis=0, axis_index_groups=same_core(n))

    def attn_weights(layer):
        if ring is None:
            every = gathered(attn_blocks[layer])
            qo = every[:, :u].reshape(D, LANES)
            columns = qo[:, QKVH:]
            halves = (columns[:HALF], columns[HALF:])
            qkv, kept_rows, sent = qo[:, :QKVH], pick(low_core, *halves), pick(low_core, *halves[::-1])
            small = every[:, u:].reshape(n, len(SMALL), LANES).astype(F32)
            found = [small[:, i, : size * r].reshape(size * D) for i, size in enumerate(SMALL)]
            bq, bu = found[4].reshape(3, 2, PAIRS, PAIR), found[6].reshape(chips, 2, f)
            found[4] = pick(low_core, bq[:, 0], bq[:, 1]).transpose(1, 0, 2).reshape(QKVH)
            found[5] = found[5] + found[7]
            found[6] = pick(low_core, bu[:, 0], bu[:, 1]).reshape(FFH)
        else:
            shapes = [((D, QKVH), BF16), ((HALF, HALF), BF16), ((HALF, HALF), BF16), ((8, LANES), F32)]
            qkv, kept_rows, sent, vec = pl.pallas_call(
                assemble_attn_kernel,
                in_specs=[smem()] + [vmem()] * (chips + 1),
                out_specs=[vmem()] * 4,
                out_shape=[jax.ShapeDtypeStruct(*shape) for shape in shapes],
                scratch_shapes=[
                    pltpu.VMEM((D, HALF), BF16),
                    pltpu.VMEM((chips, PAD, 256), F32),
                    pltpu.VMEM((8, D), F32),
                    pltpu.VMEM((1, 3 * D), F32),
                    pltpu.VMEM((2, 1, FFH), F32),
                ],
                compiler_params=kernel_params(),
            )(place, *track.finish(("attn", layer)))
            widths = (D, D, D, D, QKVH, D, FFH)
            found = [vec[i, :w] for i, w in enumerate(widths)]
        got = swap_core(sent)
        out = jnp.concatenate([pick(low_core, kept_rows, got), pick(low_core, got, kept_rows)], axis=1)
        names = ("g1", "b1", "g2", "b2", "bqkv", "bout", "bup")
        return {"qkv": qkv, "out": out, **dict(zip(names, found))}

    def mlp_weights(layer):
        if layer == 1 and ring is not None:
            up, down = pl.pallas_call(
                assemble_whole_kernel,
                in_specs=[vmem()],
                out_specs=[vmem()] * 2,
                out_shape=[jax.ShapeDtypeStruct((D, FFH), BF16), jax.ShapeDtypeStruct((FFH, D), BF16)],
                compiler_params=kernel_params(),
            )(every_mlp_1)
        elif ring is None:
            every = gathered(mlp_blocks[layer])
            up, folded = every[:, :u].reshape(D, FFH), every[:, u:]
            down = jnp.stack([folded[:, :, :D], folded[:, :, D:]], axis=1).reshape(FFH, D)
        else:
            up, down = pl.pallas_call(
                assemble_mlp_kernel,
                in_specs=[smem()] + [vmem()] * (chips + 1),
                out_specs=[vmem()] * 2,
                out_shape=[jax.ShapeDtypeStruct((D, FFH), BF16), jax.ShapeDtypeStruct((FFH, D), BF16)],
                compiler_params=kernel_params(),
            )(place, *track.finish(("mlp", layer)))
        return {"up": up, "down": down}

    length = tokens.shape[1]

    def paired(own):
        got = swap_core(own)
        return jnp.concatenate([pick(low_core, own, got), pick(low_core, got, own)])

    def own_half(rows):
        return pick(low_core, rows[:length], rows[length:])

    def other_half(rows):
        return pick(low_core, rows[length:], rows[:length])

    def summed(part):
        return own_half(part) + swap_core(other_half(part).astype(BF16)).astype(F32)

    own_tokens = pick(low_section, tokens[0], tokens[1])
    own_seg = pick(low_section, segments[0], segments[1])
    own_cot = pick(low_section, cotangent[0], cotangent[1])
    cot_low = own_cot.astype(BF16)
    (both, own_seg) = track.step((own_tokens, own_seg))
    table, begin = rotary_tables(paired(own_seg[None]))
    both = paired(both)

    every_mlp_1 = None if ring is None else gathered(mlp_blocks[1])
    weights_0 = attn_weights(0)
    if ring is not None:
        track.push(0, ("attn", 1), ring.gather(attn_blocks[1]))
        track.push(1, ("mlp", 0), ring.gather(mlp_blocks[0]))
    saved_0 = forward_attend(both, weights_0, table, begin, track)
    weights_0.update(mlp_weights(0))
    part, saved_0 = forward_hidden(saved_0, weights_0, track)
    mid = (own_tokens.astype(F32) + summed(part) + weights_0["bout"]).astype(BF16)
    (mid,) = track.step((mid,))
    both = paired(mid)
    weights_1 = attn_weights(1)
    saved_1 = forward_attend(both, weights_1, table, begin, track)
    weights_1.update(mlp_weights(1))
    part, saved_1 = forward_hidden(saved_1, weights_1, track)
    last = (mid.astype(F32) + summed(part) + weights_1["bout"]).astype(BF16)
    kept_rows, got = pick(low_section, mid, last), swap_section(pick(low_section, last, mid))
    outputs = jnp.stack([pick(low_section, kept_rows, got), pick(low_section, got, kept_rows)])

    def reduce_group(name, group):
        if ring is None or name == ("d_mlp", 1):
            total = lax.psum_scatter(group, "dp", scatter_dimension=0, axis_index_groups=same_core(n))
            track.rows[0].done[name] = total.astype(F32)
            return
        block_of = lambda chip: lax.dynamic_index_in_dim(group, chip, 0, keepdims=False)
        track.push(int(name[0] == "d_mlp"), name, ring.scatter(block_of, group.shape[1]))

    def send_mlp(layer, two, d_up, middle, grad):
        if ring is None:
            up_grad, down_rows = dot_tn(two, d_up), dot_tn(middle, grad).reshape(chips, 2, u, D)
            down_rows = jnp.concatenate([down_rows[:, 0], down_rows[:, 1]], axis=2)
            group = jnp.concatenate([up_grad.reshape(chips, u, LANES), down_rows], axis=1).astype(BF16)
        else:
            rows = two.shape[0]
            group = pl.pallas_call(
                grads_mlp_kernel,
                grid=(2,),
                in_specs=[
                    pl.BlockSpec((rows, HALF), lambda g: (0, g)),
                    pl.BlockSpec((rows, FFH), lambda g: (0, 0)),
                    pl.BlockSpec((rows, FFH // 2), lambda g: (0, g)),
                    pl.BlockSpec((rows, D), lambda g: (0, 0)),
                ],
                out_specs=pl.BlockSpec((chips // 2, 2 * u, LANES), lambda g: (g, 0, 0)),
                out_shape=jax.ShapeDtypeStruct((chips, 2 * u, LANES), BF16),
                compiler_params=kernel_params(),
            )(two, d_up, middle, grad)
        reduce_group(("d_mlp", layer), group)

    def send_attn(layer, one, d_fused, out_rows, small, bias):
        bq = small[4].reshape(PAIRS, 3, PAIR).transpose(1, 0, 2)
        bu = small[6].reshape(chips, f)
        none_q, none_u = jnp.zeros_like(bq), jnp.zeros_like(bu)
        bq = jnp.stack([pick(low_core, bq, none_q), pick(low_core, none_q, bq)], axis=1).reshape(1, 3 * D)
        bu = jnp.stack([pick(low_core, bu, none_u), pick(low_core, none_u, bu)], axis=1).reshape(1, FF)
        if ring is None:
            vectors = [v.reshape(n, 1, -1) for v in (*small[:4], bq, bias, bu, bias)]
            rows = [jnp.pad(v, ((0, 0), (0, 0), (0, LANES - v.shape[2]))) for v in vectors]
            flat = jnp.concatenate(rows, axis=1).astype(BF16).reshape(chips, PAD, LANES)
            qo = jnp.concatenate([dot_tn(one, d_fused).astype(BF16), out_rows], axis=1)
            group = jnp.concatenate([qo.reshape(chips, u, LANES), flat], axis=1)
        else:
            unit = jnp.stack([*small[:4], bias, bias, bias, bias])
            rows = one.shape[0]
            group = pl.pallas_call(
                grads_attn_kernel,
                grid=(2,),
                in_specs=[
                    pl.BlockSpec((rows, HALF), lambda g: (0, g)),
                    pl.BlockSpec((rows, QKVH), lambda g: (0, 0)),
                    pl.BlockSpec((HALF, HALF), lambda g: (g, 0)),
                    pl.BlockSpec((8, HALF), lambda g: (0, g)),
                    pl.BlockSpec((1, 3 * HALF), lambda g: (0, g)),
                    pl.BlockSpec((1, FFH), lambda g: (0, g)),
                ],
                out_specs=pl.BlockSpec((chips // 2, u + PAD, LANES), lambda g: (g, 0, 0)),
                out_shape=jax.ShapeDtypeStruct((chips, u + PAD, LANES), BF16),
                scratch_shapes=[pltpu.VMEM((PAD, LANES), F32)],
                compiler_params=kernel_params(),
            )(one, d_fused, out_rows, unit, bq, bu)
        reduce_group(("d_attn", layer), group)

    def out_rows_of(ctx, grad):
        out_grad = dot_tn(ctx, grad).astype(BF16)
        halves = (out_grad[:, :HALF], out_grad[:, HALF:])
        kept_columns = pick(low_core, *halves)
        got = swap_core(pick(low_core, *halves[::-1]))
        return jnp.concatenate([pick(low_core, kept_columns, got), pick(low_core, got, kept_columns)])

    def back(layer, saved, weights, low_grad):
        grad = paired(low_grad)
        part, d_fused, small = backward(
            saved, grad, weights, table, begin, track, lambda *parts: send_mlp(layer, *parts)
        )
        out_rows = out_rows_of(saved[4], grad)
        send_attn(layer, saved[1], d_fused, out_rows, small, jnp.sum(low_grad.astype(F32), axis=0))
        return part

    part = back(1, saved_1, weights_1, cot_low)
    grad_1 = own_cot + summed(part)
    low_1 = grad_1.astype(BF16)
    (low_1, grad_1) = track.step((low_1, grad_1))
    part = back(0, saved_0, weights_0, low_1)
    grad_0 = low_1.astype(F32) + summed(part)
    (grad_0,) = track.step((grad_0,))
    sent = swap_section(pick(low_section, grad_1, grad_0).astype(BF16)).astype(F32)
    kept_rows = pick(low_section, grad_0, grad_1)
    in_grads = jnp.stack([pick(low_section, kept_rows, sent), pick(low_section, sent, kept_rows)])

    def of_section(kind):
        zero, one_ = track.finish((kind, 0)), track.finish((kind, 1))
        got = swap_section(pick(low_section, one_, zero).astype(BF16))
        return pick(low_section, zero, one_) + got.astype(F32)

    def of_core(block, half):
        keep = pick(low_core, block[:half], block[half:])
        got = swap_core(pick(low_core, block[half:], block[:half]).astype(BF16)).astype(F32)
        return pick(low_core, keep, got), pick(low_core, got, keep), keep + got

    mlp = of_section("d_mlp")
    m0, m1, _ = of_core(mlp[:u], r)
    up_out = jnp.stack([m0.reshape(r, chips, f), m1.reshape(r, chips, f)], axis=2).reshape(r, FF)
    down_out = jnp.concatenate([mlp[u:, :D], mlp[u:, D:]])
    attn = of_section("d_attn")
    rows = len(SMALL)
    a0, a1, both_sum = of_core(
        jnp.concatenate([attn[:r], attn[u : u + rows], attn[r:u], attn[u + rows :]]), r + rows
    )
    qkv_out = jnp.concatenate(
        [
            half[:r, (3 * p + i) * PAIR : (3 * p + i + 1) * PAIR]
            for i in range(3)
            for half in (a0, a1)
            for p in range(PAIRS)
        ],
        axis=1,
    )
    out_out = jnp.concatenate([a0[:r, QKVH:], a1[:r, QKVH:]], axis=1)
    g1, b1, g2, b2, bq, bo, bu, bd = [both_sum[r + i : r + i + 1, : size * r] for i, size in enumerate(SMALL)]
    return (
        outputs[None],
        in_grads[None],
        g1,
        b1,
        g2,
        b2,
        qkv_out[None],
        bq,
        out_out[None],
        bo,
        up_out[None],
        bu,
        down_out[None],
        bd,
    )


def solution(mesh):
    row, matrix = P("section", "dp"), P("section", "dp", None)
    params = (row, row, row, row, matrix, row, matrix, row, matrix, row, matrix, row)
    return jax.shard_map(
        body,
        mesh=mesh,
        in_specs=(P(None, "dp", None), P(None, "dp"), P(None, "dp", None)) + params,
        out_specs=(P("section", None, "dp", None), P("section", None, "dp", None)) + params,
        check_vma=False,
    )
```

```python
import jax
import jax.numpy as jnp
import numpy as np
from jax import lax
from jax.experimental import pallas as pl
from jax.experimental.pallas import tpu as pltpu
from jax.sharding import PartitionSpec as P

D = 768
HEADS = 12
HEAD_DIM = 64
FF = 3072
ROT = 16
HALF = D // 2
PAIR = 2 * HEAD_DIM
PAIRS = HALF // PAIR
FFH = FF // 2
LANES = 2 * D
QKVH = 3 * HALF
PAD = 16
SCALE = HEAD_DIM**-0.5
F32 = jnp.float32
BF16 = jnp.bfloat16

SMALL = (1, 1, 1, 1, 3, 1, 4, 1)


def pick(is_zero, first, second):
    return jnp.where(is_zero, first, second)


def swap_core(block):
    n = lax.axis_size("dp")
    return lax.ppermute(block, "dp", [(i, i ^ 1) for i in range(n)])


def swap_section(block):
    return lax.ppermute(block, "section", [(0, 1), (1, 0)])


def ring_order(chips):
    rows = chips // 2
    return [2 * z for z in range(rows)] + [2 * z + 1 for z in reversed(range(rows))]


class Ring:
    def __init__(self, n):
        self.chips = n // 2
        self.order = ring_order(self.chips)
        chip = lax.axis_index("dp") // 2
        row = chip // 2
        self.position = jnp.where(chip % 2 == 0, row, self.chips - 1 - row)
        self.right = self.route(1)
        self.left = self.route(-1)

    def route(self, step):
        k = len(self.order)
        pairs = []
        for i in range(k):
            source, target = self.order[i], self.order[(i + step) % k]
            pairs += [(2 * source, 2 * target), (2 * source + 1, 2 * target + 1)]
        return pairs

    def chip_at(self, offset):
        at = (self.position + offset + self.chips) % self.chips
        turn = at >= self.chips // 2
        return 2 * jnp.where(turn, self.chips - 1 - at, at) + turn.astype(jnp.int32)

    def gather(self, own):
        (own,) = yield [own]
        found = [own]
        reach = self.chips // 2
        ahead = back = own
        for k in range(1, reach):
            ahead = lax.ppermute(ahead, "dp", self.right)
            back = lax.ppermute(back, "dp", self.left)
            ahead, back = yield [ahead, back]
            found += [ahead, back]
        cut = own.shape[0] // 32 * 16
        ahead = lax.ppermute(ahead[:cut], "dp", self.right)
        back = lax.ppermute(back[cut:], "dp", self.left)
        ahead, back = yield [ahead, back]
        return found + [ahead, back]

    def found_at(self):
        reach = self.chips // 2
        offsets = [0] + [o for k in range(1, reach) for o in (-k, k)] + [reach]
        return self.chip_at(jnp.asarray(np.array(offsets, np.int32)))

    def scatter(self, block_of, rows):
        reach = self.chips // 2
        cut = rows // 32 * 16
        far = block_of(self.chip_at(reach))
        ahead, back = yield [far[:cut], far[cut:]]
        ahead = lax.ppermute(ahead, "dp", self.right)
        back = lax.ppermute(back, "dp", self.left)
        ahead, back = yield [ahead, back]
        own = block_of(self.chip_at(reach - 1))
        ahead = jnp.concatenate([add_low(ahead, own[:cut]), own[cut:]])
        own = block_of(self.chip_at(1 - reach))
        back = jnp.concatenate([own[:cut], add_low(back, own[cut:])])
        for k in range(reach - 2, -1, -1):
            ahead = lax.ppermute(ahead, "dp", self.right)
            back = lax.ppermute(back, "dp", self.left)
            ahead, back = yield [ahead, back]
            if k:
                ahead = add_low(ahead, block_of(self.chip_at(k)))
                back = add_low(back, block_of(self.chip_at(-k)))
        own = block_of(self.chip_at(0))
        return own.astype(F32) + ahead.astype(F32) + back.astype(F32)


class Tracks:
    def __init__(self):
        self.waiting, self.active, self.done = ([], []), [None, None], {}

    def push(self, row, name, steps):
        self.waiting[row].append((name, steps))

    def step(self, values=()):
        for row in (0, 1):
            if self.active[row] is None and self.waiting[row]:
                name, steps = self.waiting[row].pop(0)
                self.active[row] = (name, steps, next(steps))
        held = [a[2] if a else [] for a in self.active]
        held, values = lax.optimization_barrier((held, values))
        for row in (0, 1):
            if self.active[row]:
                name, steps, _ = self.active[row]
                try:
                    self.active[row] = (name, steps, steps.send(held[row]))
                except StopIteration as end:
                    self.done[name] = end.value
                    self.active[row] = None
                    if self.waiting[row]:
                        name, steps = self.waiting[row].pop(0)
                        first, _ = lax.optimization_barrier((next(steps), held[row]))
                        self.active[row] = (name, steps, steps.send(first))
        return values

    def finish(self, name):
        while name not in self.done:
            self.step()
        return self.done[name]


def add_low(one, two):
    return (one.astype(F32) + two.astype(F32)).astype(BF16)


def same_core(n):
    return [[c + 2 * i for i in range(n // 2)] for c in (0, 1)]


def rotary_tables(segs):
    length = segs.shape[1]
    begin = jnp.sum((segs[:, None, :] < segs[:, :, None]).astype(jnp.int32), axis=2)
    place = (jnp.arange(length, dtype=jnp.int32)[None] - begin).reshape(-1).astype(F32)[:, None]
    half = ROT // 2
    freq = 10000.0 ** (-2.0 * jnp.arange(half, dtype=F32) / ROT)
    rest = jnp.zeros(HEAD_DIM - ROT, F32)
    freq = jnp.tile(jnp.concatenate([freq, freq, rest]), 2)[None]
    first = np.tile(np.arange(HEAD_DIM) < half, 2)[None]
    angle = place * freq
    sin = jnp.sin(angle)
    return jnp.concatenate([jnp.cos(angle), jnp.where(first, -sin, sin)], axis=1), begin.reshape(-1)[:, None]


def turned(x, table, sign):
    lane = lax.broadcasted_iota(jnp.int32, x.shape, 1) & (HEAD_DIM - 1)
    partner = jnp.where(lane < ROT // 2, pltpu.roll(x, PAIR - ROT // 2, 1), pltpu.roll(x, ROT // 2, 1))
    moved = partner * table[:, PAIR:]
    return x * table[:, :PAIR] + moved if sign > 0 else x * table[:, :PAIR] - moved


def dot_nt(a, b):
    return lax.dot_general(a, b, (((1,), (1,)), ((), ())), preferred_element_type=F32)


def dot_tn(a, b):
    return lax.dot_general(a, b, (((0,), (0,)), ((), ())), preferred_element_type=F32)


def kept(begin, row0, rows, keys):
    key = lax.broadcasted_iota(jnp.int32, (rows, keys), 1)
    row = lax.broadcasted_iota(jnp.int32, (rows, keys), 0) + row0
    return (key <= row) & (key >= begin)


def attend_kernel(joined_ref, table_ref, begin_ref, qkv_ref, ctx_ref, lse_ref):
    length = joined_ref.shape[0]
    table = table_ref[...]
    query = turned(joined_ref[:, :PAIR], table, 1).astype(BF16)
    key = turned(joined_ref[:, PAIR : 2 * PAIR], table, 1).astype(BF16)
    value = joined_ref[:, 2 * PAIR :].astype(BF16)
    qkv_ref[:, :PAIR] = query
    qkv_ref[:, PAIR : 2 * PAIR] = key
    qkv_ref[:, 2 * PAIR :] = value
    allowed = kept(begin_ref[...], 0, length, length)
    first = lax.broadcasted_iota(jnp.int32, (length, PAIR), 1) < HEAD_DIM
    scaled = query.astype(F32) * SCALE
    heads = [jnp.where(first == (h == 0), scaled, 0.0).astype(BF16) for h in range(2)]
    scores = [jnp.where(allowed, dot_nt(q, key), -1e30) for q in heads]
    peaks = [jnp.max(s, axis=1, keepdims=True) for s in scores]
    exps = [jnp.exp(s - p) for s, p in zip(scores, peaks)]
    totals = [jnp.sum(e, axis=1, keepdims=True) for e in exps]
    ctx = [
        jnp.dot(e.astype(BF16), value, preferred_element_type=F32) * (1.0 / t) for e, t in zip(exps, totals)
    ]
    lses = [p + jnp.log(t) for p, t in zip(peaks, totals)]
    ctx_ref[...] = jnp.where(first, ctx[0], ctx[1]).astype(BF16)
    lse_ref[...] = jnp.where(first, lses[0], lses[1])


def attend_back_kernel(qkv_ref, lse_ref, dctx_ref, table_ref, begin_ref, out_ref):
    length = qkv_ref.shape[0]
    chunk = length // 2
    first = lax.broadcasted_iota(jnp.int32, (chunk, PAIR), 1) < HEAD_DIM
    parts = []
    for i in range(2):
        rows, keys = pl.ds(i * chunk, chunk), (i + 1) * chunk
        allowed = kept(begin_ref[rows, :], i * chunk, chunk, keys)
        key, value = qkv_ref[:keys, PAIR : 2 * PAIR], qkv_ref[:keys, 2 * PAIR :]
        scaled, grad = qkv_ref[rows, :PAIR].astype(F32) * SCALE, dctx_ref[rows, :].astype(F32)
        qs = [jnp.where(first == (h == 0), scaled, 0.0).astype(BF16) for h in range(2)]
        dos = [jnp.where(first == (h == 0), grad, 0.0).astype(BF16) for h in range(2)]
        lses = [lse_ref[rows, h * HEAD_DIM : h * HEAD_DIM + 1] for h in range(2)]
        ps = [jnp.exp(jnp.where(allowed, dot_nt(q, key) - lse, -1e30)) for q, lse in zip(qs, lses)]
        dps = [dot_nt(do, value) for do in dos]
        inner = [jnp.sum(p * dp, axis=1, keepdims=True) for p, dp in zip(ps, dps)]
        dss = [(p * (dp - m)).astype(BF16) for p, dp, m in zip(ps, dps, inner)]
        dqs = [jnp.dot(ds, key, preferred_element_type=F32) for ds in dss]
        dv = dot_tn(ps[0].astype(BF16), dos[0]) + dot_tn(ps[1].astype(BF16), dos[1])
        dk = dot_tn(dss[0], qs[0]) + dot_tn(dss[1], qs[1])
        parts.append((jnp.where(first, dqs[0], dqs[1]) * SCALE, dk, dv))
    (dq0, dk0, dv0), (dq1, dk1, dv1) = parts
    table = table_ref[...]
    out_ref[:, :PAIR] = turned(jnp.concatenate([dq0, dq1]), table, -1).astype(BF16)
    dk = jnp.concatenate([dk0 + dk1[:chunk], dk1[chunk:]])
    out_ref[:, PAIR : 2 * PAIR] = turned(dk, table, -1).astype(BF16)
    out_ref[:, 2 * PAIR :] = jnp.concatenate([dv0 + dv1[:chunk], dv1[chunk:]]).astype(BF16)


def smem():
    return pl.BlockSpec(memory_space=pltpu.SMEM)


def whole(shape):
    return pl.BlockSpec(shape, lambda i: (0,) * len(shape))


def vmem():
    return pl.BlockSpec(memory_space=pltpu.VMEM)


def pack_kernel(core_ref, wq_ref, wo_ref, wu_ref, wd_ref, *refs):
    small_refs, (attn_keep, attn_send, mlp_keep, mlp_send, fold_ref, rows_ref) = refs[:-6], refs[-6:]
    r, chips, f = wq_ref.shape[1], D // wq_ref.shape[1] // 2, wd_ref.shape[1]
    rows_ref[...] = jnp.zeros_like(rows_ref)
    for i, ref in enumerate(small_refs):
        rows_ref[i : i + 1, : ref.shape[1]] = ref[...].astype(F32)
    rows = rows_ref[...].astype(BF16)
    attn_keep[r:, :] = rows
    attn_send[r:, :] = rows
    fold_ref[:, :D] = wd_ref[0, : f // 2]
    fold_ref[:, D:] = wd_ref[0, f // 2 :]
    for core, targets in ((0, (attn_keep, attn_send)), (1, (attn_send, attn_keep))):

        @pl.when(core_ref[0] == core)
        def _(targets=targets):
            for t, ref in enumerate(targets):
                for p in range(PAIRS):
                    for i in range(3):
                        at, to = D * i + HALF * t + PAIR * p, (3 * p + i) * PAIR
                        ref[:r, to : to + PAIR] = wq_ref[0, :, at : at + PAIR]
                ref[:r, QKVH:] = wo_ref[0, :, HALF * t : HALF * (t + 1)]

    for core, targets in ((0, (mlp_keep, mlp_send)), (1, (mlp_send, mlp_keep))):

        @pl.when(core_ref[0] == core)
        def _(targets=targets):
            for t, ref in enumerate(targets):
                for j in range(chips):
                    at = (2 * j + t) * f
                    ref[:, j * f : (j + 1) * f] = wu_ref[0, :, at : at + f]


def assemble_attn_kernel(place_ref, *refs):
    blocks, (qkv_ref, keep_ref, send_ref, vec_ref, col_ref, row_ref, all_ref, bq_ref, bu_ref) = refs[:-9], refs[-9:]
    chips = len(blocks) - 1
    core = place_ref[chips]
    u = blocks[0].shape[0] - PAD
    n = 2 * chips
    r, f = u // 2, 2 * u
    for k in range(chips):
        chip = place_ref[k]
        if k < chips - 1:
            parts = [(0, u, blocks[k], 0)]
            small = blocks[k][u:, :]
        else:
            cut = blocks[k].shape[0]
            parts = [(0, cut, blocks[k], 0), (cut, u - cut, blocks[k + 1], 0)]
            small = blocks[k + 1][u - cut :, :]
        for start, count, ref, at in parts:
            rows = pl.ds(pl.multiple_of(chip * u + start, 16), count)
            qkv_ref[rows, :] = ref[at : at + count, :QKVH]
            col_ref[rows, :] = ref[at : at + count, QKVH:]
        row_ref[chip] = small[:, : row_ref.shape[2]].astype(F32)
    keep_ref[...] = col_ref[pl.ds(pl.multiple_of(core * HALF, HALF), HALF), :]
    send_ref[...] = col_ref[pl.ds(pl.multiple_of((1 - core) * HALF, HALF), HALF), :]
    for i in range(n):
        piece = row_ref[i // 2, 8 * (i % 2) : 8 * (i % 2) + 8, :]
        all_ref[:, r * i : r * (i + 1)] = piece[:, :r]
        bq_ref[:, 3 * r * i : 3 * r * (i + 1)] = piece[4:5, : 3 * r]
        bu_ref[i % 2, :, f * (i // 2) : f * (i // 2 + 1)] = piece[6:7, :f]
    vec_ref[...] = jnp.zeros_like(vec_ref)
    vec_ref[:, :D] = all_ref[...]
    vec_ref[5:6, :D] = all_ref[5:6, :] + all_ref[7:8, :]
    for c in range(2):

        @pl.when(core == c)
        def _(c=c):
            for p in range(PAIRS):
                for i in range(3):
                    at, to = D * i + HALF * c + PAIR * p, (3 * p + i) * PAIR
                    vec_ref[4:5, to : to + PAIR] = bq_ref[:, at : at + PAIR]
            vec_ref[6:7, :] = bu_ref[c]


def assemble_mlp_kernel(place_ref, *refs):
    blocks, (up_ref, down_ref) = refs[:-2], refs[-2:]
    chips = len(blocks) - 1
    u = blocks[0].shape[0] // 2
    for k in range(chips):
        chip = place_ref[k]
        if k < chips - 1:
            up, down = blocks[k].at[:u], blocks[k].at[u:]
        else:
            up, down = blocks[k], blocks[k + 1]
        up_ref[pl.ds(pl.multiple_of(chip * u, 16), u), :] = up[...]
        down_ref[pl.ds(pl.multiple_of(chip * 2 * u, 16), u), :] = down[:, :D]
        down_ref[pl.ds(pl.multiple_of(chip * 2 * u + u, 16), u), :] = down[:, D:]


def grads_mlp_kernel(two_ref, d_up_ref, middle_ref, grad_ref, out_ref):
    count, u = out_ref.shape[0], out_ref.shape[1] // 2
    up = dot_tn(two_ref[...], d_up_ref[...]).astype(BF16)
    for i in range(count):
        out_ref[i, :u, :] = up[u * i : u * (i + 1)]
    down = dot_tn(middle_ref[...], grad_ref[...]).astype(BF16)
    for i in range(count):
        out_ref[i, u:, :D] = down[2 * u * i : 2 * u * i + u]
        out_ref[i, u:, D:] = down[2 * u * i + u : 2 * u * (i + 1)]


def grads_attn_kernel(one_ref, fused_ref, out_rows_ref, all_ref, bq_ref, bu_ref, out_ref, row_ref):
    count, u = out_ref.shape[0], out_ref.shape[1] - PAD
    r = u // 2
    qkv = dot_tn(one_ref[...], fused_ref[...]).astype(BF16)
    for i in range(count):
        out_ref[i, :u, :QKVH] = qkv[u * i : u * (i + 1)]
        out_ref[i, :u, QKVH:] = out_rows_ref[u * i : u * (i + 1), :]
        row_ref[...] = jnp.zeros_like(row_ref)
        for c in range(2):
            d = 2 * i + c
            row_ref[8 * c : 8 * c + 8, :r] = all_ref[:, r * d : r * (d + 1)]
            row_ref[8 * c + 4 : 8 * c + 5, : 3 * r] = bq_ref[:, 3 * r * d : 3 * r * (d + 1)]
            row_ref[8 * c + 6 : 8 * c + 7, : 4 * r] = bu_ref[:, 4 * r * d : 4 * r * (d + 1)]
        out_ref[i, u:, :] = row_ref[...].astype(BF16)


def kernel_params():
    return pltpu.CompilerParams(vmem_limit_bytes=40 * 1024 * 1024)


def per_pair(length, width):
    return pl.BlockSpec((length, width), lambda s, p: (s, p))


def per_row(length, width):
    return pl.BlockSpec((length, width), lambda s, p: (s, 0))


def attend(joined, table, begin):
    tokens = joined.shape[0]
    length = tokens // 2
    return pl.pallas_call(
        attend_kernel,
        grid=(2, PAIRS),
        in_specs=[per_pair(length, 3 * PAIR), per_row(length, 2 * PAIR), per_row(length, 1)],
        out_specs=[per_pair(length, 3 * PAIR), per_pair(length, PAIR), per_pair(length, PAIR)],
        out_shape=[
            jax.ShapeDtypeStruct((tokens, QKVH), BF16),
            jax.ShapeDtypeStruct((tokens, HALF), BF16),
            jax.ShapeDtypeStruct((tokens, HALF), F32),
        ],
        compiler_params=kernel_params(),
        cost_estimate=pl.CostEstimate(flops=20_000_000_000, bytes_accessed=12_000_000, transcendentals=3_000_000),
    )(joined, table, begin)


def attend_back(qkv, lse, dctx, table, begin):
    tokens = qkv.shape[0]
    length = tokens // 2
    return pl.pallas_call(
        attend_back_kernel,
        grid=(2, PAIRS),
        in_specs=[
            per_pair(length, 3 * PAIR),
            per_pair(length, PAIR),
            per_pair(length, PAIR),
            per_row(length, 2 * PAIR),
            per_row(length, 1),
        ],
        out_specs=per_pair(length, 3 * PAIR),
        out_shape=jax.ShapeDtypeStruct((tokens, QKVH), BF16),
        compiler_params=kernel_params(),
        cost_estimate=pl.CostEstimate(flops=30_000_000_000, bytes_accessed=12_000_000, transcendentals=3_000_000),
    )(qkv, lse, dctx, table, begin)


def normalized(rows):
    center = rows - jnp.mean(rows, axis=-1, keepdims=True)
    spread = jnp.mean(center * center, axis=-1, keepdims=True)
    scale = lax.rsqrt(spread + 1e-05)
    return center * scale, scale


def matmul(a, b):
    return jnp.dot(a, b, preferred_element_type=F32)


def forward_attend(source, weights, table, begin, track):
    normed, scale = normalized(source.astype(F32))
    one = (normed * weights["g1"] + weights["b1"]).astype(BF16)
    two = (normed * weights["g2"] + weights["b2"]).astype(BF16)
    joined = matmul(one, weights["qkv"]) + weights["bqkv"]
    one, two, joined = track.step((one, two, joined))
    qkv, ctx, lse = track.step(attend(joined, table, begin))
    return source, one, two, qkv, ctx, lse


def forward_hidden(saved, weights, track):
    two, ctx = saved[2], saved[4]
    up = matmul(two, weights["up"]) + weights["bup"]
    phi = 0.5 * (1.0 + lax.erf(up * np.float32(0.5**0.5)))
    middle = (up * phi).astype(BF16)
    slope = (phi + up * jnp.exp(-0.5 * up * up) * np.float32((2 * np.pi) ** -0.5)).astype(BF16)
    middle, slope = track.step((middle, slope))
    part = matmul(ctx, weights["out"]) + matmul(middle, weights["down"])
    (part,) = track.step((part,))
    return part, (*saved, middle, slope)


def back_attend(saved, grad, weights, table, begin, track):
    qkv, lse = saved[3], saved[5]
    d_ctx = dot_nt(grad, weights["out"]).astype(BF16)
    d_fused = attend_back(qkv, lse, d_ctx, table, begin)
    (d_fused,) = track.step((d_fused,))
    d_one = dot_nt(d_fused, weights["qkv"])
    return d_fused, d_one


def back_hidden(slope, grad, weights, track):
    d_up = (dot_nt(grad, weights["down"]) * slope.astype(F32)).astype(BF16)
    (d_up,) = track.step((d_up,))
    return d_up, dot_nt(d_up, weights["up"])


def back_norms(source, d_one, d_two, weights):
    normed, scale = normalized(source.astype(F32))
    mixed = d_one * weights["g1"] + d_two * weights["g2"]
    part = scale * (
        mixed
        - jnp.mean(mixed, axis=-1, keepdims=True)
        - normed * jnp.mean(mixed * normed, axis=-1, keepdims=True)
    )
    sums = (
        jnp.sum(d_one * normed, axis=0),
        jnp.sum(d_one, axis=0),
        jnp.sum(d_two * normed, axis=0),
        jnp.sum(d_two, axis=0),
    )
    return part, sums


def body(
    tokens,
    segments,
    cotangent,
    ln1_gain,
    ln1_bias,
    ln2_gain,
    ln2_bias,
    qkv_weight,
    qkv_bias,
    out_weight,
    out_bias,
    up_weight,
    up_bias,
    down_weight,
    down_bias,
):
    n = lax.axis_size("dp")
    chips = n // 2
    r = D // n
    u = 2 * r
    f = FF // n
    section = lax.axis_index("section")
    dp = lax.axis_index("dp")
    core = lax.rem(dp, 2)
    low_core, low_section = core == 0, section == 0
    ring = Ring(n) if chips == 8 else None

    track = Tracks()

    vectors = (ln1_gain, ln1_bias, ln2_gain, ln2_bias, qkv_bias, out_bias, up_bias, down_bias)
    core_scalar = core[None].astype(jnp.int32)
    weights_in = (qkv_weight, out_weight, up_weight, down_weight)

    def packed():
        if ring is not None:
            shapes = [(r + 8, LANES)] * 2 + [(r, LANES)] * 2 + [(u, LANES)]
            return pl.pallas_call(
                pack_kernel,
                grid=(1,),
                in_specs=[smem()] + [whole(v.shape) for v in weights_in + vectors],
                out_specs=[vmem()] * 5,
                out_shape=[jax.ShapeDtypeStruct(shape, BF16) for shape in shapes],
                scratch_shapes=[pltpu.VMEM((8, LANES), F32)],
                compiler_params=kernel_params(),
            )(core_scalar, *weights_in, *vectors)
        rows = jnp.concatenate([jnp.pad(v, ((0, 0), (0, LANES - v.shape[1]))) for v in vectors])
        attn, hidden = [], []
        for t in (0, 1):
            columns = [
                qkv_weight[0, :, D * i + HALF * t + PAIR * p : D * i + HALF * t + PAIR * (p + 1)]
                for p in range(PAIRS)
                for i in range(3)
            ] + [out_weight[0, :, HALF * t : HALF * (t + 1)]]
            attn.append(jnp.concatenate([jnp.concatenate(columns, axis=1), rows]))
            hidden.append(up_weight[0].reshape(r, chips, 2, f)[:, :, t].reshape(r, FFH))
        halves = [pick(low_core, *x) for x in (attn, attn[::-1], hidden, hidden[::-1])]
        down = down_weight[0]
        return halves + [jnp.concatenate([down[:u], down[u:]], axis=1)]

    def shared(mine, sent):
        theirs = swap_core(sent)
        return pick(low_core, mine, theirs), pick(low_core, theirs, mine)

    attn_keep, attn_send, mlp_keep, mlp_send, folded = packed()
    a, b = shared(attn_keep, attn_send)
    attn_block = jnp.concatenate([a[:r], b[:r], a[r:], b[r:]])
    other = swap_section(attn_block)
    attn_blocks = (pick(low_section, attn_block, other), pick(low_section, other, attn_block))
    a, b = shared(mlp_keep, mlp_send)
    mlp_block = jnp.concatenate([a, b, folded])
    other = swap_section(mlp_block)
    mlp_blocks = (pick(low_section, mlp_block, other), pick(low_section, other, mlp_block))

    if ring is not None:
        track.push(0, ("attn", 0), ring.gather(attn_blocks[0]))

    place = None if ring is None else jnp.append(ring.found_at(), core)

    def gathered(own):
        return lax.all_gather(own, "dp", axis=0, axis_index_groups=same_core(n))

    def attn_weights(layer):
        if ring is None:
            every = gathered(attn_blocks[layer])
            qo = every[:, :u].reshape(D, LANES)
            columns = qo[:, QKVH:]
            halves = (columns[:HALF], columns[HALF:])
            qkv, kept_rows, sent = qo[:, :QKVH], pick(low_core, *halves), pick(low_core, *halves[::-1])
            small = every[:, u:].reshape(n, len(SMALL), LANES).astype(F32)
            found = [small[:, i, : size * r].reshape(size * D) for i, size in enumerate(SMALL)]
            bq, bu = found[4].reshape(3, 2, PAIRS, PAIR), found[6].reshape(chips, 2, f)
            found[4] = pick(low_core, bq[:, 0], bq[:, 1]).transpose(1, 0, 2).reshape(QKVH)
            found[5] = found[5] + found[7]
            found[6] = pick(low_core, bu[:, 0], bu[:, 1]).reshape(FFH)
        else:
            shapes = [((D, QKVH), BF16), ((HALF, HALF), BF16), ((HALF, HALF), BF16), ((8, LANES), F32)]
            qkv, kept_rows, sent, vec = pl.pallas_call(
                assemble_attn_kernel,
                in_specs=[smem()] + [vmem()] * (chips + 1),
                out_specs=[vmem()] * 4,
                out_shape=[jax.ShapeDtypeStruct(*shape) for shape in shapes],
                scratch_shapes=[
                    pltpu.VMEM((D, HALF), BF16),
                    pltpu.VMEM((chips, PAD, 256), F32),
                    pltpu.VMEM((8, D), F32),
                    pltpu.VMEM((1, 3 * D), F32),
                    pltpu.VMEM((2, 1, FFH), F32),
                ],
                compiler_params=kernel_params(),
            )(place, *track.finish(("attn", layer)))
            widths = (D, D, D, D, QKVH, D, FFH)
            found = [vec[i, :w] for i, w in enumerate(widths)]
        got = swap_core(sent)
        out = jnp.concatenate([pick(low_core, kept_rows, got), pick(low_core, got, kept_rows)], axis=1)
        names = ("g1", "b1", "g2", "b2", "bqkv", "bout", "bup")
        return {"qkv": qkv, "out": out, **dict(zip(names, found))}

    def mlp_weights(layer):
        if ring is None:
            every = gathered(mlp_blocks[layer])
            up, folded = every[:, :u].reshape(D, FFH), every[:, u:]
            down = jnp.stack([folded[:, :, :D], folded[:, :, D:]], axis=1).reshape(FFH, D)
        else:
            up, down = pl.pallas_call(
                assemble_mlp_kernel,
                in_specs=[smem()] + [vmem()] * (chips + 1),
                out_specs=[vmem()] * 2,
                out_shape=[jax.ShapeDtypeStruct((D, FFH), BF16), jax.ShapeDtypeStruct((FFH, D), BF16)],
                compiler_params=kernel_params(),
            )(place, *track.finish(("mlp", layer)))
        return {"up": up, "down": down}

    length = tokens.shape[1]

    def paired(own):
        got = swap_core(own)
        return jnp.concatenate([pick(low_core, own, got), pick(low_core, got, own)])

    def own_half(rows):
        return pick(low_core, rows[:length], rows[length:])

    def other_half(rows):
        return pick(low_core, rows[length:], rows[:length])

    def summed(part):
        return own_half(part) + swap_core(other_half(part).astype(BF16)).astype(F32)

    own_tokens = pick(low_section, tokens[0], tokens[1])
    own_seg = pick(low_section, segments[0], segments[1])
    own_cot = pick(low_section, cotangent[0], cotangent[1])
    cot_low = own_cot.astype(BF16)
    (both, own_seg) = track.step((own_tokens, own_seg))
    table, begin = rotary_tables(paired(own_seg[None]))
    both = paired(both)

    weights_0 = attn_weights(0)
    if ring is not None:
        track.push(0, ("attn", 1), ring.gather(attn_blocks[1]))
        track.push(0, ("mlp", 1), ring.gather(mlp_blocks[1]))
        track.push(1, ("mlp", 0), ring.gather(mlp_blocks[0]))
    saved_0 = forward_attend(both, weights_0, table, begin, track)
    weights_0.update(mlp_weights(0))
    part, saved_0 = forward_hidden(saved_0, weights_0, track)
    mid = (own_tokens.astype(F32) + summed(part) + weights_0["bout"]).astype(BF16)
    (mid,) = track.step((mid,))
    both = paired(mid)
    weights_1 = attn_weights(1)
    def reduce_group(name, group):
        if ring is None:
            total = lax.psum_scatter(group, "dp", scatter_dimension=0, axis_index_groups=same_core(n))
            track.done[name] = total.astype(F32)
            return
        block_of = lambda chip: lax.dynamic_index_in_dim(group, chip, 0, keepdims=False)
        track.push(int(name[0] == "d_mlp"), name, ring.scatter(block_of, group.shape[1]))

    def send_mlp(layer, two, d_up, middle, grad):
        if ring is None:
            up_grad, down_rows = dot_tn(two, d_up), dot_tn(middle, grad).reshape(chips, 2, u, D)
            down_rows = jnp.concatenate([down_rows[:, 0], down_rows[:, 1]], axis=2)
            group = jnp.concatenate([up_grad.reshape(chips, u, LANES), down_rows], axis=1).astype(BF16)
        else:
            rows = two.shape[0]
            group = pl.pallas_call(
                grads_mlp_kernel,
                grid=(2,),
                in_specs=[
                    pl.BlockSpec((rows, HALF), lambda g: (0, g)),
                    pl.BlockSpec((rows, FFH), lambda g: (0, 0)),
                    pl.BlockSpec((rows, FFH // 2), lambda g: (0, g)),
                    pl.BlockSpec((rows, D), lambda g: (0, 0)),
                ],
                out_specs=pl.BlockSpec((chips // 2, 2 * u, LANES), lambda g: (g, 0, 0)),
                out_shape=jax.ShapeDtypeStruct((chips, 2 * u, LANES), BF16),
                compiler_params=kernel_params(),
            )(two, d_up, middle, grad)
        reduce_group(("d_mlp", layer), group)

    def send_attn(layer, one, d_fused, out_rows, small, bias):
        bq = small[4].reshape(PAIRS, 3, PAIR).transpose(1, 0, 2)
        bu = small[6].reshape(chips, f)
        none_q, none_u = jnp.zeros_like(bq), jnp.zeros_like(bu)
        bq = jnp.stack([pick(low_core, bq, none_q), pick(low_core, none_q, bq)], axis=1).reshape(1, 3 * D)
        bu = jnp.stack([pick(low_core, bu, none_u), pick(low_core, none_u, bu)], axis=1).reshape(1, FF)
        if ring is None:
            vectors = [v.reshape(n, 1, -1) for v in (*small[:4], bq, bias, bu, bias)]
            rows = [jnp.pad(v, ((0, 0), (0, 0), (0, LANES - v.shape[2]))) for v in vectors]
            flat = jnp.concatenate(rows, axis=1).astype(BF16).reshape(chips, PAD, LANES)
            qo = jnp.concatenate([dot_tn(one, d_fused).astype(BF16), out_rows], axis=1)
            group = jnp.concatenate([qo.reshape(chips, u, LANES), flat], axis=1)
        else:
            unit = jnp.stack([*small[:4], bias, bias, bias, bias])
            rows = one.shape[0]
            group = pl.pallas_call(
                grads_attn_kernel,
                grid=(2,),
                in_specs=[
                    pl.BlockSpec((rows, HALF), lambda g: (0, g)),
                    pl.BlockSpec((rows, QKVH), lambda g: (0, 0)),
                    pl.BlockSpec((HALF, HALF), lambda g: (g, 0)),
                    pl.BlockSpec((8, HALF), lambda g: (0, g)),
                    pl.BlockSpec((1, 3 * HALF), lambda g: (0, g)),
                    pl.BlockSpec((1, FFH), lambda g: (0, g)),
                ],
                out_specs=pl.BlockSpec((chips // 2, u + PAD, LANES), lambda g: (g, 0, 0)),
                out_shape=jax.ShapeDtypeStruct((chips, u + PAD, LANES), BF16),
                scratch_shapes=[pltpu.VMEM((PAD, LANES), F32)],
                compiler_params=kernel_params(),
            )(one, d_fused, out_rows, unit, bq, bu)
        reduce_group(("d_attn", layer), group)

    def out_rows_of(ctx, grad):
        out_grad = dot_tn(ctx, grad).astype(BF16)
        halves = (out_grad[:, :HALF], out_grad[:, HALF:])
        kept_columns = pick(low_core, *halves)
        got = swap_core(pick(low_core, *halves[::-1]))
        return jnp.concatenate([pick(low_core, kept_columns, got), pick(low_core, got, kept_columns)])

    def sums_of(rows):
        return jnp.sum(rows.astype(F32), axis=0)

    grad = paired(cot_low)
    saved_1 = forward_attend(both, weights_1, table, begin, track)
    d_fused, d_one = back_attend(saved_1, grad, weights_1, table, begin, track)
    out_rows = out_rows_of(saved_1[4], grad)
    (d_one, out_rows) = track.step((d_one, out_rows))
    weights_1.update(mlp_weights(1))
    part, (source, one, two, _, _, _, middle, slope) = forward_hidden(saved_1, weights_1, track)
    last = (mid.astype(F32) + summed(part) + weights_1["bout"]).astype(BF16)
    kept_rows, got = pick(low_section, mid, last), swap_section(pick(low_section, last, mid))
    outputs = jnp.stack([pick(low_section, kept_rows, got), pick(low_section, got, kept_rows)])
    d_up, d_two = back_hidden(slope, grad, weights_1, track)
    send_mlp(1, two, d_up, middle, grad)
    (d_two,) = track.step((d_two,))
    part, sums = back_norms(source, d_one, d_two, weights_1)
    small = (*sums, sums_of(d_fused), None, sums_of(d_up))
    (part,) = track.step((part,))
    send_attn(1, one, d_fused, out_rows, small, sums_of(cot_low))
    grad_1 = own_cot + summed(part)
    low_1 = grad_1.astype(BF16)
    (low_1, grad_1) = track.step((low_1, grad_1))

    source, one, two, _, ctx, _, middle, slope = saved_0
    grad = paired(low_1)
    d_up, d_two = back_hidden(slope, grad, weights_0, track)
    send_mlp(0, two, d_up, middle, grad)
    (d_two,) = track.step((d_two,))
    out_rows = out_rows_of(ctx, grad)
    d_fused, d_one = back_attend(saved_0, grad, weights_0, table, begin, track)
    (d_one,) = track.step((d_one,))
    part, sums = back_norms(source, d_one, d_two, weights_0)
    small = (*sums, sums_of(d_fused), None, sums_of(d_up))
    send_attn(0, one, d_fused, out_rows, small, sums_of(low_1))
    grad_0 = low_1.astype(F32) + summed(part)
    (grad_0,) = track.step((grad_0,))
    sent = swap_section(pick(low_section, grad_1, grad_0).astype(BF16)).astype(F32)
    kept_rows = pick(low_section, grad_0, grad_1)
    in_grads = jnp.stack([pick(low_section, kept_rows, sent), pick(low_section, sent, kept_rows)])

    def of_section(kind):
        zero, one_ = track.finish((kind, 0)), track.finish((kind, 1))
        got = swap_section(pick(low_section, one_, zero).astype(BF16))
        return pick(low_section, zero, one_) + got.astype(F32)

    def of_core(block, half):
        keep = pick(low_core, block[:half], block[half:])
        got = swap_core(pick(low_core, block[half:], block[:half]).astype(BF16)).astype(F32)
        return pick(low_core, keep, got), pick(low_core, got, keep), keep + got

    mlp = of_section("d_mlp")
    m0, m1, _ = of_core(mlp[:u], r)
    up_out = jnp.stack([m0.reshape(r, chips, f), m1.reshape(r, chips, f)], axis=2).reshape(r, FF)
    down_out = jnp.concatenate([mlp[u:, :D], mlp[u:, D:]])
    attn = of_section("d_attn")
    rows = len(SMALL)
    a0, a1, both_sum = of_core(
        jnp.concatenate([attn[:r], attn[u : u + rows], attn[r:u], attn[u + rows :]]), r + rows
    )
    qkv_out = jnp.concatenate(
        [
            half[:r, (3 * p + i) * PAIR : (3 * p + i + 1) * PAIR]
            for i in range(3)
            for half in (a0, a1)
            for p in range(PAIRS)
        ],
        axis=1,
    )
    out_out = jnp.concatenate([a0[:r, QKVH:], a1[:r, QKVH:]], axis=1)
    g1, b1, g2, b2, bq, bo, bu, bd = [both_sum[r + i : r + i + 1, : size * r] for i, size in enumerate(SMALL)]
    return (
        outputs[None],
        in_grads[None],
        g1,
        b1,
        g2,
        b2,
        qkv_out[None],
        bq,
        out_out[None],
        bo,
        up_out[None],
        bu,
        down_out[None],
        bd,
    )


def solution(mesh):
    row, matrix = P("section", "dp"), P("section", "dp", None)
    params = (row, row, row, row, matrix, row, matrix, row, matrix, row, matrix, row)
    return jax.shard_map(
        body,
        mesh=mesh,
        in_specs=(P(None, "dp", None), P(None, "dp"), P(None, "dp", None)) + params,
        out_specs=(P("section", None, "dp", None), P("section", None, "dp", None)) + params,
        check_vma=False,
    )
```

```python
import jax
import jax.numpy as jnp
import numpy as np
from jax import lax
from jax.experimental import pallas as pl
from jax.experimental.pallas import tpu as pltpu
from jax.sharding import PartitionSpec as P

D = 768
HEADS = 12
HEAD_DIM = 64
FF = 3072
ROT = 16
HALF = D // 2
PAIR = 2 * HEAD_DIM
PAIRS = HALF // PAIR
FFH = FF // 2
LANES = 2 * D
QKVH = 3 * HALF
PAD = 16
SCALE = HEAD_DIM**-0.5
F32 = jnp.float32
BF16 = jnp.bfloat16

SMALL = (1, 1, 1, 1, 3, 1, 4, 1)


def pick(is_zero, first, second):
    return jnp.where(is_zero, first, second)


def swap_core(block):
    n = lax.axis_size("dp")
    return lax.ppermute(block, "dp", [(i, i ^ 1) for i in range(n)])


def swap_section(block):
    return lax.ppermute(block, "section", [(0, 1), (1, 0)])


def ring_order(chips):
    rows = chips // 2
    return [2 * z for z in range(rows)] + [2 * z + 1 for z in reversed(range(rows))]


class Ring:
    def __init__(self, n):
        self.chips = n // 2
        self.order = ring_order(self.chips)
        chip = lax.axis_index("dp") // 2
        row = chip // 2
        self.position = jnp.where(chip % 2 == 0, row, self.chips - 1 - row)
        self.right = self.route(1)
        self.left = self.route(-1)

    def route(self, step):
        k = len(self.order)
        pairs = []
        for i in range(k):
            source, target = self.order[i], self.order[(i + step) % k]
            pairs += [(2 * source, 2 * target), (2 * source + 1, 2 * target + 1)]
        return pairs

    def chip_at(self, offset):
        at = (self.position + offset + self.chips) % self.chips
        turn = at >= self.chips // 2
        return 2 * jnp.where(turn, self.chips - 1 - at, at) + turn.astype(jnp.int32)

    def gather(self, own):
        (own,) = yield [own]
        found = [own]
        reach = self.chips // 2
        ahead = back = own
        for k in range(1, reach):
            ahead = lax.ppermute(ahead, "dp", self.right)
            back = lax.ppermute(back, "dp", self.left)
            ahead, back = yield [ahead, back]
            found += [ahead, back]
        cut = own.shape[0] // 32 * 16
        ahead = lax.ppermute(ahead[:cut], "dp", self.right)
        back = lax.ppermute(back[cut:], "dp", self.left)
        ahead, back = yield [ahead, back]
        return found + [ahead, back]

    def found_at(self):
        reach = self.chips // 2
        offsets = [0] + [o for k in range(1, reach) for o in (-k, k)] + [reach]
        return self.chip_at(jnp.asarray(np.array(offsets, np.int32)))

    def scatter(self, block_of, rows):
        reach = self.chips // 2
        cut = rows // 32 * 16
        far = block_of(self.chip_at(reach))
        ahead, back = yield [far[:cut], far[cut:]]
        ahead = lax.ppermute(ahead, "dp", self.right)
        back = lax.ppermute(back, "dp", self.left)
        ahead, back = yield [ahead, back]
        own = block_of(self.chip_at(reach - 1))
        ahead = jnp.concatenate([add_low(ahead, own[:cut]), own[cut:]])
        own = block_of(self.chip_at(1 - reach))
        back = jnp.concatenate([own[:cut], add_low(back, own[cut:])])
        for k in range(reach - 2, -1, -1):
            ahead = lax.ppermute(ahead, "dp", self.right)
            back = lax.ppermute(back, "dp", self.left)
            ahead, back = yield [ahead, back]
            if k:
                ahead = add_low(ahead, block_of(self.chip_at(k)))
                back = add_low(back, block_of(self.chip_at(-k)))
        own = block_of(self.chip_at(0))
        return own.astype(F32) + ahead.astype(F32) + back.astype(F32)


class Tracks:
    def __init__(self):
        self.waiting, self.active, self.done = ([], []), [None, None], {}

    def push(self, row, name, steps):
        self.waiting[row].append((name, steps))

    def step(self, values=()):
        for row in (0, 1):
            if self.active[row] is None and self.waiting[row]:
                name, steps = self.waiting[row].pop(0)
                self.active[row] = (name, steps, next(steps))
        held = [a[2] if a else [] for a in self.active]
        held, values = lax.optimization_barrier((held, values))
        for row in (0, 1):
            if self.active[row]:
                name, steps, _ = self.active[row]
                try:
                    self.active[row] = (name, steps, steps.send(held[row]))
                except StopIteration as end:
                    self.done[name] = end.value
                    self.active[row] = None
                    if self.waiting[row]:
                        name, steps = self.waiting[row].pop(0)
                        first, _ = lax.optimization_barrier((next(steps), held[row]))
                        self.active[row] = (name, steps, steps.send(first))
        return values

    def finish(self, name):
        while name not in self.done:
            self.step()
        return self.done[name]


def add_low(one, two):
    return (one.astype(F32) + two.astype(F32)).astype(BF16)


def same_core(n):
    return [[c + 2 * i for i in range(n // 2)] for c in (0, 1)]


def rotary_tables(segs):
    length = segs.shape[1]
    begin = jnp.sum((segs[:, None, :] < segs[:, :, None]).astype(jnp.int32), axis=2)
    place = (jnp.arange(length, dtype=jnp.int32)[None] - begin).reshape(-1).astype(F32)[:, None]
    half = ROT // 2
    freq = 10000.0 ** (-2.0 * jnp.arange(half, dtype=F32) / ROT)
    rest = jnp.zeros(HEAD_DIM - ROT, F32)
    freq = jnp.tile(jnp.concatenate([freq, freq, rest]), 2)[None]
    first = np.tile(np.arange(HEAD_DIM) < half, 2)[None]
    angle = place * freq
    sin = jnp.sin(angle)
    return jnp.concatenate([jnp.cos(angle), jnp.where(first, -sin, sin)], axis=1), begin.reshape(-1)[:, None]


def turned(x, table, sign):
    lane = lax.broadcasted_iota(jnp.int32, x.shape, 1) & (HEAD_DIM - 1)
    partner = jnp.where(lane < ROT // 2, pltpu.roll(x, PAIR - ROT // 2, 1), pltpu.roll(x, ROT // 2, 1))
    moved = partner * table[:, PAIR:]
    return x * table[:, :PAIR] + moved if sign > 0 else x * table[:, :PAIR] - moved


def dot_nt(a, b):
    return lax.dot_general(a, b, (((1,), (1,)), ((), ())), preferred_element_type=F32)


def dot_tn(a, b):
    return lax.dot_general(a, b, (((0,), (0,)), ((), ())), preferred_element_type=F32)


def kept(begin, row0, rows, keys):
    key = lax.broadcasted_iota(jnp.int32, (rows, keys), 1)
    row = lax.broadcasted_iota(jnp.int32, (rows, keys), 0) + row0
    return (key <= row) & (key >= begin)


def attend_kernel(joined_ref, table_ref, begin_ref, qkv_ref, ctx_ref, lse_ref):
    length = joined_ref.shape[0]
    table = table_ref[...]
    query = turned(joined_ref[:, :PAIR], table, 1).astype(BF16)
    key = turned(joined_ref[:, PAIR : 2 * PAIR], table, 1).astype(BF16)
    value = joined_ref[:, 2 * PAIR :].astype(BF16)
    qkv_ref[:, :PAIR] = query
    qkv_ref[:, PAIR : 2 * PAIR] = key
    qkv_ref[:, 2 * PAIR :] = value
    allowed = kept(begin_ref[...], 0, length, length)
    first = lax.broadcasted_iota(jnp.int32, (length, PAIR), 1) < HEAD_DIM
    scaled = query.astype(F32) * SCALE
    heads = [jnp.where(first == (h == 0), scaled, 0.0).astype(BF16) for h in range(2)]
    scores = [jnp.where(allowed, dot_nt(q, key), -1e30) for q in heads]
    peaks = [jnp.max(s, axis=1, keepdims=True) for s in scores]
    exps = [jnp.exp(s - p) for s, p in zip(scores, peaks)]
    totals = [jnp.sum(e, axis=1, keepdims=True) for e in exps]
    ctx = [
        jnp.dot(e.astype(BF16), value, preferred_element_type=F32) * (1.0 / t) for e, t in zip(exps, totals)
    ]
    lses = [p + jnp.log(t) for p, t in zip(peaks, totals)]
    ctx_ref[...] = jnp.where(first, ctx[0], ctx[1]).astype(BF16)
    lse_ref[...] = jnp.where(first, lses[0], lses[1])


def attend_back_kernel(qkv_ref, lse_ref, dctx_ref, table_ref, begin_ref, out_ref):
    length = qkv_ref.shape[0]
    chunk = length // 2
    first = lax.broadcasted_iota(jnp.int32, (chunk, PAIR), 1) < HEAD_DIM
    parts = []
    for i in range(2):
        rows, keys = pl.ds(i * chunk, chunk), (i + 1) * chunk
        allowed = kept(begin_ref[rows, :], i * chunk, chunk, keys)
        key, value = qkv_ref[:keys, PAIR : 2 * PAIR], qkv_ref[:keys, 2 * PAIR :]
        scaled, grad = qkv_ref[rows, :PAIR].astype(F32) * SCALE, dctx_ref[rows, :].astype(F32)
        qs = [jnp.where(first == (h == 0), scaled, 0.0).astype(BF16) for h in range(2)]
        dos = [jnp.where(first == (h == 0), grad, 0.0).astype(BF16) for h in range(2)]
        lses = [lse_ref[rows, h * HEAD_DIM : h * HEAD_DIM + 1] for h in range(2)]
        ps = [jnp.exp(jnp.where(allowed, dot_nt(q, key) - lse, -1e30)) for q, lse in zip(qs, lses)]
        dps = [dot_nt(do, value) for do in dos]
        inner = [jnp.sum(p * dp, axis=1, keepdims=True) for p, dp in zip(ps, dps)]
        dss = [(p * (dp - m)).astype(BF16) for p, dp, m in zip(ps, dps, inner)]
        dqs = [jnp.dot(ds, key, preferred_element_type=F32) for ds in dss]
        dv = dot_tn(ps[0].astype(BF16), dos[0]) + dot_tn(ps[1].astype(BF16), dos[1])
        dk = dot_tn(dss[0], qs[0]) + dot_tn(dss[1], qs[1])
        parts.append((jnp.where(first, dqs[0], dqs[1]) * SCALE, dk, dv))
    (dq0, dk0, dv0), (dq1, dk1, dv1) = parts
    table = table_ref[...]
    out_ref[:, :PAIR] = turned(jnp.concatenate([dq0, dq1]), table, -1).astype(BF16)
    dk = jnp.concatenate([dk0 + dk1[:chunk], dk1[chunk:]])
    out_ref[:, PAIR : 2 * PAIR] = turned(dk, table, -1).astype(BF16)
    out_ref[:, 2 * PAIR :] = jnp.concatenate([dv0 + dv1[:chunk], dv1[chunk:]]).astype(BF16)


def smem():
    return pl.BlockSpec(memory_space=pltpu.SMEM)


def vmem():
    return pl.BlockSpec(memory_space=pltpu.VMEM)


def pack_kernel(core_ref, wq_ref, wo_ref, wu_ref, wd_ref, *refs):
    small = len(SMALL)
    sources = (wq_ref, wo_ref, wu_ref, wd_ref, *refs[:small])
    attn_keep, attn_send, mlp_keep, mlp_send, fold_ref, rows_ref = refs[small : small + 6]
    held, sems = refs[small + 6 : -1], refs[-1]
    copies = [pltpu.make_async_copy(s, h, sems.at[i]) for i, (s, h) in enumerate(zip(sources, held))]
    for copy in copies:
        copy.start()
    for copy in copies:
        copy.wait()
    wq_ref, wo_ref, wu_ref, wd_ref, *small_refs = held
    r, chips, f = wq_ref.shape[1], D // wq_ref.shape[1] // 2, wd_ref.shape[1]
    rows_ref[...] = jnp.zeros_like(rows_ref)
    for i, ref in enumerate(small_refs):
        rows_ref[i : i + 1, : ref.shape[1]] = ref[...].astype(F32)
    rows = rows_ref[...].astype(BF16)
    attn_keep[r:, :] = rows
    attn_send[r:, :] = rows
    fold_ref[:, :D] = wd_ref[0, : f // 2]
    fold_ref[:, D:] = wd_ref[0, f // 2 :]
    for core, targets in ((0, (attn_keep, attn_send)), (1, (attn_send, attn_keep))):

        @pl.when(core_ref[0] == core)
        def _(targets=targets):
            for t, ref in enumerate(targets):
                for p in range(PAIRS):
                    for i in range(3):
                        at, to = D * i + HALF * t + PAIR * p, (3 * p + i) * PAIR
                        ref[:r, to : to + PAIR] = wq_ref[0, :, at : at + PAIR]
                ref[:r, QKVH:] = wo_ref[0, :, HALF * t : HALF * (t + 1)]

    for core, targets in ((0, (mlp_keep, mlp_send)), (1, (mlp_send, mlp_keep))):

        @pl.when(core_ref[0] == core)
        def _(targets=targets):
            for t, ref in enumerate(targets):
                for j in range(chips):
                    at = (2 * j + t) * f
                    ref[:, j * f : (j + 1) * f] = wu_ref[0, :, at : at + f]


def assemble_attn_kernel(place_ref, *refs):
    blocks, (qkv_ref, keep_ref, send_ref, vec_ref, col_ref, row_ref, all_ref, bq_ref, bu_ref) = refs[:-9], refs[-9:]
    chips = len(blocks) - 1
    core = place_ref[chips]
    u = blocks[0].shape[0] - PAD
    n = 2 * chips
    r, f = u // 2, 2 * u
    for k in range(chips):
        chip = place_ref[k]
        if k < chips - 1:
            parts = [(0, u, blocks[k], 0)]
            small = blocks[k][u:, :]
        else:
            cut = blocks[k].shape[0]
            parts = [(0, cut, blocks[k], 0), (cut, u - cut, blocks[k + 1], 0)]
            small = blocks[k + 1][u - cut :, :]
        for start, count, ref, at in parts:
            rows = pl.ds(pl.multiple_of(chip * u + start, 16), count)
            qkv_ref[rows, :] = ref[at : at + count, :QKVH]
            col_ref[rows, :] = ref[at : at + count, QKVH:]
        row_ref[chip] = small[:, : row_ref.shape[2]].astype(F32)
    keep_ref[...] = col_ref[pl.ds(pl.multiple_of(core * HALF, HALF), HALF), :]
    send_ref[...] = col_ref[pl.ds(pl.multiple_of((1 - core) * HALF, HALF), HALF), :]
    for i in range(n):
        piece = row_ref[i // 2, 8 * (i % 2) : 8 * (i % 2) + 8, :]
        all_ref[:, r * i : r * (i + 1)] = piece[:, :r]
        bq_ref[:, 3 * r * i : 3 * r * (i + 1)] = piece[4:5, : 3 * r]
        bu_ref[i % 2, :, f * (i // 2) : f * (i // 2 + 1)] = piece[6:7, :f]
    vec_ref[...] = jnp.zeros_like(vec_ref)
    vec_ref[:, :D] = all_ref[...]
    vec_ref[5:6, :D] = all_ref[5:6, :] + all_ref[7:8, :]
    for c in range(2):

        @pl.when(core == c)
        def _(c=c):
            for p in range(PAIRS):
                for i in range(3):
                    at, to = D * i + HALF * c + PAIR * p, (3 * p + i) * PAIR
                    vec_ref[4:5, to : to + PAIR] = bq_ref[:, at : at + PAIR]
            vec_ref[6:7, :] = bu_ref[c]


def assemble_mlp_kernel(place_ref, *refs):
    blocks, (up_ref, down_ref) = refs[:-2], refs[-2:]
    chips = len(blocks) - 1
    u = blocks[0].shape[0] // 2
    for k in range(chips):
        chip = place_ref[k]
        if k < chips - 1:
            up, down = blocks[k].at[:u], blocks[k].at[u:]
        else:
            up, down = blocks[k], blocks[k + 1]
        up_ref[pl.ds(pl.multiple_of(chip * u, 16), u), :] = up[...]
        down_ref[pl.ds(pl.multiple_of(chip * 2 * u, 16), u), :] = down[:, :D]
        down_ref[pl.ds(pl.multiple_of(chip * 2 * u + u, 16), u), :] = down[:, D:]


def grads_mlp_kernel(two_ref, d_up_ref, middle_ref, grad_ref, out_ref):
    count, u = out_ref.shape[0], out_ref.shape[1] // 2
    up = dot_tn(two_ref[...], d_up_ref[...]).astype(BF16)
    for i in range(count):
        out_ref[i, :u, :] = up[u * i : u * (i + 1)]
    down = dot_tn(middle_ref[...], grad_ref[...]).astype(BF16)
    for i in range(count):
        out_ref[i, u:, :D] = down[2 * u * i : 2 * u * i + u]
        out_ref[i, u:, D:] = down[2 * u * i + u : 2 * u * (i + 1)]


def grads_attn_kernel(one_ref, fused_ref, out_rows_ref, all_ref, bq_ref, bu_ref, out_ref, row_ref):
    count, u = out_ref.shape[0], out_ref.shape[1] - PAD
    r = u // 2
    qkv = dot_tn(one_ref[...], fused_ref[...]).astype(BF16)
    for i in range(count):
        out_ref[i, :u, :QKVH] = qkv[u * i : u * (i + 1)]
        out_ref[i, :u, QKVH:] = out_rows_ref[u * i : u * (i + 1), :]
        row_ref[...] = jnp.zeros_like(row_ref)
        for c in range(2):
            d = 2 * i + c
            row_ref[8 * c : 8 * c + 8, :r] = all_ref[:, r * d : r * (d + 1)]
            row_ref[8 * c + 4 : 8 * c + 5, : 3 * r] = bq_ref[:, 3 * r * d : 3 * r * (d + 1)]
            row_ref[8 * c + 6 : 8 * c + 7, : 4 * r] = bu_ref[:, 4 * r * d : 4 * r * (d + 1)]
        out_ref[i, u:, :] = row_ref[...].astype(BF16)


def kernel_params():
    return pltpu.CompilerParams(vmem_limit_bytes=40 * 1024 * 1024)


def per_pair(length, width):
    return pl.BlockSpec((length, width), lambda s, p: (s, p))


def per_row(length, width):
    return pl.BlockSpec((length, width), lambda s, p: (s, 0))


def attend(joined, table, begin):
    tokens = joined.shape[0]
    length = tokens // 2
    return pl.pallas_call(
        attend_kernel,
        grid=(2, PAIRS),
        in_specs=[per_pair(length, 3 * PAIR), per_row(length, 2 * PAIR), per_row(length, 1)],
        out_specs=[per_pair(length, 3 * PAIR), per_pair(length, PAIR), per_pair(length, PAIR)],
        out_shape=[
            jax.ShapeDtypeStruct((tokens, QKVH), BF16),
            jax.ShapeDtypeStruct((tokens, HALF), BF16),
            jax.ShapeDtypeStruct((tokens, HALF), F32),
        ],
        compiler_params=kernel_params(),
        cost_estimate=pl.CostEstimate(flops=20_000_000_000, bytes_accessed=12_000_000, transcendentals=3_000_000),
    )(joined, table, begin)


def attend_back(qkv, lse, dctx, table, begin):
    tokens = qkv.shape[0]
    length = tokens // 2
    return pl.pallas_call(
        attend_back_kernel,
        grid=(2, PAIRS),
        in_specs=[
            per_pair(length, 3 * PAIR),
            per_pair(length, PAIR),
            per_pair(length, PAIR),
            per_row(length, 2 * PAIR),
            per_row(length, 1),
        ],
        out_specs=per_pair(length, 3 * PAIR),
        out_shape=jax.ShapeDtypeStruct((tokens, QKVH), BF16),
        compiler_params=kernel_params(),
        cost_estimate=pl.CostEstimate(flops=30_000_000_000, bytes_accessed=12_000_000, transcendentals=3_000_000),
    )(qkv, lse, dctx, table, begin)


def normalized(rows):
    center = rows - jnp.mean(rows, axis=-1, keepdims=True)
    spread = jnp.mean(center * center, axis=-1, keepdims=True)
    scale = lax.rsqrt(spread + 1e-05)
    return center * scale, scale


def matmul(a, b):
    return jnp.dot(a, b, preferred_element_type=F32)


def forward_attend(source, weights, table, begin, track):
    normed, scale = normalized(source.astype(F32))
    one = (normed * weights["g1"] + weights["b1"]).astype(BF16)
    two = (normed * weights["g2"] + weights["b2"]).astype(BF16)
    joined = matmul(one, weights["qkv"]) + weights["bqkv"]
    qkv, ctx, lse = track.step(attend(joined, table, begin))
    return source, one, two, qkv, ctx, lse


def forward_hidden(saved, weights):
    two, ctx = saved[2], saved[4]
    up = matmul(two, weights["up"]) + weights["bup"]
    phi = 0.5 * (1.0 + lax.erf(up * np.float32(0.5**0.5)))
    middle = (up * phi).astype(BF16)
    slope = (phi + up * jnp.exp(-0.5 * up * up) * np.float32((2 * np.pi) ** -0.5)).astype(BF16)
    part = matmul(ctx, weights["out"]) + matmul(middle, weights["down"])
    return part, (*saved, middle, slope)


def back_attend(saved, grad, weights, table, begin, track):
    qkv, lse = saved[3], saved[5]
    d_ctx = dot_nt(grad, weights["out"]).astype(BF16)
    d_fused = attend_back(qkv, lse, d_ctx, table, begin)
    (d_fused,) = track.step((d_fused,))
    d_one = dot_nt(d_fused, weights["qkv"])
    return d_fused, d_one


def back_hidden(slope, grad, weights):
    d_up = (dot_nt(grad, weights["down"]) * slope.astype(F32)).astype(BF16)
    return d_up, dot_nt(d_up, weights["up"])


def back_norms(source, d_one, d_two, weights):
    normed, scale = normalized(source.astype(F32))
    mixed = d_one * weights["g1"] + d_two * weights["g2"]
    part = scale * (
        mixed
        - jnp.mean(mixed, axis=-1, keepdims=True)
        - normed * jnp.mean(mixed * normed, axis=-1, keepdims=True)
    )
    sums = (
        jnp.sum(d_one * normed, axis=0),
        jnp.sum(d_one, axis=0),
        jnp.sum(d_two * normed, axis=0),
        jnp.sum(d_two, axis=0),
    )
    return part, sums


def body(
    tokens,
    segments,
    cotangent,
    ln1_gain,
    ln1_bias,
    ln2_gain,
    ln2_bias,
    qkv_weight,
    qkv_bias,
    out_weight,
    out_bias,
    up_weight,
    up_bias,
    down_weight,
    down_bias,
):
    n = lax.axis_size("dp")
    chips = n // 2
    r = D // n
    u = 2 * r
    f = FF // n
    section = lax.axis_index("section")
    dp = lax.axis_index("dp")
    core = lax.rem(dp, 2)
    low_core, low_section = core == 0, section == 0
    ring = Ring(n) if chips == 8 else None

    track = Tracks()

    vectors = (ln1_gain, ln1_bias, ln2_gain, ln2_bias, qkv_bias, out_bias, up_bias, down_bias)
    core_scalar = core[None].astype(jnp.int32)
    weights_in = (qkv_weight, out_weight, up_weight, down_weight)

    def packed():
        if ring is not None:
            shapes = [(r + 8, LANES)] * 2 + [(r, LANES)] * 2 + [(u, LANES)]
            return pl.pallas_call(
                pack_kernel,
                in_specs=[smem()] + [pl.BlockSpec(memory_space=pltpu.HBM)] * len(weights_in + vectors),
                out_specs=[vmem()] * 5,
                out_shape=[jax.ShapeDtypeStruct(shape, BF16) for shape in shapes],
                scratch_shapes=[pltpu.VMEM((8, LANES), F32)]
                + [pltpu.VMEM(v.shape, BF16) for v in weights_in + vectors]
                + [pltpu.SemaphoreType.DMA((len(weights_in + vectors),))],
                compiler_params=kernel_params(),
            )(core_scalar, *weights_in, *vectors)
        rows = jnp.concatenate([jnp.pad(v, ((0, 0), (0, LANES - v.shape[1]))) for v in vectors])
        attn, hidden = [], []
        for t in (0, 1):
            columns = [
                qkv_weight[0, :, D * i + HALF * t + PAIR * p : D * i + HALF * t + PAIR * (p + 1)]
                for p in range(PAIRS)
                for i in range(3)
            ] + [out_weight[0, :, HALF * t : HALF * (t + 1)]]
            attn.append(jnp.concatenate([jnp.concatenate(columns, axis=1), rows]))
            hidden.append(up_weight[0].reshape(r, chips, 2, f)[:, :, t].reshape(r, FFH))
        halves = [pick(low_core, *x) for x in (attn, attn[::-1], hidden, hidden[::-1])]
        down = down_weight[0]
        return halves + [jnp.concatenate([down[:u], down[u:]], axis=1)]

    def shared(mine, sent):
        theirs = swap_core(sent)
        return pick(low_core, mine, theirs), pick(low_core, theirs, mine)

    attn_keep, attn_send, mlp_keep, mlp_send, folded = packed()
    a, b = shared(attn_keep, attn_send)
    attn_block = jnp.concatenate([a[:r], b[:r], a[r:], b[r:]])
    other = swap_section(attn_block)
    attn_blocks = (pick(low_section, attn_block, other), pick(low_section, other, attn_block))
    a, b = shared(mlp_keep, mlp_send)
    mlp_block = jnp.concatenate([a, b, folded])
    other = swap_section(mlp_block)
    mlp_blocks = (pick(low_section, mlp_block, other), pick(low_section, other, mlp_block))

    if ring is not None:
        track.push(0, ("attn", 0), ring.gather(attn_blocks[0]))

    place = None if ring is None else jnp.append(ring.found_at(), core)

    def gathered(own):
        return lax.all_gather(own, "dp", axis=0, axis_index_groups=same_core(n))

    def attn_weights(layer):
        if ring is None:
            every = gathered(attn_blocks[layer])
            qo = every[:, :u].reshape(D, LANES)
            columns = qo[:, QKVH:]
            halves = (columns[:HALF], columns[HALF:])
            qkv, kept_rows, sent = qo[:, :QKVH], pick(low_core, *halves), pick(low_core, *halves[::-1])
            small = every[:, u:].reshape(n, len(SMALL), LANES).astype(F32)
            found = [small[:, i, : size * r].reshape(size * D) for i, size in enumerate(SMALL)]
            bq, bu = found[4].reshape(3, 2, PAIRS, PAIR), found[6].reshape(chips, 2, f)
            found[4] = pick(low_core, bq[:, 0], bq[:, 1]).transpose(1, 0, 2).reshape(QKVH)
            found[5] = found[5] + found[7]
            found[6] = pick(low_core, bu[:, 0], bu[:, 1]).reshape(FFH)
        else:
            shapes = [((D, QKVH), BF16), ((HALF, HALF), BF16), ((HALF, HALF), BF16), ((8, LANES), F32)]
            qkv, kept_rows, sent, vec = pl.pallas_call(
                assemble_attn_kernel,
                in_specs=[smem()] + [vmem()] * (chips + 1),
                out_specs=[vmem()] * 4,
                out_shape=[jax.ShapeDtypeStruct(*shape) for shape in shapes],
                scratch_shapes=[
                    pltpu.VMEM((D, HALF), BF16),
                    pltpu.VMEM((chips, PAD, 256), F32),
                    pltpu.VMEM((8, D), F32),
                    pltpu.VMEM((1, 3 * D), F32),
                    pltpu.VMEM((2, 1, FFH), F32),
                ],
                compiler_params=kernel_params(),
            )(place, *track.finish(("attn", layer)))
            widths = (D, D, D, D, QKVH, D, FFH)
            found = [vec[i, :w] for i, w in enumerate(widths)]
        got = swap_core(sent)
        out = jnp.concatenate([pick(low_core, kept_rows, got), pick(low_core, got, kept_rows)], axis=1)
        names = ("g1", "b1", "g2", "b2", "bqkv", "bout", "bup")
        return {"qkv": qkv, "out": out, **dict(zip(names, found))}

    def mlp_weights(layer):
        if ring is None:
            every = gathered(mlp_blocks[layer])
            up, folded = every[:, :u].reshape(D, FFH), every[:, u:]
            down = jnp.stack([folded[:, :, :D], folded[:, :, D:]], axis=1).reshape(FFH, D)
        else:
            up, down = pl.pallas_call(
                assemble_mlp_kernel,
                in_specs=[smem()] + [vmem()] * (chips + 1),
                out_specs=[vmem()] * 2,
                out_shape=[jax.ShapeDtypeStruct((D, FFH), BF16), jax.ShapeDtypeStruct((FFH, D), BF16)],
                compiler_params=kernel_params(),
            )(place, *track.finish(("mlp", layer)))
        return {"up": up, "down": down}

    length = tokens.shape[1]

    def paired(own):
        got = swap_core(own)
        return jnp.concatenate([pick(low_core, own, got), pick(low_core, got, own)])

    def own_half(rows):
        return pick(low_core, rows[:length], rows[length:])

    def other_half(rows):
        return pick(low_core, rows[length:], rows[:length])

    def summed(part):
        return own_half(part) + swap_core(other_half(part).astype(BF16)).astype(F32)

    own_tokens = pick(low_section, tokens[0], tokens[1])
    own_seg = pick(low_section, segments[0], segments[1])
    own_cot = pick(low_section, cotangent[0], cotangent[1])
    cot_low = own_cot.astype(BF16)
    (both, own_seg) = track.step((own_tokens, own_seg))
    table, begin = rotary_tables(paired(own_seg[None]))
    both = paired(both)

    weights_0 = attn_weights(0)
    if ring is not None:
        track.push(0, ("attn", 1), ring.gather(attn_blocks[1]))
        track.push(0, ("mlp", 1), ring.gather(mlp_blocks[1]))
        track.push(1, ("mlp", 0), ring.gather(mlp_blocks[0]))
        (both,) = track.step((both,))
    saved_0 = forward_attend(both, weights_0, table, begin, track)
    weights_0.update(mlp_weights(0))
    part, saved_0 = forward_hidden(saved_0, weights_0)
    mid = (own_tokens.astype(F32) + summed(part) + weights_0["bout"]).astype(BF16)
    (mid,) = track.step((mid,))
    both = paired(mid)
    weights_1 = attn_weights(1)
    def reduce_group(name, group):
        if ring is None:
            total = lax.psum_scatter(group, "dp", scatter_dimension=0, axis_index_groups=same_core(n))
            track.done[name] = total.astype(F32)
            return
        block_of = lambda chip: lax.dynamic_index_in_dim(group, chip, 0, keepdims=False)
        track.push(int(name[0] == "d_mlp"), name, ring.scatter(block_of, group.shape[1]))

    def send_mlp(layer, two, d_up, middle, grad):
        if ring is None:
            up_grad, down_rows = dot_tn(two, d_up), dot_tn(middle, grad).reshape(chips, 2, u, D)
            down_rows = jnp.concatenate([down_rows[:, 0], down_rows[:, 1]], axis=2)
            group = jnp.concatenate([up_grad.reshape(chips, u, LANES), down_rows], axis=1).astype(BF16)
        else:
            rows = two.shape[0]
            group = pl.pallas_call(
                grads_mlp_kernel,
                grid=(2,),
                in_specs=[
                    pl.BlockSpec((rows, HALF), lambda g: (0, g)),
                    pl.BlockSpec((rows, FFH), lambda g: (0, 0)),
                    pl.BlockSpec((rows, FFH // 2), lambda g: (0, g)),
                    pl.BlockSpec((rows, D), lambda g: (0, 0)),
                ],
                out_specs=pl.BlockSpec((chips // 2, 2 * u, LANES), lambda g: (g, 0, 0)),
                out_shape=jax.ShapeDtypeStruct((chips, 2 * u, LANES), BF16),
                compiler_params=kernel_params(),
            )(two, d_up, middle, grad)
        reduce_group(("d_mlp", layer), group)

    def send_attn(layer, one, d_fused, out_rows, small, bias):
        bq = small[4].reshape(PAIRS, 3, PAIR).transpose(1, 0, 2)
        bu = small[6].reshape(chips, f)
        none_q, none_u = jnp.zeros_like(bq), jnp.zeros_like(bu)
        bq = jnp.stack([pick(low_core, bq, none_q), pick(low_core, none_q, bq)], axis=1).reshape(1, 3 * D)
        bu = jnp.stack([pick(low_core, bu, none_u), pick(low_core, none_u, bu)], axis=1).reshape(1, FF)
        if ring is None:
            vectors = [v.reshape(n, 1, -1) for v in (*small[:4], bq, bias, bu, bias)]
            rows = [jnp.pad(v, ((0, 0), (0, 0), (0, LANES - v.shape[2]))) for v in vectors]
            flat = jnp.concatenate(rows, axis=1).astype(BF16).reshape(chips, PAD, LANES)
            qo = jnp.concatenate([dot_tn(one, d_fused).astype(BF16), out_rows], axis=1)
            group = jnp.concatenate([qo.reshape(chips, u, LANES), flat], axis=1)
        else:
            unit = jnp.stack([*small[:4], bias, bias, bias, bias])
            rows = one.shape[0]
            group = pl.pallas_call(
                grads_attn_kernel,
                grid=(2,),
                in_specs=[
                    pl.BlockSpec((rows, HALF), lambda g: (0, g)),
                    pl.BlockSpec((rows, QKVH), lambda g: (0, 0)),
                    pl.BlockSpec((HALF, HALF), lambda g: (g, 0)),
                    pl.BlockSpec((8, HALF), lambda g: (0, g)),
                    pl.BlockSpec((1, 3 * HALF), lambda g: (0, g)),
                    pl.BlockSpec((1, FFH), lambda g: (0, g)),
                ],
                out_specs=pl.BlockSpec((chips // 2, u + PAD, LANES), lambda g: (g, 0, 0)),
                out_shape=jax.ShapeDtypeStruct((chips, u + PAD, LANES), BF16),
                scratch_shapes=[pltpu.VMEM((PAD, LANES), F32)],
                compiler_params=kernel_params(),
            )(one, d_fused, out_rows, unit, bq, bu)
        reduce_group(("d_attn", layer), group)

    def out_rows_of(ctx, grad):
        out_grad = dot_tn(ctx, grad).astype(BF16)
        halves = (out_grad[:, :HALF], out_grad[:, HALF:])
        kept_columns = pick(low_core, *halves)
        got = swap_core(pick(low_core, *halves[::-1]))
        return jnp.concatenate([pick(low_core, kept_columns, got), pick(low_core, got, kept_columns)])

    def sums_of(rows):
        return jnp.sum(rows.astype(F32), axis=0)

    grad = paired(cot_low)
    saved_1 = forward_attend(both, weights_1, table, begin, track)
    d_fused, d_one = back_attend(saved_1, grad, weights_1, table, begin, track)
    out_rows = out_rows_of(saved_1[4], grad)
    weights_1.update(mlp_weights(1))
    part, (source, one, two, _, _, _, middle, slope) = forward_hidden(saved_1, weights_1)
    last = (mid.astype(F32) + summed(part) + weights_1["bout"]).astype(BF16)
    kept_rows, got = pick(low_section, mid, last), swap_section(pick(low_section, last, mid))
    outputs = jnp.stack([pick(low_section, kept_rows, got), pick(low_section, got, kept_rows)])
    d_up, d_two = back_hidden(slope, grad, weights_1)
    send_mlp(1, two, d_up, middle, grad)
    part, sums = back_norms(source, d_one, d_two, weights_1)
    small = (*sums, sums_of(d_fused), None, sums_of(d_up))
    send_attn(1, one, d_fused, out_rows, small, sums_of(cot_low))
    (part,) = track.step((part,))
    grad_1 = own_cot + summed(part)
    low_1 = grad_1.astype(BF16)

    source, one, two, _, ctx, _, middle, slope = saved_0
    grad = paired(low_1)
    d_up, d_two = back_hidden(slope, grad, weights_0)
    send_mlp(0, two, d_up, middle, grad)
    (d_two,) = track.step((d_two,))
    out_rows = out_rows_of(ctx, grad)
    d_fused, d_one = back_attend(saved_0, grad, weights_0, table, begin, track)
    part, sums = back_norms(source, d_one, d_two, weights_0)
    small = (*sums, sums_of(d_fused), None, sums_of(d_up))
    send_attn(0, one, d_fused, out_rows, small, sums_of(low_1))
    grad_0 = low_1.astype(F32) + summed(part)
    (grad_0,) = track.step((grad_0,))
    sent = swap_section(pick(low_section, grad_1, grad_0).astype(BF16)).astype(F32)
    kept_rows = pick(low_section, grad_0, grad_1)
    in_grads = jnp.stack([pick(low_section, kept_rows, sent), pick(low_section, sent, kept_rows)])

    def of_section(kind):
        zero, one_ = track.finish((kind, 0)), track.finish((kind, 1))
        got = swap_section(pick(low_section, one_, zero).astype(BF16))
        return pick(low_section, zero, one_) + got.astype(F32)

    def of_core(block, half):
        keep = pick(low_core, block[:half], block[half:])
        got = swap_core(pick(low_core, block[half:], block[:half]).astype(BF16)).astype(F32)
        return pick(low_core, keep, got), pick(low_core, got, keep), keep + got

    mlp = of_section("d_mlp")
    m0, m1, _ = of_core(mlp[:u], r)
    up_out = jnp.stack([m0.reshape(r, chips, f), m1.reshape(r, chips, f)], axis=2).reshape(r, FF)
    down_out = jnp.concatenate([mlp[u:, :D], mlp[u:, D:]])
    attn = of_section("d_attn")
    rows = len(SMALL)
    a0, a1, both_sum = of_core(
        jnp.concatenate([attn[:r], attn[u : u + rows], attn[r:u], attn[u + rows :]]), r + rows
    )
    qkv_out = jnp.concatenate(
        [
            half[:r, (3 * p + i) * PAIR : (3 * p + i + 1) * PAIR]
            for i in range(3)
            for half in (a0, a1)
            for p in range(PAIRS)
        ],
        axis=1,
    )
    out_out = jnp.concatenate([a0[:r, QKVH:], a1[:r, QKVH:]], axis=1)
    g1, b1, g2, b2, bq, bo, bu, bd = [both_sum[r + i : r + i + 1, : size * r] for i, size in enumerate(SMALL)]
    return (
        outputs[None],
        in_grads[None],
        g1,
        b1,
        g2,
        b2,
        qkv_out[None],
        bq,
        out_out[None],
        bo,
        up_out[None],
        bu,
        down_out[None],
        bd,
    )


def solution(mesh):
    row, matrix = P("section", "dp"), P("section", "dp", None)
    params = (row, row, row, row, matrix, row, matrix, row, matrix, row, matrix, row)
    return jax.shard_map(
        body,
        mesh=mesh,
        in_specs=(P(None, "dp", None), P(None, "dp"), P(None, "dp", None)) + params,
        out_specs=(P("section", None, "dp", None), P("section", None, "dp", None)) + params,
        check_vma=False,
    )
```

```python
import jax
import jax.numpy as jnp
import numpy as np
from jax import lax
from jax.experimental import pallas as pl
from jax.experimental.pallas import tpu as pltpu
from jax.sharding import PartitionSpec as P

D = 768
HEADS = 12
HEAD_DIM = 64
FF = 3072
ROT = 16
HALF = D // 2
PAIR = 2 * HEAD_DIM
PAIRS = HALF // PAIR
FFH = FF // 2
LANES = 2 * D
QKVH = 3 * HALF
PAD = 16
SCALE = HEAD_DIM**-0.5
F32 = jnp.float32
BF16 = jnp.bfloat16

SMALL = (1, 1, 1, 1, 3, 1, 4, 1)


def pick(is_zero, first, second):
    return jnp.where(is_zero, first, second)


def swap_core(block):
    n = lax.axis_size("dp")
    return lax.ppermute(block, "dp", [(i, i ^ 1) for i in range(n)])


def swap_section(block):
    return lax.ppermute(block, "section", [(0, 1), (1, 0)])


def ring_order(chips):
    rows = chips // 2
    return [2 * z for z in range(rows)] + [2 * z + 1 for z in reversed(range(rows))]


class Ring:
    def __init__(self, n):
        self.chips = n // 2
        self.order = ring_order(self.chips)
        chip = lax.axis_index("dp") // 2
        row = chip // 2
        self.position = jnp.where(chip % 2 == 0, row, self.chips - 1 - row)
        self.right = self.route(1)
        self.left = self.route(-1)

    def route(self, step):
        k = len(self.order)
        pairs = []
        for i in range(k):
            source, target = self.order[i], self.order[(i + step) % k]
            pairs += [(2 * source, 2 * target), (2 * source + 1, 2 * target + 1)]
        return pairs

    def chip_at(self, offset):
        at = (self.position + offset + self.chips) % self.chips
        turn = at >= self.chips // 2
        return 2 * jnp.where(turn, self.chips - 1 - at, at) + turn.astype(jnp.int32)

    def gather(self, own):
        (own,) = yield [own]
        found = [own]
        reach = self.chips // 2
        ahead = back = own
        for k in range(1, reach):
            ahead = lax.ppermute(ahead, "dp", self.right)
            back = lax.ppermute(back, "dp", self.left)
            ahead, back = yield [ahead, back]
            found += [ahead, back]
        cut = own.shape[0] // 32 * 16
        ahead = lax.ppermute(ahead[:cut], "dp", self.right)
        back = lax.ppermute(back[cut:], "dp", self.left)
        ahead, back = yield [ahead, back]
        return found + [ahead, back]

    def found_at(self):
        reach = self.chips // 2
        offsets = [0] + [o for k in range(1, reach) for o in (-k, k)] + [reach]
        return self.chip_at(jnp.asarray(np.array(offsets, np.int32)))

    def scatter(self, block_of, rows):
        reach = self.chips // 2
        cut = rows // 32 * 16
        far = block_of(self.chip_at(reach))
        ahead, back = yield [far[:cut], far[cut:]]
        ahead = lax.ppermute(ahead, "dp", self.right)
        back = lax.ppermute(back, "dp", self.left)
        ahead, back = yield [ahead, back]
        own = block_of(self.chip_at(reach - 1))
        ahead = jnp.concatenate([add_low(ahead, own[:cut]), own[cut:]])
        own = block_of(self.chip_at(1 - reach))
        back = jnp.concatenate([own[:cut], add_low(back, own[cut:])])
        for k in range(reach - 2, -1, -1):
            ahead = lax.ppermute(ahead, "dp", self.right)
            back = lax.ppermute(back, "dp", self.left)
            ahead, back = yield [ahead, back]
            if k:
                ahead = add_low(ahead, block_of(self.chip_at(k)))
                back = add_low(back, block_of(self.chip_at(-k)))
        own = block_of(self.chip_at(0))
        return own.astype(F32) + ahead.astype(F32) + back.astype(F32)


class Tracks:
    def __init__(self):
        self.waiting, self.active, self.done = ([], []), [None, None], {}

    def push(self, row, name, steps):
        self.waiting[row].append((name, steps))

    def step(self, values=()):
        for row in (0, 1):
            if self.active[row] is None and self.waiting[row]:
                name, steps = self.waiting[row].pop(0)
                self.active[row] = (name, steps, next(steps))
        held = [a[2] if a else [] for a in self.active]
        held, values = lax.optimization_barrier((held, values))
        for row in (0, 1):
            if self.active[row]:
                name, steps, _ = self.active[row]
                try:
                    self.active[row] = (name, steps, steps.send(held[row]))
                except StopIteration as end:
                    self.done[name] = end.value
                    self.active[row] = None
                    if self.waiting[row]:
                        name, steps = self.waiting[row].pop(0)
                        first, _ = lax.optimization_barrier((next(steps), held[row]))
                        self.active[row] = (name, steps, steps.send(first))
        return values

    def finish(self, name):
        while name not in self.done:
            self.step()
        return self.done[name]


def add_low(one, two):
    return (one.astype(F32) + two.astype(F32)).astype(BF16)


def same_core(n):
    return [[c + 2 * i for i in range(n // 2)] for c in (0, 1)]


def rotary_tables(segs):
    length = segs.shape[1]
    begin = jnp.sum((segs[:, None, :] < segs[:, :, None]).astype(jnp.int32), axis=2)
    place = (jnp.arange(length, dtype=jnp.int32)[None] - begin).reshape(-1).astype(F32)[:, None]
    half = ROT // 2
    freq = 10000.0 ** (-2.0 * jnp.arange(half, dtype=F32) / ROT)
    rest = jnp.zeros(HEAD_DIM - ROT, F32)
    freq = jnp.tile(jnp.concatenate([freq, freq, rest]), 2)[None]
    first = np.tile(np.arange(HEAD_DIM) < half, 2)[None]
    angle = place * freq
    sin = jnp.sin(angle)
    return jnp.concatenate([jnp.cos(angle), jnp.where(first, -sin, sin)], axis=1), begin.reshape(-1)[:, None]


def turned(x, table, sign):
    lane = lax.broadcasted_iota(jnp.int32, x.shape, 1) & (HEAD_DIM - 1)
    partner = jnp.where(lane < ROT // 2, pltpu.roll(x, PAIR - ROT // 2, 1), pltpu.roll(x, ROT // 2, 1))
    moved = partner * table[:, PAIR:]
    return x * table[:, :PAIR] + moved if sign > 0 else x * table[:, :PAIR] - moved


def dot_nt(a, b):
    return lax.dot_general(a, b, (((1,), (1,)), ((), ())), preferred_element_type=F32)


def dot_tn(a, b):
    return lax.dot_general(a, b, (((0,), (0,)), ((), ())), preferred_element_type=F32)


def kept(begin, row0, rows, keys):
    key = lax.broadcasted_iota(jnp.int32, (rows, keys), 1)
    row = lax.broadcasted_iota(jnp.int32, (rows, keys), 0) + row0
    return (key <= row) & (key >= begin)


def attend_kernel(joined_ref, table_ref, begin_ref, qkv_ref, ctx_ref, lse_ref):
    length = joined_ref.shape[0]
    table = table_ref[...]
    query = turned(joined_ref[:, :PAIR], table, 1).astype(BF16)
    key = turned(joined_ref[:, PAIR : 2 * PAIR], table, 1).astype(BF16)
    value = joined_ref[:, 2 * PAIR :].astype(BF16)
    qkv_ref[:, :PAIR] = query
    qkv_ref[:, PAIR : 2 * PAIR] = key
    qkv_ref[:, 2 * PAIR :] = value
    allowed = kept(begin_ref[...], 0, length, length)
    first = lax.broadcasted_iota(jnp.int32, (length, PAIR), 1) < HEAD_DIM
    scaled = query.astype(F32) * SCALE
    heads = [jnp.where(first == (h == 0), scaled, 0.0).astype(BF16) for h in range(2)]
    scores = [jnp.where(allowed, dot_nt(q, key), -1e30) for q in heads]
    peaks = [jnp.max(s, axis=1, keepdims=True) for s in scores]
    exps = [jnp.exp(s - p) for s, p in zip(scores, peaks)]
    totals = [jnp.sum(e, axis=1, keepdims=True) for e in exps]
    ctx = [
        jnp.dot(e.astype(BF16), value, preferred_element_type=F32) * (1.0 / t) for e, t in zip(exps, totals)
    ]
    lses = [p + jnp.log(t) for p, t in zip(peaks, totals)]
    ctx_ref[...] = jnp.where(first, ctx[0], ctx[1]).astype(BF16)
    lse_ref[...] = jnp.where(first, lses[0], lses[1])


def attend_back_kernel(qkv_ref, lse_ref, dctx_ref, table_ref, begin_ref, out_ref):
    length = qkv_ref.shape[0]
    chunk = length // 2
    first = lax.broadcasted_iota(jnp.int32, (chunk, PAIR), 1) < HEAD_DIM
    parts = []
    for i in range(2):
        rows, keys = pl.ds(i * chunk, chunk), (i + 1) * chunk
        allowed = kept(begin_ref[rows, :], i * chunk, chunk, keys)
        key, value = qkv_ref[:keys, PAIR : 2 * PAIR], qkv_ref[:keys, 2 * PAIR :]
        scaled, grad = qkv_ref[rows, :PAIR].astype(F32) * SCALE, dctx_ref[rows, :].astype(F32)
        qs = [jnp.where(first == (h == 0), scaled, 0.0).astype(BF16) for h in range(2)]
        dos = [jnp.where(first == (h == 0), grad, 0.0).astype(BF16) for h in range(2)]
        lses = [lse_ref[rows, h * HEAD_DIM : h * HEAD_DIM + 1] for h in range(2)]
        ps = [jnp.exp(jnp.where(allowed, dot_nt(q, key) - lse, -1e30)) for q, lse in zip(qs, lses)]
        dps = [dot_nt(do, value) for do in dos]
        inner = [jnp.sum(p * dp, axis=1, keepdims=True) for p, dp in zip(ps, dps)]
        dss = [(p * (dp - m)).astype(BF16) for p, dp, m in zip(ps, dps, inner)]
        dqs = [jnp.dot(ds, key, preferred_element_type=F32) for ds in dss]
        dv = dot_tn(ps[0].astype(BF16), dos[0]) + dot_tn(ps[1].astype(BF16), dos[1])
        dk = dot_tn(dss[0], qs[0]) + dot_tn(dss[1], qs[1])
        parts.append((jnp.where(first, dqs[0], dqs[1]) * SCALE, dk, dv))
    (dq0, dk0, dv0), (dq1, dk1, dv1) = parts
    table = table_ref[...]
    out_ref[:, :PAIR] = turned(jnp.concatenate([dq0, dq1]), table, -1).astype(BF16)
    dk = jnp.concatenate([dk0 + dk1[:chunk], dk1[chunk:]])
    out_ref[:, PAIR : 2 * PAIR] = turned(dk, table, -1).astype(BF16)
    out_ref[:, 2 * PAIR :] = jnp.concatenate([dv0 + dv1[:chunk], dv1[chunk:]]).astype(BF16)


def smem():
    return pl.BlockSpec(memory_space=pltpu.SMEM)


def whole(shape):
    return pl.BlockSpec(shape, lambda i: (0,) * len(shape))


def vmem():
    return pl.BlockSpec(memory_space=pltpu.VMEM)


def pack_kernel(core_ref, wq_ref, wo_ref, wu_ref, wd_ref, *refs):
    small_refs, (attn_keep, attn_send, mlp_keep, mlp_send, fold_ref, rows_ref) = refs[:-6], refs[-6:]
    r, chips, f = wq_ref.shape[1], D // wq_ref.shape[1] // 2, wd_ref.shape[1]
    rows_ref[...] = jnp.zeros_like(rows_ref)
    for i, ref in enumerate(small_refs):
        rows_ref[i : i + 1, : ref.shape[1]] = ref[...].astype(F32)
    rows = rows_ref[...].astype(BF16)
    attn_keep[r:, :] = rows
    attn_send[r:, :] = rows
    fold_ref[:, :D] = wd_ref[0, : f // 2]
    fold_ref[:, D:] = wd_ref[0, f // 2 :]
    for core, targets in ((0, (attn_keep, attn_send)), (1, (attn_send, attn_keep))):

        @pl.when(core_ref[0] == core)
        def _(targets=targets):
            for t, ref in enumerate(targets):
                for p in range(PAIRS):
                    for i in range(3):
                        at, to = D * i + HALF * t + PAIR * p, (3 * p + i) * PAIR
                        ref[:r, to : to + PAIR] = wq_ref[0, :, at : at + PAIR]
                ref[:r, QKVH:] = wo_ref[0, :, HALF * t : HALF * (t + 1)]

    for core, targets in ((0, (mlp_keep, mlp_send)), (1, (mlp_send, mlp_keep))):

        @pl.when(core_ref[0] == core)
        def _(targets=targets):
            for t, ref in enumerate(targets):
                for j in range(chips):
                    at = (2 * j + t) * f
                    ref[:, j * f : (j + 1) * f] = wu_ref[0, :, at : at + f]


def assemble_attn_kernel(place_ref, *refs):
    blocks, (qkv_ref, keep_ref, send_ref, vec_ref, col_ref, row_ref, all_ref, bq_ref, bu_ref) = refs[:-9], refs[-9:]
    chips = len(blocks) - 1
    core = place_ref[chips]
    u = blocks[0].shape[0] - PAD
    n = 2 * chips
    r, f = u // 2, 2 * u
    for k in range(chips):
        chip = place_ref[k]
        if k < chips - 1:
            parts = [(0, u, blocks[k], 0)]
            small = blocks[k][u:, :]
        else:
            cut = blocks[k].shape[0]
            parts = [(0, cut, blocks[k], 0), (cut, u - cut, blocks[k + 1], 0)]
            small = blocks[k + 1][u - cut :, :]
        for start, count, ref, at in parts:
            rows = pl.ds(pl.multiple_of(chip * u + start, 16), count)
            qkv_ref[rows, :] = ref[at : at + count, :QKVH]
            col_ref[rows, :] = ref[at : at + count, QKVH:]
        row_ref[chip] = small[:, : row_ref.shape[2]].astype(F32)
    keep_ref[...] = col_ref[pl.ds(pl.multiple_of(core * HALF, HALF), HALF), :]
    send_ref[...] = col_ref[pl.ds(pl.multiple_of((1 - core) * HALF, HALF), HALF), :]
    for i in range(n):
        piece = row_ref[i // 2, 8 * (i % 2) : 8 * (i % 2) + 8, :]
        all_ref[:, r * i : r * (i + 1)] = piece[:, :r]
        bq_ref[:, 3 * r * i : 3 * r * (i + 1)] = piece[4:5, : 3 * r]
        bu_ref[i % 2, :, f * (i // 2) : f * (i // 2 + 1)] = piece[6:7, :f]
    vec_ref[...] = jnp.zeros_like(vec_ref)
    vec_ref[:, :D] = all_ref[...]
    vec_ref[5:6, :D] = all_ref[5:6, :] + all_ref[7:8, :]
    for c in range(2):

        @pl.when(core == c)
        def _(c=c):
            for p in range(PAIRS):
                for i in range(3):
                    at, to = D * i + HALF * c + PAIR * p, (3 * p + i) * PAIR
                    vec_ref[4:5, to : to + PAIR] = bq_ref[:, at : at + PAIR]
            vec_ref[6:7, :] = bu_ref[c]


def assemble_mlp_kernel(place_ref, *refs):
    blocks, (up_ref, down_ref) = refs[:-2], refs[-2:]
    chips = len(blocks) - 1
    u = blocks[0].shape[0] // 2
    for k in range(chips):
        chip = place_ref[k]
        if k < chips - 1:
            up, down = blocks[k].at[:u], blocks[k].at[u:]
        else:
            up, down = blocks[k], blocks[k + 1]
        up_ref[pl.ds(pl.multiple_of(chip * u, 16), u), :] = up[...]
        down_ref[pl.ds(pl.multiple_of(chip * 2 * u, 16), u), :] = down[:, :D]
        down_ref[pl.ds(pl.multiple_of(chip * 2 * u + u, 16), u), :] = down[:, D:]


def grads_mlp_kernel(two_ref, d_up_ref, middle_ref, grad_ref, out_ref):
    count, u = out_ref.shape[0], out_ref.shape[1] // 2
    up = dot_tn(two_ref[...], d_up_ref[...]).astype(BF16)
    for i in range(count):
        out_ref[i, :u, :] = up[u * i : u * (i + 1)]
    down = dot_tn(middle_ref[...], grad_ref[...]).astype(BF16)
    for i in range(count):
        out_ref[i, u:, :D] = down[2 * u * i : 2 * u * i + u]
        out_ref[i, u:, D:] = down[2 * u * i + u : 2 * u * (i + 1)]


def grads_attn_kernel(one_ref, fused_ref, out_rows_ref, all_ref, bq_ref, bu_ref, out_ref, row_ref):
    count, u = out_ref.shape[0], out_ref.shape[1] - PAD
    r = u // 2
    qkv = dot_tn(one_ref[...], fused_ref[...]).astype(BF16)
    for i in range(count):
        out_ref[i, :u, :QKVH] = qkv[u * i : u * (i + 1)]
        out_ref[i, :u, QKVH:] = out_rows_ref[u * i : u * (i + 1), :]
        row_ref[...] = jnp.zeros_like(row_ref)
        for c in range(2):
            d = 2 * i + c
            row_ref[8 * c : 8 * c + 8, :r] = all_ref[:, r * d : r * (d + 1)]
            row_ref[8 * c + 4 : 8 * c + 5, : 3 * r] = bq_ref[:, 3 * r * d : 3 * r * (d + 1)]
            row_ref[8 * c + 6 : 8 * c + 7, : 4 * r] = bu_ref[:, 4 * r * d : 4 * r * (d + 1)]
        out_ref[i, u:, :] = row_ref[...].astype(BF16)


def kernel_params():
    return pltpu.CompilerParams(vmem_limit_bytes=40 * 1024 * 1024)


def per_pair(length, width):
    return pl.BlockSpec((length, width), lambda s, p: (s, p))


def per_row(length, width):
    return pl.BlockSpec((length, width), lambda s, p: (s, 0))


def attend(joined, table, begin):
    tokens = joined.shape[0]
    length = tokens // 2
    return pl.pallas_call(
        attend_kernel,
        grid=(2, PAIRS),
        in_specs=[per_pair(length, 3 * PAIR), per_row(length, 2 * PAIR), per_row(length, 1)],
        out_specs=[per_pair(length, 3 * PAIR), per_pair(length, PAIR), per_pair(length, PAIR)],
        out_shape=[
            jax.ShapeDtypeStruct((tokens, QKVH), BF16),
            jax.ShapeDtypeStruct((tokens, HALF), BF16),
            jax.ShapeDtypeStruct((tokens, HALF), F32),
        ],
        compiler_params=kernel_params(),
        cost_estimate=pl.CostEstimate(flops=20_000_000_000, bytes_accessed=12_000_000, transcendentals=3_000_000),
    )(joined, table, begin)


def attend_back(qkv, lse, dctx, table, begin):
    tokens = qkv.shape[0]
    length = tokens // 2
    return pl.pallas_call(
        attend_back_kernel,
        grid=(2, PAIRS),
        in_specs=[
            per_pair(length, 3 * PAIR),
            per_pair(length, PAIR),
            per_pair(length, PAIR),
            per_row(length, 2 * PAIR),
            per_row(length, 1),
        ],
        out_specs=per_pair(length, 3 * PAIR),
        out_shape=jax.ShapeDtypeStruct((tokens, QKVH), BF16),
        compiler_params=kernel_params(),
        cost_estimate=pl.CostEstimate(flops=30_000_000_000, bytes_accessed=12_000_000, transcendentals=3_000_000),
    )(qkv, lse, dctx, table, begin)


def normalized(rows):
    center = rows - jnp.mean(rows, axis=-1, keepdims=True)
    spread = jnp.mean(center * center, axis=-1, keepdims=True)
    scale = lax.rsqrt(spread + 1e-05)
    return center * scale, scale


def matmul(a, b):
    return jnp.dot(a, b, preferred_element_type=F32)


def norms(source, weights):
    normed, scale = normalized(source.astype(F32))
    one = (normed * weights["g1"] + weights["b1"]).astype(BF16)
    return one, (normed * weights["g2"] + weights["b2"]).astype(BF16)


def joined_of(one, weights):
    return matmul(one, weights["qkv"]) + weights["bqkv"]


def hidden(two, weights):
    up = matmul(two, weights["up"]) + weights["bup"]
    phi = 0.5 * (1.0 + lax.erf(up * np.float32(0.5**0.5)))
    slope = phi + up * jnp.exp(-0.5 * up * up) * np.float32((2 * np.pi) ** -0.5)
    return (up * phi).astype(BF16), slope.astype(BF16)


def branch_part(ctx, middle, weights):
    return matmul(ctx, weights["out"]) + matmul(middle, weights["down"])


def back_attend(qkv, lse, grad, weights, table, begin, track):
    d_ctx = dot_nt(grad, weights["out"]).astype(BF16)
    d_fused = attend_back(qkv, lse, d_ctx, table, begin)
    (d_fused,) = track.step((d_fused,))
    d_one = dot_nt(d_fused, weights["qkv"])
    return d_fused, d_one


def back_hidden(slope, grad, weights):
    d_up = (dot_nt(grad, weights["down"]) * slope.astype(F32)).astype(BF16)
    return d_up, dot_nt(d_up, weights["up"])


def back_norms(source, d_one, d_two, weights):
    normed, scale = normalized(source.astype(F32))
    mixed = d_one * weights["g1"] + d_two * weights["g2"]
    part = scale * (
        mixed
        - jnp.mean(mixed, axis=-1, keepdims=True)
        - normed * jnp.mean(mixed * normed, axis=-1, keepdims=True)
    )
    sums = (
        jnp.sum(d_one * normed, axis=0),
        jnp.sum(d_one, axis=0),
        jnp.sum(d_two * normed, axis=0),
        jnp.sum(d_two, axis=0),
    )
    return part, sums


def body(
    tokens,
    segments,
    cotangent,
    ln1_gain,
    ln1_bias,
    ln2_gain,
    ln2_bias,
    qkv_weight,
    qkv_bias,
    out_weight,
    out_bias,
    up_weight,
    up_bias,
    down_weight,
    down_bias,
):
    n = lax.axis_size("dp")
    chips = n // 2
    r = D // n
    u = 2 * r
    f = FF // n
    section = lax.axis_index("section")
    dp = lax.axis_index("dp")
    core = lax.rem(dp, 2)
    low_core, low_section = core == 0, section == 0
    ring = Ring(n) if chips == 8 else None

    track = Tracks()

    vectors = (ln1_gain, ln1_bias, ln2_gain, ln2_bias, qkv_bias, out_bias, up_bias, down_bias)
    core_scalar = core[None].astype(jnp.int32)
    weights_in = (qkv_weight, out_weight, up_weight, down_weight)

    def packed():
        if ring is not None:
            shapes = [(r + 8, LANES)] * 2 + [(r, LANES)] * 2 + [(u, LANES)]
            return pl.pallas_call(
                pack_kernel,
                grid=(1,),
                in_specs=[smem()] + [whole(v.shape) for v in weights_in + vectors],
                out_specs=[vmem()] * 5,
                out_shape=[jax.ShapeDtypeStruct(shape, BF16) for shape in shapes],
                scratch_shapes=[pltpu.VMEM((8, LANES), F32)],
                compiler_params=kernel_params(),
            )(core_scalar, *weights_in, *vectors)
        rows = jnp.concatenate([jnp.pad(v, ((0, 0), (0, LANES - v.shape[1]))) for v in vectors])
        attn, hidden = [], []
        for t in (0, 1):
            columns = [
                qkv_weight[0, :, D * i + HALF * t + PAIR * p : D * i + HALF * t + PAIR * (p + 1)]
                for p in range(PAIRS)
                for i in range(3)
            ] + [out_weight[0, :, HALF * t : HALF * (t + 1)]]
            attn.append(jnp.concatenate([jnp.concatenate(columns, axis=1), rows]))
            hidden.append(up_weight[0].reshape(r, chips, 2, f)[:, :, t].reshape(r, FFH))
        halves = [pick(low_core, *x) for x in (attn, attn[::-1], hidden, hidden[::-1])]
        down = down_weight[0]
        return halves + [jnp.concatenate([down[:u], down[u:]], axis=1)]

    def shared(mine, sent):
        theirs = swap_core(sent)
        return pick(low_core, mine, theirs), pick(low_core, theirs, mine)

    attn_keep, attn_send, mlp_keep, mlp_send, folded = packed()
    a, b = shared(attn_keep, attn_send)
    attn_block = jnp.concatenate([a[:r], b[:r], a[r:], b[r:]])
    other = swap_section(attn_block)
    attn_blocks = (pick(low_section, attn_block, other), pick(low_section, other, attn_block))
    a, b = shared(mlp_keep, mlp_send)
    mlp_block = jnp.concatenate([a, b, folded])
    other = swap_section(mlp_block)
    mlp_blocks = (pick(low_section, mlp_block, other), pick(low_section, other, mlp_block))

    if ring is not None:
        track.push(0, ("attn", 0), ring.gather(attn_blocks[0]))

    place = None if ring is None else jnp.append(ring.found_at(), core)

    def gathered(own):
        return lax.all_gather(own, "dp", axis=0, axis_index_groups=same_core(n))

    def attn_weights(layer):
        if ring is None:
            every = gathered(attn_blocks[layer])
            qo = every[:, :u].reshape(D, LANES)
            columns = qo[:, QKVH:]
            halves = (columns[:HALF], columns[HALF:])
            qkv, kept_rows, sent = qo[:, :QKVH], pick(low_core, *halves), pick(low_core, *halves[::-1])
            small = every[:, u:].reshape(n, len(SMALL), LANES).astype(F32)
            found = [small[:, i, : size * r].reshape(size * D) for i, size in enumerate(SMALL)]
            bq, bu = found[4].reshape(3, 2, PAIRS, PAIR), found[6].reshape(chips, 2, f)
            found[4] = pick(low_core, bq[:, 0], bq[:, 1]).transpose(1, 0, 2).reshape(QKVH)
            found[5] = found[5] + found[7]
            found[6] = pick(low_core, bu[:, 0], bu[:, 1]).reshape(FFH)
        else:
            shapes = [((D, QKVH), BF16), ((HALF, HALF), BF16), ((HALF, HALF), BF16), ((8, LANES), F32)]
            qkv, kept_rows, sent, vec = pl.pallas_call(
                assemble_attn_kernel,
                in_specs=[smem()] + [vmem()] * (chips + 1),
                out_specs=[vmem()] * 4,
                out_shape=[jax.ShapeDtypeStruct(*shape) for shape in shapes],
                scratch_shapes=[
                    pltpu.VMEM((D, HALF), BF16),
                    pltpu.VMEM((chips, PAD, 256), F32),
                    pltpu.VMEM((8, D), F32),
                    pltpu.VMEM((1, 3 * D), F32),
                    pltpu.VMEM((2, 1, FFH), F32),
                ],
                compiler_params=kernel_params(),
            )(place, *track.finish(("attn", layer)))
            widths = (D, D, D, D, QKVH, D, FFH)
            found = [vec[i, :w] for i, w in enumerate(widths)]
        got = swap_core(sent)
        out = jnp.concatenate([pick(low_core, kept_rows, got), pick(low_core, got, kept_rows)], axis=1)
        names = ("g1", "b1", "g2", "b2", "bqkv", "bout", "bup")
        return {"qkv": qkv, "out": out, **dict(zip(names, found))}

    def mlp_weights(layer):
        if ring is None:
            every = gathered(mlp_blocks[layer])
            up, folded = every[:, :u].reshape(D, FFH), every[:, u:]
            down = jnp.stack([folded[:, :, :D], folded[:, :, D:]], axis=1).reshape(FFH, D)
        else:
            up, down = pl.pallas_call(
                assemble_mlp_kernel,
                in_specs=[smem()] + [vmem()] * (chips + 1),
                out_specs=[vmem()] * 2,
                out_shape=[jax.ShapeDtypeStruct((D, FFH), BF16), jax.ShapeDtypeStruct((FFH, D), BF16)],
                compiler_params=kernel_params(),
            )(place, *track.finish(("mlp", layer)))
        return {"up": up, "down": down}

    length = tokens.shape[1]

    def paired(own):
        got = swap_core(own)
        return jnp.concatenate([pick(low_core, own, got), pick(low_core, got, own)])

    def own_half(rows):
        return pick(low_core, rows[:length], rows[length:])

    def other_half(rows):
        return pick(low_core, rows[length:], rows[:length])

    def summed(part):
        return own_half(part) + swap_core(other_half(part).astype(BF16)).astype(F32)

    own_tokens = pick(low_section, tokens[0], tokens[1])
    own_seg = pick(low_section, segments[0], segments[1])
    own_cot = pick(low_section, cotangent[0], cotangent[1])
    cot_low = own_cot.astype(BF16)
    (both, own_seg) = track.step((own_tokens, own_seg))
    table, begin = rotary_tables(paired(own_seg[None]))
    both = paired(both)

    weights_0 = attn_weights(0)
    if ring is not None:
        track.push(0, ("attn", 1), ring.gather(attn_blocks[1]))
        track.push(0, ("mlp", 1), ring.gather(mlp_blocks[1]))
        track.push(1, ("mlp", 0), ring.gather(mlp_blocks[0]))
    source_0 = both
    one_0, two_0 = norms(both, weights_0)
    one_0, two_0, joined = track.step((one_0, two_0, joined_of(one_0, weights_0)))
    qkv_0, ctx_0, lse_0 = track.step(attend(joined, table, begin))
    weights_0.update(mlp_weights(0))
    middle_0, slope_0 = track.step(hidden(two_0, weights_0))
    (part,) = track.step((branch_part(ctx_0, middle_0, weights_0),))
    mid = (own_tokens.astype(F32) + summed(part) + weights_0["bout"]).astype(BF16)
    (mid,) = track.step((mid,))
    source_1 = paired(mid)
    weights_1 = attn_weights(1)

    def reduce_group(name, group):
        if ring is None:
            total = lax.psum_scatter(group, "dp", scatter_dimension=0, axis_index_groups=same_core(n))
            track.done[name] = total.astype(F32)
            return
        block_of = lambda chip: lax.dynamic_index_in_dim(group, chip, 0, keepdims=False)
        track.push(int(name[0] == "d_mlp"), name, ring.scatter(block_of, group.shape[1]))

    def send_mlp(layer, two, d_up, middle, grad):
        if ring is None:
            up_grad, down_rows = dot_tn(two, d_up), dot_tn(middle, grad).reshape(chips, 2, u, D)
            down_rows = jnp.concatenate([down_rows[:, 0], down_rows[:, 1]], axis=2)
            group = jnp.concatenate([up_grad.reshape(chips, u, LANES), down_rows], axis=1).astype(BF16)
        else:
            rows = two.shape[0]
            group = pl.pallas_call(
                grads_mlp_kernel,
                grid=(2,),
                in_specs=[
                    pl.BlockSpec((rows, HALF), lambda g: (0, g)),
                    pl.BlockSpec((rows, FFH), lambda g: (0, 0)),
                    pl.BlockSpec((rows, FFH // 2), lambda g: (0, g)),
                    pl.BlockSpec((rows, D), lambda g: (0, 0)),
                ],
                out_specs=pl.BlockSpec((chips // 2, 2 * u, LANES), lambda g: (g, 0, 0)),
                out_shape=jax.ShapeDtypeStruct((chips, 2 * u, LANES), BF16),
                compiler_params=kernel_params(),
            )(two, d_up, middle, grad)
        reduce_group(("d_mlp", layer), group)

    def send_attn(layer, one, d_fused, out_rows, small, bias):
        bq = small[4].reshape(PAIRS, 3, PAIR).transpose(1, 0, 2)
        bu = small[6].reshape(chips, f)
        none_q, none_u = jnp.zeros_like(bq), jnp.zeros_like(bu)
        bq = jnp.stack([pick(low_core, bq, none_q), pick(low_core, none_q, bq)], axis=1).reshape(1, 3 * D)
        bu = jnp.stack([pick(low_core, bu, none_u), pick(low_core, none_u, bu)], axis=1).reshape(1, FF)
        if ring is None:
            vectors = [v.reshape(n, 1, -1) for v in (*small[:4], bq, bias, bu, bias)]
            rows = [jnp.pad(v, ((0, 0), (0, 0), (0, LANES - v.shape[2]))) for v in vectors]
            flat = jnp.concatenate(rows, axis=1).astype(BF16).reshape(chips, PAD, LANES)
            qo = jnp.concatenate([dot_tn(one, d_fused).astype(BF16), out_rows], axis=1)
            group = jnp.concatenate([qo.reshape(chips, u, LANES), flat], axis=1)
        else:
            unit = jnp.stack([*small[:4], bias, bias, bias, bias])
            rows = one.shape[0]
            group = pl.pallas_call(
                grads_attn_kernel,
                grid=(2,),
                in_specs=[
                    pl.BlockSpec((rows, HALF), lambda g: (0, g)),
                    pl.BlockSpec((rows, QKVH), lambda g: (0, 0)),
                    pl.BlockSpec((HALF, HALF), lambda g: (g, 0)),
                    pl.BlockSpec((8, HALF), lambda g: (0, g)),
                    pl.BlockSpec((1, 3 * HALF), lambda g: (0, g)),
                    pl.BlockSpec((1, FFH), lambda g: (0, g)),
                ],
                out_specs=pl.BlockSpec((chips // 2, u + PAD, LANES), lambda g: (g, 0, 0)),
                out_shape=jax.ShapeDtypeStruct((chips, u + PAD, LANES), BF16),
                scratch_shapes=[pltpu.VMEM((PAD, LANES), F32)],
                compiler_params=kernel_params(),
            )(one, d_fused, out_rows, unit, bq, bu)
        reduce_group(("d_attn", layer), group)

    def out_rows_of(ctx, grad):
        out_grad = dot_tn(ctx, grad).astype(BF16)
        halves = (out_grad[:, :HALF], out_grad[:, HALF:])
        kept_columns = pick(low_core, *halves)
        got = swap_core(pick(low_core, *halves[::-1]))
        return jnp.concatenate([pick(low_core, kept_columns, got), pick(low_core, got, kept_columns)])

    def sums_of(rows):
        return jnp.sum(rows.astype(F32), axis=0)

    grad = paired(cot_low)
    one, two = norms(source_1, weights_1)
    weights_1.update(mlp_weights(1))
    middle, slope = hidden(two, weights_1)
    d_up, d_two = back_hidden(slope, grad, weights_1)
    send_mlp(1, two, d_up, middle, grad)
    (one, d_two) = track.step((one, d_two))
    qkv, ctx, lse = track.step(attend(joined_of(one, weights_1), table, begin))
    d_fused, d_one = back_attend(qkv, lse, grad, weights_1, table, begin, track)
    out_rows = out_rows_of(ctx, grad)
    part, sums = back_norms(source_1, d_one, d_two, weights_1)
    small = (*sums, sums_of(d_fused), None, sums_of(d_up))
    (part,) = track.step((part,))
    send_attn(1, one, d_fused, out_rows, small, sums_of(cot_low))
    grad_1 = own_cot + summed(part)
    low_1 = grad_1.astype(BF16)
    (low_1, grad_1) = track.step((low_1, grad_1))

    last = (mid.astype(F32) + summed(branch_part(ctx, middle, weights_1)) + weights_1["bout"]).astype(BF16)
    kept_out, got_out = pick(low_section, mid, last), swap_section(pick(low_section, last, mid))

    grad = paired(low_1)
    d_up, d_two = back_hidden(slope_0, grad, weights_0)
    send_mlp(0, two_0, d_up, middle_0, grad)
    (d_two,) = track.step((d_two,))
    out_rows = out_rows_of(ctx_0, grad)
    d_fused, d_one = back_attend(qkv_0, lse_0, grad, weights_0, table, begin, track)
    part, sums = back_norms(source_0, d_one, d_two, weights_0)
    small = (*sums, sums_of(d_fused), None, sums_of(d_up))
    (part, got_out) = track.step((part, got_out))
    send_attn(0, one_0, d_fused, out_rows, small, sums_of(low_1))
    grad_0 = low_1.astype(F32) + summed(part)
    (grad_0,) = track.step((grad_0,))
    outputs = jnp.stack([pick(low_section, kept_out, got_out), pick(low_section, got_out, kept_out)])
    sent = swap_section(pick(low_section, grad_1, grad_0).astype(BF16)).astype(F32)
    kept_rows = pick(low_section, grad_0, grad_1)
    in_grads = jnp.stack([pick(low_section, kept_rows, sent), pick(low_section, sent, kept_rows)])

    def of_section(kind):
        zero, one_ = track.finish((kind, 0)), track.finish((kind, 1))
        got = swap_section(pick(low_section, one_, zero).astype(BF16))
        return pick(low_section, zero, one_) + got.astype(F32)

    def of_core(block, half):
        keep = pick(low_core, block[:half], block[half:])
        got = swap_core(pick(low_core, block[half:], block[:half]).astype(BF16)).astype(F32)
        return pick(low_core, keep, got), pick(low_core, got, keep), keep + got

    mlp = of_section("d_mlp")
    m0, m1, _ = of_core(mlp[:u], r)
    up_out = jnp.stack([m0.reshape(r, chips, f), m1.reshape(r, chips, f)], axis=2).reshape(r, FF)
    down_out = jnp.concatenate([mlp[u:, :D], mlp[u:, D:]])
    attn = of_section("d_attn")
    rows = len(SMALL)
    a0, a1, both_sum = of_core(
        jnp.concatenate([attn[:r], attn[u : u + rows], attn[r:u], attn[u + rows :]]), r + rows
    )
    qkv_out = jnp.concatenate(
        [
            half[:r, (3 * p + i) * PAIR : (3 * p + i + 1) * PAIR]
            for i in range(3)
            for half in (a0, a1)
            for p in range(PAIRS)
        ],
        axis=1,
    )
    out_out = jnp.concatenate([a0[:r, QKVH:], a1[:r, QKVH:]], axis=1)
    g1, b1, g2, b2, bq, bo, bu, bd = [both_sum[r + i : r + i + 1, : size * r] for i, size in enumerate(SMALL)]
    return (
        outputs[None],
        in_grads[None],
        g1,
        b1,
        g2,
        b2,
        qkv_out[None],
        bq,
        out_out[None],
        bo,
        up_out[None],
        bu,
        down_out[None],
        bd,
    )


def solution(mesh):
    row, matrix = P("section", "dp"), P("section", "dp", None)
    params = (row, row, row, row, matrix, row, matrix, row, matrix, row, matrix, row)
    return jax.shard_map(
        body,
        mesh=mesh,
        in_specs=(P(None, "dp", None), P(None, "dp"), P(None, "dp", None)) + params,
        out_specs=(P("section", None, "dp", None), P("section", None, "dp", None)) + params,
        check_vma=False,
    )
```

```python
import jax
import jax.numpy as jnp
import numpy as np
from jax import lax
from jax.experimental import pallas as pl
from jax.experimental.pallas import tpu as pltpu
from jax.sharding import PartitionSpec as P

D = 768
HEADS = 12
HEAD_DIM = 64
FF = 3072
ROT = 16
HALF = D // 2
PAIR = 2 * HEAD_DIM
PAIRS = HALF // PAIR
FFH = FF // 2
LANES = 2 * D
QKVH = 3 * HALF
PAD = 16
SCALE = HEAD_DIM**-0.5
F32 = jnp.float32
BF16 = jnp.bfloat16

SMALL = (1, 1, 1, 1, 3, 1, 4, 1)


def pick(is_zero, first, second):
    return jnp.where(is_zero, first, second)


def swap_core(block):
    n = lax.axis_size("dp")
    return lax.ppermute(block, "dp", [(i, i ^ 1) for i in range(n)])


def swap_section(block):
    return lax.ppermute(block, "section", [(0, 1), (1, 0)])


def ring_order(chips):
    rows = chips // 2
    return [2 * z for z in range(rows)] + [2 * z + 1 for z in reversed(range(rows))]


class Ring:
    def __init__(self, n):
        self.chips = n // 2
        self.order = ring_order(self.chips)
        chip = lax.axis_index("dp") // 2
        row = chip // 2
        self.position = jnp.where(chip % 2 == 0, row, self.chips - 1 - row)
        self.right = self.route(1)
        self.left = self.route(-1)

    def route(self, step):
        k = len(self.order)
        pairs = []
        for i in range(k):
            source, target = self.order[i], self.order[(i + step) % k]
            pairs += [(2 * source, 2 * target), (2 * source + 1, 2 * target + 1)]
        return pairs

    def chip_at(self, offset):
        at = (self.position + offset + self.chips) % self.chips
        turn = at >= self.chips // 2
        return 2 * jnp.where(turn, self.chips - 1 - at, at) + turn.astype(jnp.int32)

    def gather(self, own):
        (own,) = yield [own]
        found = [own]
        reach = self.chips // 2
        ahead = back = own
        for k in range(1, reach):
            ahead = lax.ppermute(ahead, "dp", self.right)
            back = lax.ppermute(back, "dp", self.left)
            ahead, back = yield [ahead, back]
            found += [ahead, back]
        cut = own.shape[0] // 32 * 16
        ahead = lax.ppermute(ahead[:cut], "dp", self.right)
        back = lax.ppermute(back[cut:], "dp", self.left)
        ahead, back = yield [ahead, back]
        return found + [ahead, back]

    def found_at(self):
        reach = self.chips // 2
        offsets = [0] + [o for k in range(1, reach) for o in (-k, k)] + [reach]
        return self.chip_at(jnp.asarray(np.array(offsets, np.int32)))

    def scatter(self, block_of, rows):
        reach = self.chips // 2
        cut = rows // 32 * 16
        far = block_of(self.chip_at(reach))
        ahead, back = yield [far[:cut], far[cut:]]
        ahead = lax.ppermute(ahead, "dp", self.right)
        back = lax.ppermute(back, "dp", self.left)
        ahead, back = yield [ahead, back]
        own = block_of(self.chip_at(reach - 1))
        ahead = jnp.concatenate([add_low(ahead, own[:cut]), own[cut:]])
        own = block_of(self.chip_at(1 - reach))
        back = jnp.concatenate([own[:cut], add_low(back, own[cut:])])
        for k in range(reach - 2, -1, -1):
            ahead = lax.ppermute(ahead, "dp", self.right)
            back = lax.ppermute(back, "dp", self.left)
            ahead, back = yield [ahead, back]
            if k:
                ahead = add_low(ahead, block_of(self.chip_at(k)))
                back = add_low(back, block_of(self.chip_at(-k)))
        own = block_of(self.chip_at(0))
        return own.astype(F32) + ahead.astype(F32) + back.astype(F32)


class Tracks:
    def __init__(self):
        self.waiting, self.active, self.done = ([], []), [None, None], {}

    def push(self, row, name, steps):
        self.waiting[row].append((name, steps))

    def step(self, values=()):
        for row in (0, 1):
            if self.active[row] is None and self.waiting[row]:
                name, steps = self.waiting[row].pop(0)
                self.active[row] = (name, steps, next(steps))
        held = [a[2] if a else [] for a in self.active]
        held, values = lax.optimization_barrier((held, values))
        for row in (0, 1):
            if self.active[row]:
                name, steps, _ = self.active[row]
                try:
                    self.active[row] = (name, steps, steps.send(held[row]))
                except StopIteration as end:
                    self.done[name] = end.value
                    self.active[row] = None
                    if self.waiting[row]:
                        name, steps = self.waiting[row].pop(0)
                        first, _ = lax.optimization_barrier((next(steps), held[row]))
                        self.active[row] = (name, steps, steps.send(first))
        return values

    def finish(self, name):
        while name not in self.done:
            self.step()
        return self.done[name]


def add_low(one, two):
    return (one.astype(F32) + two.astype(F32)).astype(BF16)


def same_core(n):
    return [[c + 2 * i for i in range(n // 2)] for c in (0, 1)]


def rotary_tables(segs):
    length = segs.shape[1]
    begin = jnp.sum((segs[:, None, :] < segs[:, :, None]).astype(jnp.int32), axis=2)
    place = (jnp.arange(length, dtype=jnp.int32)[None] - begin).reshape(-1).astype(F32)[:, None]
    half = ROT // 2
    freq = 10000.0 ** (-2.0 * jnp.arange(half, dtype=F32) / ROT)
    rest = jnp.zeros(HEAD_DIM - ROT, F32)
    freq = jnp.tile(jnp.concatenate([freq, freq, rest]), 2)[None]
    first = np.tile(np.arange(HEAD_DIM) < half, 2)[None]
    angle = place * freq
    sin = jnp.sin(angle)
    return jnp.concatenate([jnp.cos(angle), jnp.where(first, -sin, sin)], axis=1), begin.reshape(-1)[:, None]


def turned(x, table, sign):
    lane = lax.broadcasted_iota(jnp.int32, x.shape, 1) & (HEAD_DIM - 1)
    partner = jnp.where(lane < ROT // 2, pltpu.roll(x, PAIR - ROT // 2, 1), pltpu.roll(x, ROT // 2, 1))
    moved = partner * table[:, PAIR:]
    return x * table[:, :PAIR] + moved if sign > 0 else x * table[:, :PAIR] - moved


def dot_nt(a, b):
    return lax.dot_general(a, b, (((1,), (1,)), ((), ())), preferred_element_type=F32)


def dot_tn(a, b):
    return lax.dot_general(a, b, (((0,), (0,)), ((), ())), preferred_element_type=F32)


def kept(begin, row0, rows, keys):
    key = lax.broadcasted_iota(jnp.int32, (rows, keys), 1)
    row = lax.broadcasted_iota(jnp.int32, (rows, keys), 0) + row0
    return (key <= row) & (key >= begin)


def attend_kernel(joined_ref, table_ref, begin_ref, qkv_ref, ctx_ref, lse_ref):
    length = joined_ref.shape[0]
    table = table_ref[...]
    query = turned(joined_ref[:, :PAIR], table, 1).astype(BF16)
    key = turned(joined_ref[:, PAIR : 2 * PAIR], table, 1).astype(BF16)
    value = joined_ref[:, 2 * PAIR :].astype(BF16)
    qkv_ref[:, :PAIR] = query
    qkv_ref[:, PAIR : 2 * PAIR] = key
    qkv_ref[:, 2 * PAIR :] = value
    allowed = kept(begin_ref[...], 0, length, length)
    first = lax.broadcasted_iota(jnp.int32, (length, PAIR), 1) < HEAD_DIM
    scaled = query.astype(F32) * SCALE
    heads = [jnp.where(first == (h == 0), scaled, 0.0).astype(BF16) for h in range(2)]
    scores = [jnp.where(allowed, dot_nt(q, key), -1e30) for q in heads]
    peaks = [jnp.max(s, axis=1, keepdims=True) for s in scores]
    exps = [jnp.exp(s - p) for s, p in zip(scores, peaks)]
    totals = [jnp.sum(e, axis=1, keepdims=True) for e in exps]
    ctx = [
        jnp.dot(e.astype(BF16), value, preferred_element_type=F32) * (1.0 / t) for e, t in zip(exps, totals)
    ]
    lses = [p + jnp.log(t) for p, t in zip(peaks, totals)]
    ctx_ref[...] = jnp.where(first, ctx[0], ctx[1]).astype(BF16)
    lse_ref[...] = jnp.where(first, lses[0], lses[1])


def attend_back_kernel(qkv_ref, lse_ref, dctx_ref, table_ref, begin_ref, out_ref):
    length = qkv_ref.shape[0]
    chunk = length // 2
    first = lax.broadcasted_iota(jnp.int32, (chunk, PAIR), 1) < HEAD_DIM
    parts = []
    for i in range(2):
        rows, keys = pl.ds(i * chunk, chunk), (i + 1) * chunk
        allowed = kept(begin_ref[rows, :], i * chunk, chunk, keys)
        key, value = qkv_ref[:keys, PAIR : 2 * PAIR], qkv_ref[:keys, 2 * PAIR :]
        scaled, grad = qkv_ref[rows, :PAIR].astype(F32) * SCALE, dctx_ref[rows, :].astype(F32)
        qs = [jnp.where(first == (h == 0), scaled, 0.0).astype(BF16) for h in range(2)]
        dos = [jnp.where(first == (h == 0), grad, 0.0).astype(BF16) for h in range(2)]
        lses = [lse_ref[rows, h * HEAD_DIM : h * HEAD_DIM + 1] for h in range(2)]
        ps = [jnp.exp(jnp.where(allowed, dot_nt(q, key) - lse, -1e30)) for q, lse in zip(qs, lses)]
        dps = [dot_nt(do, value) for do in dos]
        inner = [jnp.sum(p * dp, axis=1, keepdims=True) for p, dp in zip(ps, dps)]
        dss = [(p * (dp - m)).astype(BF16) for p, dp, m in zip(ps, dps, inner)]
        dqs = [jnp.dot(ds, key, preferred_element_type=F32) for ds in dss]
        dv = dot_tn(ps[0].astype(BF16), dos[0]) + dot_tn(ps[1].astype(BF16), dos[1])
        dk = dot_tn(dss[0], qs[0]) + dot_tn(dss[1], qs[1])
        parts.append((jnp.where(first, dqs[0], dqs[1]) * SCALE, dk, dv))
    (dq0, dk0, dv0), (dq1, dk1, dv1) = parts
    table = table_ref[...]
    out_ref[:, :PAIR] = turned(jnp.concatenate([dq0, dq1]), table, -1).astype(BF16)
    dk = jnp.concatenate([dk0 + dk1[:chunk], dk1[chunk:]])
    out_ref[:, PAIR : 2 * PAIR] = turned(dk, table, -1).astype(BF16)
    out_ref[:, 2 * PAIR :] = jnp.concatenate([dv0 + dv1[:chunk], dv1[chunk:]]).astype(BF16)


def smem():
    return pl.BlockSpec(memory_space=pltpu.SMEM)


def whole(shape):
    return pl.BlockSpec(shape, lambda i: (0,) * len(shape))


def vmem():
    return pl.BlockSpec(memory_space=pltpu.VMEM)


def pack_kernel(core_ref, wq_ref, wo_ref, wu_ref, wd_ref, *refs):
    small_refs, (attn_keep, attn_send, mlp_keep, mlp_send, fold_ref, rows_ref) = refs[:-6], refs[-6:]
    r, chips, f = wq_ref.shape[1], D // wq_ref.shape[1] // 2, wd_ref.shape[1]
    rows_ref[...] = jnp.zeros_like(rows_ref)
    for i, ref in enumerate(small_refs):
        rows_ref[i : i + 1, : ref.shape[1]] = ref[...].astype(F32)
    rows = rows_ref[...].astype(BF16)
    attn_keep[r:, :] = rows
    attn_send[r:, :] = rows
    fold_ref[:, :D] = wd_ref[0, : f // 2]
    fold_ref[:, D:] = wd_ref[0, f // 2 :]
    for core, targets in ((0, (attn_keep, attn_send)), (1, (attn_send, attn_keep))):

        @pl.when(core_ref[0] == core)
        def _(targets=targets):
            for t, ref in enumerate(targets):
                for p in range(PAIRS):
                    for i in range(3):
                        at, to = D * i + HALF * t + PAIR * p, (3 * p + i) * PAIR
                        ref[:r, to : to + PAIR] = wq_ref[0, :, at : at + PAIR]
                ref[:r, QKVH:] = wo_ref[0, :, HALF * t : HALF * (t + 1)]

    for core, targets in ((0, (mlp_keep, mlp_send)), (1, (mlp_send, mlp_keep))):

        @pl.when(core_ref[0] == core)
        def _(targets=targets):
            for t, ref in enumerate(targets):
                for j in range(chips):
                    at = (2 * j + t) * f
                    ref[:, j * f : (j + 1) * f] = wu_ref[0, :, at : at + f]


def assemble_attn_kernel(place_ref, *refs):
    blocks, (qkv_ref, keep_ref, send_ref, vec_ref, col_ref, row_ref, all_ref, bq_ref, bu_ref) = refs[:-9], refs[-9:]
    chips = len(blocks) - 1
    core = place_ref[chips]
    u = blocks[0].shape[0] - PAD
    n = 2 * chips
    r, f = u // 2, 2 * u
    for k in range(chips):
        chip = place_ref[k]
        if k < chips - 1:
            parts = [(0, u, blocks[k], 0)]
            small = blocks[k][u:, :]
        else:
            cut = blocks[k].shape[0]
            parts = [(0, cut, blocks[k], 0), (cut, u - cut, blocks[k + 1], 0)]
            small = blocks[k + 1][u - cut :, :]
        for start, count, ref, at in parts:
            rows = pl.ds(pl.multiple_of(chip * u + start, 16), count)
            qkv_ref[rows, :] = ref[at : at + count, :QKVH]
            col_ref[rows, :] = ref[at : at + count, QKVH:]
        row_ref[chip] = small[:, : row_ref.shape[2]].astype(F32)
    keep_ref[...] = col_ref[pl.ds(pl.multiple_of(core * HALF, HALF), HALF), :]
    send_ref[...] = col_ref[pl.ds(pl.multiple_of((1 - core) * HALF, HALF), HALF), :]
    for i in range(n):
        piece = row_ref[i // 2, 8 * (i % 2) : 8 * (i % 2) + 8, :]
        all_ref[:, r * i : r * (i + 1)] = piece[:, :r]
        bq_ref[:, 3 * r * i : 3 * r * (i + 1)] = piece[4:5, : 3 * r]
        bu_ref[i % 2, :, f * (i // 2) : f * (i // 2 + 1)] = piece[6:7, :f]
    vec_ref[...] = jnp.zeros_like(vec_ref)
    vec_ref[:, :D] = all_ref[...]
    vec_ref[5:6, :D] = all_ref[5:6, :] + all_ref[7:8, :]
    for c in range(2):

        @pl.when(core == c)
        def _(c=c):
            for p in range(PAIRS):
                for i in range(3):
                    at, to = D * i + HALF * c + PAIR * p, (3 * p + i) * PAIR
                    vec_ref[4:5, to : to + PAIR] = bq_ref[:, at : at + PAIR]
            vec_ref[6:7, :] = bu_ref[c]


def assemble_mlp_kernel(place_ref, *refs):
    blocks, (up_ref, down_ref) = refs[:-2], refs[-2:]
    chips = len(blocks) - 1
    u = blocks[0].shape[0] // 2
    for k in range(chips):
        chip = place_ref[k]
        if k < chips - 1:
            up, down = blocks[k].at[:u], blocks[k].at[u:]
        else:
            up, down = blocks[k], blocks[k + 1]
        up_ref[pl.ds(pl.multiple_of(chip * u, 16), u), :] = up[...]
        down_ref[pl.ds(pl.multiple_of(chip * 2 * u, 16), u), :] = down[:, :D]
        down_ref[pl.ds(pl.multiple_of(chip * 2 * u + u, 16), u), :] = down[:, D:]


def grads_mlp_kernel(two_ref, d_up_ref, middle_ref, grad_ref, out_ref):
    count, u = out_ref.shape[0], out_ref.shape[1] // 2
    up = dot_tn(two_ref[...], d_up_ref[...]).astype(BF16)
    for i in range(count):
        out_ref[i, :u, :] = up[u * i : u * (i + 1)]
    down = dot_tn(middle_ref[...], grad_ref[...]).astype(BF16)
    for i in range(count):
        out_ref[i, u:, :D] = down[2 * u * i : 2 * u * i + u]
        out_ref[i, u:, D:] = down[2 * u * i + u : 2 * u * (i + 1)]


def grads_attn_kernel(one_ref, fused_ref, out_rows_ref, all_ref, bq_ref, bu_ref, out_ref, row_ref):
    count, u = out_ref.shape[0], out_ref.shape[1] - PAD
    r = u // 2
    qkv = dot_tn(one_ref[...], fused_ref[...]).astype(BF16)
    for i in range(count):
        out_ref[i, :u, :QKVH] = qkv[u * i : u * (i + 1)]
        out_ref[i, :u, QKVH:] = out_rows_ref[u * i : u * (i + 1), :]
        row_ref[...] = jnp.zeros_like(row_ref)
        for c in range(2):
            d = 2 * i + c
            row_ref[8 * c : 8 * c + 8, :r] = all_ref[:, r * d : r * (d + 1)]
            row_ref[8 * c + 4 : 8 * c + 5, : 3 * r] = bq_ref[:, 3 * r * d : 3 * r * (d + 1)]
            row_ref[8 * c + 6 : 8 * c + 7, : 4 * r] = bu_ref[:, 4 * r * d : 4 * r * (d + 1)]
        out_ref[i, u:, :] = row_ref[...].astype(BF16)


def small_cost():
    return pl.CostEstimate(flops=1000, bytes_accessed=1000, transcendentals=0)


def kernel_params():
    return pltpu.CompilerParams(vmem_limit_bytes=40 * 1024 * 1024)


def per_pair(length, width):
    return pl.BlockSpec((length, width), lambda s, p: (s, p))


def per_row(length, width):
    return pl.BlockSpec((length, width), lambda s, p: (s, 0))


def attend(joined, table, begin):
    tokens = joined.shape[0]
    length = tokens // 2
    return pl.pallas_call(
        attend_kernel,
        grid=(2, PAIRS),
        in_specs=[per_pair(length, 3 * PAIR), per_row(length, 2 * PAIR), per_row(length, 1)],
        out_specs=[per_pair(length, 3 * PAIR), per_pair(length, PAIR), per_pair(length, PAIR)],
        out_shape=[
            jax.ShapeDtypeStruct((tokens, QKVH), BF16),
            jax.ShapeDtypeStruct((tokens, HALF), BF16),
            jax.ShapeDtypeStruct((tokens, HALF), F32),
        ],
        compiler_params=kernel_params(),
        cost_estimate=small_cost(),
    )(joined, table, begin)


def attend_back(qkv, lse, dctx, table, begin):
    tokens = qkv.shape[0]
    length = tokens // 2
    return pl.pallas_call(
        attend_back_kernel,
        grid=(2, PAIRS),
        in_specs=[
            per_pair(length, 3 * PAIR),
            per_pair(length, PAIR),
            per_pair(length, PAIR),
            per_row(length, 2 * PAIR),
            per_row(length, 1),
        ],
        out_specs=per_pair(length, 3 * PAIR),
        out_shape=jax.ShapeDtypeStruct((tokens, QKVH), BF16),
        compiler_params=kernel_params(),
        cost_estimate=small_cost(),
    )(qkv, lse, dctx, table, begin)


def normalized(rows):
    center = rows - jnp.mean(rows, axis=-1, keepdims=True)
    spread = jnp.mean(center * center, axis=-1, keepdims=True)
    scale = lax.rsqrt(spread + 1e-05)
    return center * scale, scale


def matmul(a, b):
    return jnp.dot(a, b, preferred_element_type=F32)


def norms(source, weights):
    normed, scale = normalized(source.astype(F32))
    one = (normed * weights["g1"] + weights["b1"]).astype(BF16)
    return one, (normed * weights["g2"] + weights["b2"]).astype(BF16)


def joined_of(one, weights):
    return matmul(one, weights["qkv"]) + weights["bqkv"]


def hidden(two, weights):
    up = matmul(two, weights["up"]) + weights["bup"]
    phi = 0.5 * (1.0 + lax.erf(up * np.float32(0.5**0.5)))
    slope = phi + up * jnp.exp(-0.5 * up * up) * np.float32((2 * np.pi) ** -0.5)
    return (up * phi).astype(BF16), slope.astype(BF16)


def branch_part(ctx, middle, weights):
    return matmul(ctx, weights["out"]) + matmul(middle, weights["down"])


def back_attend(qkv, lse, grad, weights, table, begin, track):
    d_ctx = dot_nt(grad, weights["out"]).astype(BF16)
    d_fused = attend_back(qkv, lse, d_ctx, table, begin)
    (d_fused,) = track.step((d_fused,))
    d_one = dot_nt(d_fused, weights["qkv"])
    return d_fused, d_one


def back_hidden(slope, grad, weights):
    d_up = (dot_nt(grad, weights["down"]) * slope.astype(F32)).astype(BF16)
    return d_up, dot_nt(d_up, weights["up"])


def back_norms(source, d_one, d_two, weights):
    normed, scale = normalized(source.astype(F32))
    mixed = d_one * weights["g1"] + d_two * weights["g2"]
    part = scale * (
        mixed
        - jnp.mean(mixed, axis=-1, keepdims=True)
        - normed * jnp.mean(mixed * normed, axis=-1, keepdims=True)
    )
    sums = (
        jnp.sum(d_one * normed, axis=0),
        jnp.sum(d_one, axis=0),
        jnp.sum(d_two * normed, axis=0),
        jnp.sum(d_two, axis=0),
    )
    return part, sums


def body(
    tokens,
    segments,
    cotangent,
    ln1_gain,
    ln1_bias,
    ln2_gain,
    ln2_bias,
    qkv_weight,
    qkv_bias,
    out_weight,
    out_bias,
    up_weight,
    up_bias,
    down_weight,
    down_bias,
):
    n = lax.axis_size("dp")
    chips = n // 2
    r = D // n
    u = 2 * r
    f = FF // n
    section = lax.axis_index("section")
    dp = lax.axis_index("dp")
    core = lax.rem(dp, 2)
    low_core, low_section = core == 0, section == 0
    ring = Ring(n) if chips == 8 else None

    track = Tracks()

    vectors = (ln1_gain, ln1_bias, ln2_gain, ln2_bias, qkv_bias, out_bias, up_bias, down_bias)
    core_scalar = core[None].astype(jnp.int32)
    weights_in = (qkv_weight, out_weight, up_weight, down_weight)

    def packed():
        if ring is not None:
            shapes = [(r + 8, LANES)] * 2 + [(r, LANES)] * 2 + [(u, LANES)]
            return pl.pallas_call(
                pack_kernel,
                grid=(1,),
                in_specs=[smem()] + [whole(v.shape) for v in weights_in + vectors],
                out_specs=[vmem()] * 5,
                out_shape=[jax.ShapeDtypeStruct(shape, BF16) for shape in shapes],
                scratch_shapes=[pltpu.VMEM((8, LANES), F32)],
                compiler_params=kernel_params(),
                cost_estimate=small_cost(),
            )(core_scalar, *weights_in, *vectors)
        rows = jnp.concatenate([jnp.pad(v, ((0, 0), (0, LANES - v.shape[1]))) for v in vectors])
        attn, hidden = [], []
        for t in (0, 1):
            columns = [
                qkv_weight[0, :, D * i + HALF * t + PAIR * p : D * i + HALF * t + PAIR * (p + 1)]
                for p in range(PAIRS)
                for i in range(3)
            ] + [out_weight[0, :, HALF * t : HALF * (t + 1)]]
            attn.append(jnp.concatenate([jnp.concatenate(columns, axis=1), rows]))
            hidden.append(up_weight[0].reshape(r, chips, 2, f)[:, :, t].reshape(r, FFH))
        halves = [pick(low_core, *x) for x in (attn, attn[::-1], hidden, hidden[::-1])]
        down = down_weight[0]
        return halves + [jnp.concatenate([down[:u], down[u:]], axis=1)]

    def shared(mine, sent):
        theirs = swap_core(sent)
        return pick(low_core, mine, theirs), pick(low_core, theirs, mine)

    attn_keep, attn_send, mlp_keep, mlp_send, folded = packed()
    a, b = shared(attn_keep, attn_send)
    attn_block = jnp.concatenate([a[:r], b[:r], a[r:], b[r:]])
    other = swap_section(attn_block)
    attn_blocks = (pick(low_section, attn_block, other), pick(low_section, other, attn_block))
    a, b = shared(mlp_keep, mlp_send)
    mlp_block = jnp.concatenate([a, b, folded])
    other = swap_section(mlp_block)
    mlp_blocks = (pick(low_section, mlp_block, other), pick(low_section, other, mlp_block))

    if ring is not None:
        track.push(0, ("attn", 0), ring.gather(attn_blocks[0]))

    place = None if ring is None else jnp.append(ring.found_at(), core)

    def gathered(own):
        return lax.all_gather(own, "dp", axis=0, axis_index_groups=same_core(n))

    def attn_weights(layer):
        if ring is None:
            every = gathered(attn_blocks[layer])
            qo = every[:, :u].reshape(D, LANES)
            columns = qo[:, QKVH:]
            halves = (columns[:HALF], columns[HALF:])
            qkv, kept_rows, sent = qo[:, :QKVH], pick(low_core, *halves), pick(low_core, *halves[::-1])
            small = every[:, u:].reshape(n, len(SMALL), LANES).astype(F32)
            found = [small[:, i, : size * r].reshape(size * D) for i, size in enumerate(SMALL)]
            bq, bu = found[4].reshape(3, 2, PAIRS, PAIR), found[6].reshape(chips, 2, f)
            found[4] = pick(low_core, bq[:, 0], bq[:, 1]).transpose(1, 0, 2).reshape(QKVH)
            found[5] = found[5] + found[7]
            found[6] = pick(low_core, bu[:, 0], bu[:, 1]).reshape(FFH)
        else:
            shapes = [((D, QKVH), BF16), ((HALF, HALF), BF16), ((HALF, HALF), BF16), ((8, LANES), F32)]
            qkv, kept_rows, sent, vec = pl.pallas_call(
                assemble_attn_kernel,
                in_specs=[smem()] + [vmem()] * (chips + 1),
                out_specs=[vmem()] * 4,
                out_shape=[jax.ShapeDtypeStruct(*shape) for shape in shapes],
                scratch_shapes=[
                    pltpu.VMEM((D, HALF), BF16),
                    pltpu.VMEM((chips, PAD, 256), F32),
                    pltpu.VMEM((8, D), F32),
                    pltpu.VMEM((1, 3 * D), F32),
                    pltpu.VMEM((2, 1, FFH), F32),
                ],
                compiler_params=kernel_params(),
                cost_estimate=small_cost(),
            )(place, *track.finish(("attn", layer)))
            widths = (D, D, D, D, QKVH, D, FFH)
            found = [vec[i, :w] for i, w in enumerate(widths)]
        got = swap_core(sent)
        out = jnp.concatenate([pick(low_core, kept_rows, got), pick(low_core, got, kept_rows)], axis=1)
        names = ("g1", "b1", "g2", "b2", "bqkv", "bout", "bup")
        return {"qkv": qkv, "out": out, **dict(zip(names, found))}

    def mlp_weights(layer):
        if ring is None:
            every = gathered(mlp_blocks[layer])
            up, folded = every[:, :u].reshape(D, FFH), every[:, u:]
            down = jnp.stack([folded[:, :, :D], folded[:, :, D:]], axis=1).reshape(FFH, D)
        else:
            up, down = pl.pallas_call(
                assemble_mlp_kernel,
                in_specs=[smem()] + [vmem()] * (chips + 1),
                out_specs=[vmem()] * 2,
                out_shape=[jax.ShapeDtypeStruct((D, FFH), BF16), jax.ShapeDtypeStruct((FFH, D), BF16)],
                compiler_params=kernel_params(),
                cost_estimate=small_cost(),
            )(place, *track.finish(("mlp", layer)))
        return {"up": up, "down": down}

    length = tokens.shape[1]

    def paired(own):
        got = swap_core(own)
        return jnp.concatenate([pick(low_core, own, got), pick(low_core, got, own)])

    def own_half(rows):
        return pick(low_core, rows[:length], rows[length:])

    def other_half(rows):
        return pick(low_core, rows[length:], rows[:length])

    def summed(part):
        return own_half(part) + swap_core(other_half(part).astype(BF16)).astype(F32)

    own_tokens = pick(low_section, tokens[0], tokens[1])
    own_seg = pick(low_section, segments[0], segments[1])
    own_cot = pick(low_section, cotangent[0], cotangent[1])
    cot_low = own_cot.astype(BF16)
    (both, own_seg) = track.step((own_tokens, own_seg))
    table, begin = rotary_tables(paired(own_seg[None]))
    both = paired(both)

    weights_0 = attn_weights(0)
    if ring is not None:
        track.push(0, ("attn", 1), ring.gather(attn_blocks[1]))
        track.push(0, ("mlp", 1), ring.gather(mlp_blocks[1]))
        track.push(1, ("mlp", 0), ring.gather(mlp_blocks[0]))
    source_0 = both
    one_0, two_0 = norms(both, weights_0)
    one_0, two_0, joined = track.step((one_0, two_0, joined_of(one_0, weights_0)))
    qkv_0, ctx_0, lse_0 = track.step(attend(joined, table, begin))
    weights_0.update(mlp_weights(0))
    middle_0, slope_0 = track.step(hidden(two_0, weights_0))
    (part,) = track.step((branch_part(ctx_0, middle_0, weights_0),))
    mid = (own_tokens.astype(F32) + summed(part) + weights_0["bout"]).astype(BF16)
    (mid,) = track.step((mid,))
    source_1 = paired(mid)
    weights_1 = attn_weights(1)

    def reduce_group(name, group):
        if ring is None:
            total = lax.psum_scatter(group, "dp", scatter_dimension=0, axis_index_groups=same_core(n))
            track.done[name] = total.astype(F32)
            return
        block_of = lambda chip: lax.dynamic_index_in_dim(group, chip, 0, keepdims=False)
        track.push(int(name[0] == "d_mlp"), name, ring.scatter(block_of, group.shape[1]))

    def send_mlp(layer, two, d_up, middle, grad):
        if ring is None:
            up_grad, down_rows = dot_tn(two, d_up), dot_tn(middle, grad).reshape(chips, 2, u, D)
            down_rows = jnp.concatenate([down_rows[:, 0], down_rows[:, 1]], axis=2)
            group = jnp.concatenate([up_grad.reshape(chips, u, LANES), down_rows], axis=1).astype(BF16)
        else:
            rows = two.shape[0]
            group = pl.pallas_call(
                grads_mlp_kernel,
                grid=(2,),
                in_specs=[
                    pl.BlockSpec((rows, HALF), lambda g: (0, g)),
                    pl.BlockSpec((rows, FFH), lambda g: (0, 0)),
                    pl.BlockSpec((rows, FFH // 2), lambda g: (0, g)),
                    pl.BlockSpec((rows, D), lambda g: (0, 0)),
                ],
                out_specs=pl.BlockSpec((chips // 2, 2 * u, LANES), lambda g: (g, 0, 0)),
                out_shape=jax.ShapeDtypeStruct((chips, 2 * u, LANES), BF16),
                compiler_params=kernel_params(),
                cost_estimate=small_cost(),
            )(two, d_up, middle, grad)
        reduce_group(("d_mlp", layer), group)

    def send_attn(layer, one, d_fused, out_rows, small, bias):
        bq = small[4].reshape(PAIRS, 3, PAIR).transpose(1, 0, 2)
        bu = small[6].reshape(chips, f)
        none_q, none_u = jnp.zeros_like(bq), jnp.zeros_like(bu)
        bq = jnp.stack([pick(low_core, bq, none_q), pick(low_core, none_q, bq)], axis=1).reshape(1, 3 * D)
        bu = jnp.stack([pick(low_core, bu, none_u), pick(low_core, none_u, bu)], axis=1).reshape(1, FF)
        if ring is None:
            vectors = [v.reshape(n, 1, -1) for v in (*small[:4], bq, bias, bu, bias)]
            rows = [jnp.pad(v, ((0, 0), (0, 0), (0, LANES - v.shape[2]))) for v in vectors]
            flat = jnp.concatenate(rows, axis=1).astype(BF16).reshape(chips, PAD, LANES)
            qo = jnp.concatenate([dot_tn(one, d_fused).astype(BF16), out_rows], axis=1)
            group = jnp.concatenate([qo.reshape(chips, u, LANES), flat], axis=1)
        else:
            unit = jnp.stack([*small[:4], bias, bias, bias, bias])
            rows = one.shape[0]
            group = pl.pallas_call(
                grads_attn_kernel,
                grid=(2,),
                in_specs=[
                    pl.BlockSpec((rows, HALF), lambda g: (0, g)),
                    pl.BlockSpec((rows, QKVH), lambda g: (0, 0)),
                    pl.BlockSpec((HALF, HALF), lambda g: (g, 0)),
                    pl.BlockSpec((8, HALF), lambda g: (0, g)),
                    pl.BlockSpec((1, 3 * HALF), lambda g: (0, g)),
                    pl.BlockSpec((1, FFH), lambda g: (0, g)),
                ],
                out_specs=pl.BlockSpec((chips // 2, u + PAD, LANES), lambda g: (g, 0, 0)),
                out_shape=jax.ShapeDtypeStruct((chips, u + PAD, LANES), BF16),
                scratch_shapes=[pltpu.VMEM((PAD, LANES), F32)],
                compiler_params=kernel_params(),
                cost_estimate=small_cost(),
            )(one, d_fused, out_rows, unit, bq, bu)
        reduce_group(("d_attn", layer), group)

    def out_rows_of(ctx, grad):
        out_grad = dot_tn(ctx, grad).astype(BF16)
        halves = (out_grad[:, :HALF], out_grad[:, HALF:])
        kept_columns = pick(low_core, *halves)
        got = swap_core(pick(low_core, *halves[::-1]))
        return jnp.concatenate([pick(low_core, kept_columns, got), pick(low_core, got, kept_columns)])

    def sums_of(rows):
        return jnp.sum(rows.astype(F32), axis=0)

    grad = paired(cot_low)
    one, two = norms(source_1, weights_1)
    weights_1.update(mlp_weights(1))
    middle, slope = hidden(two, weights_1)
    d_up, d_two = back_hidden(slope, grad, weights_1)
    send_mlp(1, two, d_up, middle, grad)
    (one, d_two) = track.step((one, d_two))
    qkv, ctx, lse = track.step(attend(joined_of(one, weights_1), table, begin))
    d_fused, d_one = back_attend(qkv, lse, grad, weights_1, table, begin, track)
    out_rows = out_rows_of(ctx, grad)
    part, sums = back_norms(source_1, d_one, d_two, weights_1)
    small = (*sums, sums_of(d_fused), None, sums_of(d_up))
    (part,) = track.step((part,))
    send_attn(1, one, d_fused, out_rows, small, sums_of(cot_low))
    grad_1 = own_cot + summed(part)
    low_1 = grad_1.astype(BF16)
    (low_1, grad_1) = track.step((low_1, grad_1))

    last = (mid.astype(F32) + summed(branch_part(ctx, middle, weights_1)) + weights_1["bout"]).astype(BF16)
    kept_out, got_out = pick(low_section, mid, last), swap_section(pick(low_section, last, mid))

    grad = paired(low_1)
    d_up, d_two = back_hidden(slope_0, grad, weights_0)
    send_mlp(0, two_0, d_up, middle_0, grad)
    (d_two,) = track.step((d_two,))
    out_rows = out_rows_of(ctx_0, grad)
    d_fused, d_one = back_attend(qkv_0, lse_0, grad, weights_0, table, begin, track)
    part, sums = back_norms(source_0, d_one, d_two, weights_0)
    small = (*sums, sums_of(d_fused), None, sums_of(d_up))
    (part, got_out) = track.step((part, got_out))
    send_attn(0, one_0, d_fused, out_rows, small, sums_of(low_1))
    grad_0 = low_1.astype(F32) + summed(part)
    (grad_0,) = track.step((grad_0,))
    outputs = jnp.stack([pick(low_section, kept_out, got_out), pick(low_section, got_out, kept_out)])
    sent = swap_section(pick(low_section, grad_1, grad_0).astype(BF16)).astype(F32)
    kept_rows = pick(low_section, grad_0, grad_1)
    in_grads = jnp.stack([pick(low_section, kept_rows, sent), pick(low_section, sent, kept_rows)])

    def of_section(kind):
        zero, one_ = track.finish((kind, 0)), track.finish((kind, 1))
        got = swap_section(pick(low_section, one_, zero).astype(BF16))
        return pick(low_section, zero, one_) + got.astype(F32)

    def of_core(block, half):
        keep = pick(low_core, block[:half], block[half:])
        got = swap_core(pick(low_core, block[half:], block[:half]).astype(BF16)).astype(F32)
        return pick(low_core, keep, got), pick(low_core, got, keep), keep + got

    mlp = of_section("d_mlp")
    m0, m1, _ = of_core(mlp[:u], r)
    up_out = jnp.stack([m0.reshape(r, chips, f), m1.reshape(r, chips, f)], axis=2).reshape(r, FF)
    down_out = jnp.concatenate([mlp[u:, :D], mlp[u:, D:]])
    attn = of_section("d_attn")
    rows = len(SMALL)
    a0, a1, both_sum = of_core(
        jnp.concatenate([attn[:r], attn[u : u + rows], attn[r:u], attn[u + rows :]]), r + rows
    )
    qkv_out = jnp.concatenate(
        [
            half[:r, (3 * p + i) * PAIR : (3 * p + i + 1) * PAIR]
            for i in range(3)
            for half in (a0, a1)
            for p in range(PAIRS)
        ],
        axis=1,
    )
    out_out = jnp.concatenate([a0[:r, QKVH:], a1[:r, QKVH:]], axis=1)
    g1, b1, g2, b2, bq, bo, bu, bd = [both_sum[r + i : r + i + 1, : size * r] for i, size in enumerate(SMALL)]
    return (
        outputs[None],
        in_grads[None],
        g1,
        b1,
        g2,
        b2,
        qkv_out[None],
        bq,
        out_out[None],
        bo,
        up_out[None],
        bu,
        down_out[None],
        bd,
    )


def solution(mesh):
    row, matrix = P("section", "dp"), P("section", "dp", None)
    params = (row, row, row, row, matrix, row, matrix, row, matrix, row, matrix, row)
    return jax.shard_map(
        body,
        mesh=mesh,
        in_specs=(P(None, "dp", None), P(None, "dp"), P(None, "dp", None)) + params,
        out_specs=(P("section", None, "dp", None), P("section", None, "dp", None)) + params,
        check_vma=False,
    )
```
